32 devices in a mesh: parts: 2 (over y), rows: 4 (over z), sub: 2 (over x), dim: 2 (over core).
Axes of the slice: x: 2, y: 2, z: 4, core: 2. Of those that a mesh axis runs over, the one named last changes fastest.
Arguments:
- embeddings: bfloat16 [8192, 1024], P(('parts', 'rows', 'sub'), 'dim'), parts along dimension 0, may hold values from -48 to 48
- centroids: bfloat16 [2048, 1024], P('parts'), parts along dimension 0, may hold values from -7 to 7
- cluster_id: int32 [8192, 1], P(('parts', 'rows', 'sub')), parts along dimension 0, may hold values from 0 to 1023; in each aligned block of 512 rows (0 to 511, 512 to 1023, ...) at most 2 rows name the same one
- cluster_place: int32 [1024], replicated, may hold values from 0 to 1023, each once
Outputs:
- new_centroids: float32 [2048, 1024], P(('parts', 'rows', 'sub'), 'dim'), parts along dimension 0
- similarity: bfloat16 [2048, 16, 16], P(('parts', 'rows', 'sub'), 'dim'), parts along dimension 0
The draws below stay inside these ranges and needn't reach their ends.
There are 2 independent parts, one for each index of `parts`. The reference program is written for one: setup_inputs(seed, part) draws one part's arguments, and reference() takes and returns one part's arrays. A program takes and returns all parts, laid end to end along the dimension named above; an argument that names none is the same for every part. Nothing has to cross between parts.
Inputs may be any that keep to these rules, and one draw needn't show every extreme that they name: `cluster_id`: within the documents of one index of rows and sub no cluster appears more than 2 times. `cluster_place`: each position appears once; the owner of position p is p // 128.
All inputs are finite; a program needn't handle non-finite values.
Results may differ from the reference program's by a relative error of at most 0.002.
Values may be sent and summed in bfloat16 or wider, within the bound.
No kernel may reach another device: no remote copies, remote signals or barrier semaphores. Data moves between devices by JAX's collectives and lax.ppermute only.
A program may use at most 64 MiB of HBM per device.

```python
import math
import jax
import jax.numpy as jnp
import numpy as np
from jax import lax

E = 1024
PREFIX = 256
K = 1024
ROW_DEV = 512
MOST = 2
NROWS = 4096
SLOTS = 16
N_ROWS = 4
N_SUB = 2


def shared_centroids(key):
    return jnp.clip(jax.random.normal(key, (K, E), jnp.float32), -6.0, 6.0)


def draw_centroids(key, part):
    centre_rows = shared_centroids(key)
    return centre_rows.astype(jnp.bfloat16)


def draw_embeddings(key, part):
    key = jax.random.fold_in(key, 7)
    values = jnp.clip(jax.random.normal(key, (NROWS, E), jnp.float32), -6.0, 6.0)
    return values.astype(jnp.bfloat16)


def routed_block(own_key, own, number, rows, count, top, reach, skew):
    ranking = jax.random.permutation(own_key, count)
    heavy_load, ordinary = shares(count, rows * top, reach, skew, True), shares(count, rows * top, reach, skew, False)
    places = jnp.arange(count)

    def named(sizes, turn):
        used = int((sizes > 0).sum())
        fixed = max(1, used // 4)
        passed = fixed + (places - fixed + turn * (used - fixed)) % max(1, count - fixed)
        return jnp.zeros((count,), jnp.int32).at[ranking[jnp.where(places < fixed, places, passed)]].set(jnp.asarray(sizes, jnp.int32))

    sizes = jnp.where(number % 4 == 0, named(heavy_load, number // 4), named(ordinary, number - number // 4 - 1))
    mixed = jax.random.permutation(jax.random.fold_in(own, 3), count)
    giver, taker = mixed[0:count // 2 * 2:2], mixed[1:count // 2 * 2:2]
    margin = jnp.minimum(sizes[giver] - 1, reach - sizes[taker]) // 2
    margin = jnp.where((giver == ranking[0]) | (taker == ranking[0]) | (sizes[taker] == 0), 0, jnp.maximum(margin, 0))
    passed = jax.random.randint(jax.random.fold_in(own, 4), (count // 2,), 0, 1 << 20) % (margin + 1)
    sizes = sizes.at[giver].add(-passed).at[taker].add(passed)
    items = jnp.searchsorted(jnp.cumsum(sizes), jnp.arange(rows * top), side="right").astype(jnp.int32)
    listing = items.reshape(top, rows).T
    listing = listing[jax.random.permutation(jax.random.fold_in(own, 1), rows)]
    turn = jax.random.randint(jax.random.fold_in(own, 2), (rows, 1), 0, top)
    return jnp.take_along_axis(listing, (jnp.arange(top)[None, :] + turn) % top, axis=1)


def shares(count, total, limit, lean, full):
    portions = [(1 << 20) // math.isqrt(rank ** lean) + 1 for rank in range(1, count + 1)]
    largest = limit if full else min(limit, max(-(-total // count), total * portions[0] // sum(portions)))
    least = 1 if total - largest >= count - 1 else 0
    counts, surplus = [largest] + [least] * (count - 1), total - largest - least * (count - 1)
    while surplus > 0:
        free = [i for i in range(1, count) if counts[i] < largest] or [i for i in range(1, count) if counts[i] < limit]
        pool, budget = sum([portions[i] for i in free]), surplus
        for i in free:
            addition = min(limit - counts[i], max(1, budget * portions[i] // pool), surplus)
            counts[i] = counts[i] + addition
            surplus = surplus - addition
    return np.array(counts)


def setup_inputs(seed: int = 0, part: int = 0) -> dict:
    arg_keys = jax.random.split(jax.random.key(seed), 5)
    own_keys = jax.random.split(jax.random.fold_in(arg_keys[4], part), 5)
    embeddings = draw_embeddings(jax.random.fold_in(jax.random.fold_in(arg_keys[4], part), 71), part)
    centroids = draw_centroids(jax.random.fold_in(jax.random.fold_in(arg_keys[4], part), 71), part)
    cluster_id_keys = jax.random.split(jax.random.fold_in(own_keys[2], 1), NROWS // ROW_DEV)
    cluster_id_turns = jax.random.permutation(jax.random.fold_in(own_keys[2], 3), NROWS // ROW_DEV)
    cluster_id = jax.vmap(lambda own, number: routed_block(jax.random.fold_in(own_keys[2], 2), own, number, ROW_DEV, K, 1, MOST, 2))(cluster_id_keys, cluster_id_turns).reshape((NROWS, 1))
    cluster_place = jax.random.permutation(arg_keys[3], K).astype(jnp.int32)
    return {"embeddings": embeddings, "centroids": centroids, "cluster_id": cluster_id, "cluster_place": cluster_place}


TEMP = 0.125
SMOOTH = 1.0
EPS = 1e-05

def ranks_within(slab_ids):
    row_order = jnp.arange(ROW_DEV, dtype=jnp.int32)
    earlier = (slab_ids[:, None] == slab_ids[None, :]) & (row_order[None, :] < row_order[:, None])
    return lax.optimization_barrier(jnp.sum(earlier, axis=1, dtype=jnp.int32))

def reference(embeddings, centroids, cluster_id, cluster_place):
    sources = N_ROWS * N_SUB
    slabs = embeddings.reshape(sources, ROW_DEV, E)
    centre_prefix = centroids[:, :PREFIX]

    def one_slab(carry, slab_rows):
        total, mass = carry
        scores = jnp.dot(slab_rows[:, :PREFIX], centre_prefix.T, preferred_element_type=jnp.float32) * TEMP
        weights = jax.nn.softmax(scores, axis=-1).astype(jnp.bfloat16)
        total = total + jnp.dot(weights.T, slab_rows, preferred_element_type=jnp.float32)
        mass = mass + lax.optimization_barrier(jnp.sum(weights.astype(jnp.float32), axis=0))
        return ((total, mass), None)
    start_carry = (jnp.zeros((K, E), jnp.float32), jnp.zeros((K,), jnp.float32))
    (total, mass), unused = lax.scan(one_slab, start_carry, slabs)
    new_centroids = (total + SMOOTH * centroids.astype(jnp.float32)) / (mass + SMOOTH)[:, None]
    flat_ids = cluster_id[:, 0].astype(jnp.int32)
    within = lax.map(ranks_within, flat_ids.reshape(sources, ROW_DEV))
    slot = (jnp.arange(sources, dtype=jnp.int32)[:, None] * MOST + within).reshape(-1)
    table = jnp.full((K * SLOTS,), -1, jnp.int32)
    table = table.at[flat_ids * SLOTS + slot].set(jnp.arange(NROWS, dtype=jnp.int32)).reshape(K, SLOTS)
    inverse = jnp.zeros((K,), jnp.int32).at[cluster_place].set(jnp.arange(K, dtype=jnp.int32))

    def one_tile(position):
        cluster = inverse[position]
        members = table[cluster]
        present = (members >= 0).astype(jnp.float32)
        member_rows = embeddings[jnp.maximum(members, 0)].astype(jnp.float32)
        centred = ((member_rows - centroids[cluster].astype(jnp.float32)[None, :]) * present[:, None]).astype(jnp.bfloat16)
        gram = jnp.dot(centred, centred.T, preferred_element_type=jnp.float32)
        norms = lax.optimization_barrier(jnp.sum(jnp.square(centred.astype(jnp.float32)), axis=1))
        row_scale = lax.rsqrt(norms / E + EPS)
        return (gram / E * row_scale[:, None] * row_scale[None, :]).astype(jnp.bfloat16)
    similarity = lax.map(one_tile, jnp.arange(K, dtype=jnp.int32))
    return (new_centroids, similarity)
```

```python
import functools

import jax
import jax.numpy as jnp
from jax import lax
from jax.experimental import pallas as pl
from jax.experimental.pallas import tpu as pltpu
from jax.sharding import PartitionSpec as P

PREFIX = 256
MOST = 2

TEMP = 0.125
SMOOTH = 1.0
EPS = 1e-05

DIGIT = 32
META = 16
SUBLANES = 8
LANES = 128
F32 = jnp.float32
BF16 = jnp.bfloat16
VMEM_LIMIT = 40 * 1024 * 1024

NT = (((1,), (1,)), ((), ()))


def vmem():
    return pl.BlockSpec(memory_space=pltpu.VMEM)


def params():
    return pltpu.CompilerParams(vmem_limit_bytes=VMEM_LIMIT)


def dot(a, b):
    return jnp.dot(a, b, preferred_element_type=F32)


def dot_nt(a, b):
    return lax.dot_general(a, b, NT, preferred_element_type=F32)


def prep_kernel(subs, per, place_ref, cent_ref, inv_ref, centre_ref, own_prefix_ref, prior_ref):
    clusters = cent_ref.shape[0]
    half = centre_ref.shape[1]
    z, x, h = lax.axis_index("rows"), lax.axis_index("sub"), lax.axis_index("dim")
    row = lax.broadcasted_iota(jnp.int32, (subs * per, clusters), 0)
    ids = lax.broadcasted_iota(jnp.int32, (subs * per, clusters), 1)
    turn, within = row // per, row % per
    target = (z * subs + (x + turn) % subs) * per + within
    chosen = (place_ref[...] == target).astype(F32)
    inv_ref[...] = jnp.sum(chosen * ids.astype(F32), axis=1, keepdims=True)
    columns = cent_ref[:, pl.ds(pl.multiple_of(h * half, LANES), half)]
    centre_ref[...] = dot(chosen.astype(BF16), columns).astype(BF16)
    natural = (ids == target).astype(BF16)
    own_prefix_ref[...] = dot(natural, cent_ref[:, :PREFIX]).astype(BF16)
    prior_ref[...] = dot(natural[:per], columns).astype(BF16)


def block_kernel(first, subs, per, block_ref, near_ref, cent_ref, own_prefix_ref, inv_ref, centre_ref, *refs):
    if first:
        acc_in, (acc_ref, *row_refs) = None, refs
    else:
        acc_in, acc_ref, *row_refs = refs
    docs = block_ref.shape[0] - META
    half = block_ref.shape[1]
    h = lax.axis_index("dim")
    emb = block_ref[:docs, :]
    meta = block_ref[docs:, :].astype(F32)
    cid = ((meta[0:1, :] - 1.0) * DIGIT + meta[1:2, :])[:, :docs]
    prefix = jnp.where(h == 0, emb[:, :PREFIX], near_ref[...])

    scores = dot_nt(cent_ref[:, :PREFIX], prefix) * TEMP
    top = jnp.max(scores, axis=0, keepdims=True)
    scale = 1.0 / jnp.sum(jnp.exp(scores - top), axis=0, keepdims=True)
    own = dot_nt(own_prefix_ref[...], prefix) * TEMP
    weights = jnp.where(cid >= 0.0, jnp.exp(own - top) * scale, 0.0)
    sums = dot(weights.astype(BF16), emb)
    ones = jnp.ones((SUBLANES, docs), BF16)
    for t in range(subs):
        here = slice(t * per, (t + 1) * per)
        mass = dot_nt(ones, weights[here].astype(BF16))
        if first:
            acc_ref[t, :per, :] = sums[here]
            acc_ref[t, per:, :] = jnp.zeros((SUBLANES, half), F32)
            acc_ref[t, per:, :per] = mass
        else:
            acc_ref[t, :per, :] = acc_in[t, :per, :] + sums[here]
            acc_ref[t, per:, :] = acc_in[t, per:, :]
            acc_ref[t, per:, :per] = acc_in[t, per:, :per] + mass

    match = (inv_ref[...] == cid).astype(F32)
    before = lax.broadcasted_iota(jnp.int32, (docs, docs), 0) < lax.broadcasted_iota(jnp.int32, (docs, docs), 1)
    earlier = dot(match.astype(BF16), before.astype(F32).astype(BF16))
    groups = subs * per // SUBLANES
    picks = [jnp.where(earlier == r, match, 0.0).reshape(groups, SUBLANES, docs) for r in range(MOST)]
    pick = jnp.stack(picks, axis=1).reshape(groups * MOST * SUBLANES, docs)
    present = jnp.sum(pick, axis=1, keepdims=True)
    raw = dot(pick.astype(BF16), emb)
    centre = centre_ref[...].astype(F32).reshape(groups, 1, SUBLANES, half)
    centre = jnp.broadcast_to(centre, (groups, MOST, SUBLANES, half)).reshape(raw.shape)
    rows = jnp.where(present > 0.0, raw - centre, 0.0).astype(BF16)
    rows = rows.reshape(subs, per // SUBLANES, MOST * SUBLANES, half)
    for t in range(subs):
        row_refs[t][...] = rows[t]


def gram_kernel(plan, subs, rows, *refs):
    *member_refs, gram_ref, held = refs
    z, x = lax.axis_index("rows"), lax.axis_index("sub")
    owners, groups, packed, half = held.shape
    for t in range(subs):
        for at, (down, up) in enumerate(plan):
            source = jnp.where(z >= down, z - down, z + up) if up else z - down
            if not down and up:
                source = z + up
            valid = (source >= 0) & (source < rows)
            ref = member_refs[t * len(plan) + at]

            @pl.when(valid)
            def _(ref=ref, source=source, t=t):
                held[source * subs + (x - t + subs) % subs] = ref[...]

    size = owners * packed
    slots = size // SUBLANES
    lane = lax.broadcasted_iota(jnp.int32, (1, SUBLANES, size), 2) % SUBLANES
    same = (lane == lax.broadcasted_iota(jnp.int32, (1, SUBLANES, size), 1)).astype(F32)
    tile = min(size, 2 * LANES)
    for g in range(groups):
        mine = held[:, g].reshape(size, half)
        for start in range(0, size, tile):
            part = dot_nt(mine[start : start + tile], mine)
            part = part.reshape(tile // SUBLANES, SUBLANES, size)
            gram_ref[g, start // SUBLANES : (start + tile) // SUBLANES, :] = jnp.sum(part * same, axis=1)


def similarity_kernel(width, mine_ref, other_ref, out_ref):
    groups, slots, size = mine_ref.shape
    kept = out_ref.shape[1]
    h = lax.axis_index("dim")
    start = pl.multiple_of(h * kept, kept)
    row = lax.broadcasted_iota(jnp.int32, (slots, size), 0)
    lane = lax.broadcasted_iota(jnp.int32, (slots, size), 1)
    diagonal = row == lane // SUBLANES
    kept_row = lax.broadcasted_iota(jnp.int32, (kept, size), 0) + start
    kept_lane = lax.broadcasted_iota(jnp.int32, (kept, size), 1)
    kept_diagonal = kept_row == kept_lane // SUBLANES
    for g in range(groups):
        total = mine_ref[g] + other_ref[g]
        norms = jnp.sum(jnp.where(diagonal, total, 0.0), axis=0, keepdims=True)
        scale = lax.rsqrt(norms / width + EPS)
        spread = jnp.where(kept_diagonal, jnp.broadcast_to(scale, (kept, size)), 0.0)
        folded = spread[:, :LANES]
        for at in range(LANES, size, LANES):
            folded = folded + spread[:, at : at + LANES]
        step = SUBLANES
        while step < LANES:
            folded = folded + pltpu.roll(folded, step, 1)
            step *= 2
        row_scale = jnp.concatenate([folded] * (size // LANES), axis=1)
        own = mine_ref[g, pl.ds(start, kept), :] + other_ref[g, pl.ds(start, kept), :]
        out_ref[g] = (own / width * row_scale * scale).astype(BF16)


def centroid_kernel(per, acc_ref, *refs):
    *other_refs, prior_ref, out_ref = refs
    total = acc_ref[0]
    for other in other_refs:
        total = total + other[...]
    mass = jnp.transpose(total[per:, :LANES])[:per, :1]
    out_ref[...] = (total[:per] + SMOOTH * prior_ref[...].astype(F32)) / (mass + SMOOTH)


def shards(embeddings, centroids, cluster_id, cluster_place):
    docs, half = embeddings.shape
    clusters, width = centroids.shape
    rows, subs = lax.axis_size("rows"), lax.axis_size("sub")
    owners = rows * subs
    per = clusters // owners
    groups = per // SUBLANES
    packed = MOST * SUBLANES
    slots = owners * MOST
    z = lax.axis_index("rows")

    cid = cluster_id.reshape(1, docs)
    digits = jnp.concatenate([cid // DIGIT + 1, cid % DIGIT], axis=0).astype(BF16)
    meta = jnp.pad(digits, ((0, META - 2), (0, half - docs)))
    block = jnp.concatenate([embeddings, meta], axis=0)

    def along(value, pairs):
        return lax.ppermute(value, "rows", pairs)

    blocks, plan = [block], [(0, 0)]
    from_below, from_above, merged = block, block, None
    for step in range(1, rows):
        upward = [(i, i + 1) for i in range(step - 1, rows - 1)]
        downward = [(i, i - 1) for i in range(1, rows - step + 1)]
        if merged is not None:
            merged = along(merged, upward + downward)
        else:
            from_below = along(from_below, upward)
            from_above = along(from_above, downward)
            if 2 * step >= rows:
                merged = jnp.where(z >= step, from_below, from_above)
        if merged is None:
            blocks += [from_below, from_above]
            plan += [(step, 0), (0, step)]
        else:
            blocks.append(merged)
            plan.append((step, step))

    inv, centre, own_prefix, prior = pl.pallas_call(
        functools.partial(prep_kernel, subs, per),
        out_shape=(
            jax.ShapeDtypeStruct((subs * per, 1), F32),
            jax.ShapeDtypeStruct((subs * per, half), BF16),
            jax.ShapeDtypeStruct((subs * per, PREFIX), BF16),
            jax.ShapeDtypeStruct((per, half), BF16),
        ),
        in_specs=[vmem()] * 2,
        out_specs=(vmem(),) * 4,
        compiler_params=params(),
        name="prep",
    )(cluster_place.reshape(1, clusters), centroids)

    acc_shape = jax.ShapeDtypeStruct((subs, per + SUBLANES, half), F32)
    row_shape = jax.ShapeDtypeStruct((groups, packed, half), BF16)
    swaps = [[(i, (i + t) % subs) for i in range(subs)] for t in range(subs)]
    members = [[] for _ in range(subs)]
    acc = None
    for block in blocks:
        near = lax.ppermute(block[:docs, :PREFIX], "dim", [(0, 1)])
        first = acc is None
        operands = [block, near, centroids, own_prefix, inv, centre] + ([] if first else [acc])
        acc, *found = pl.pallas_call(
            functools.partial(block_kernel, first, subs, per),
            out_shape=(acc_shape,) + (row_shape,) * subs,
            in_specs=[vmem()] * len(operands),
            out_specs=(vmem(),) * (1 + subs),
            input_output_aliases={} if first else {6: 0},
            compiler_params=params(),
            name="block",
            cost_estimate=pl.CostEstimate(
                flops=2 * docs * (clusters * PREFIX + 4 * subs * per * half),
                bytes_accessed=4 * 1024 * 1024,
                transcendentals=docs * clusters,
            ),
        )(*operands)
        members[0].append(found[0])
        for t in range(1, subs):
            members[t].append(lax.ppermute(found[t], "sub", swaps[t]))

    others = [lax.ppermute(acc[t], "sub", swaps[t]) for t in range(1, subs)]
    new_centroids = pl.pallas_call(
        functools.partial(centroid_kernel, per),
        out_shape=jax.ShapeDtypeStruct((per, half), F32),
        in_specs=[vmem()] * (subs + 1),
        out_specs=vmem(),
        compiler_params=params(),
        name="centroids",
    )(acc, *others, prior)

    gram = pl.pallas_call(
        functools.partial(gram_kernel, plan, subs, rows),
        out_shape=jax.ShapeDtypeStruct((groups, slots, slots * SUBLANES), F32),
        in_specs=[vmem()] * (subs * len(plan)),
        out_specs=vmem(),
        scratch_shapes=[pltpu.VMEM((owners, groups, packed, half), BF16)],
        compiler_params=params(),
        name="gram",
    )(*[ref for column in members for ref in column])
    other_gram = lax.ppermute(gram, "dim", [(0, 1), (1, 0)])
    tiles = pl.pallas_call(
        functools.partial(similarity_kernel, width),
        out_shape=jax.ShapeDtypeStruct((groups, slots // 2, slots * SUBLANES), BF16),
        in_specs=[vmem()] * 2,
        out_specs=vmem(),
        compiler_params=params(),
        name="similarity",
    )(gram, other_gram)
    tiles = tiles.reshape(groups, slots // 2, slots, SUBLANES)
    similarity = jnp.transpose(tiles, (0, 3, 1, 2)).reshape(per, slots // 2, slots)
    return (new_centroids, similarity)


def solution(mesh):
    in_specs = (
        P(("parts", "rows", "sub"), "dim"),
        P("parts", None),
        P(("parts", "rows", "sub"), None),
        P(),
    )
    out_specs = (P(("parts", "rows", "sub"), "dim"), P(("parts", "rows", "sub"), "dim", None))
    return jax.shard_map(shards, mesh=mesh, in_specs=in_specs, out_specs=out_specs, check_vma=False)
```

```python
import functools

import jax
import jax.numpy as jnp
from jax import lax
from jax.experimental import pallas as pl
from jax.experimental.pallas import tpu as pltpu
from jax.sharding import PartitionSpec as P

PREFIX = 256
MOST = 2

TEMP = 0.125
SMOOTH = 1.0
EPS = 1e-05

DIGIT = 32
META = 16
SUBLANES = 8
LANES = 128
F32 = jnp.float32
BF16 = jnp.bfloat16
VMEM_LIMIT = 40 * 1024 * 1024

NT = (((1,), (1,)), ((), ()))


def call(kernel, name, out_shape, operands, aliases=None, scratch=(), flops=0, transcendentals=0):
    def whole():
        return pl.BlockSpec(memory_space=pltpu.VMEM)

    return pl.pallas_call(
        kernel,
        out_shape=tuple(out_shape),
        in_specs=[whole() for _ in operands],
        out_specs=tuple(whole() for _ in out_shape),
        input_output_aliases=aliases or {},
        scratch_shapes=list(scratch),
        compiler_params=pltpu.CompilerParams(vmem_limit_bytes=VMEM_LIMIT),
        cost_estimate=pl.CostEstimate(flops=flops, bytes_accessed=1024 * 1024, transcendentals=transcendentals),
        name=name,
    )(*operands)


def dot(a, b):
    return jnp.dot(a, b, preferred_element_type=F32)


def dot_nt(a, b):
    return lax.dot_general(a, b, NT, preferred_element_type=F32)


def tied(values, *others):
    leaves, tree = jax.tree.flatten(values)
    kept = lax.optimization_barrier(tuple(leaves) + tuple(jax.tree.leaves(others)))
    return jax.tree.unflatten(tree, kept[: len(leaves)])


def arrivals(rows):
    table = []
    for k in range(rows):
        line = []
        for z in range(rows):
            below, above = z, rows - 1 - z
            both = min(below, above)
            if k == 0:
                line.append((0, z))
            elif k <= 2 * both:
                step = (k + 1) // 2
                line.append((step, z - step if k % 2 else z + step))
            else:
                step = k - both
                line.append((step, z - step if below > above else z + step))
        table.append(line)
    return table


def pack_kernel(emb_ref, cid_ref, lead_ref, rest_ref):
    docs = emb_ref.shape[0]
    lead_ref[:docs, :] = emb_ref[:, :PREFIX]
    rest_ref[...] = emb_ref[:, PREFIX:]
    cid = cid_ref[...]
    high, low = (cid // DIGIT + 1).astype(F32), (cid % DIGIT).astype(F32)
    rows = []
    for digit in (high, low):
        rows += [digit[:, at : at + PREFIX] for at in range(0, docs, PREFIX)]
    rows.append(jnp.zeros((META - len(rows), PREFIX), F32))
    lead_ref[docs:, :] = jnp.concatenate(rows, axis=0).astype(BF16)


def ids_of(lead_ref):
    docs = lead_ref.shape[0] - META
    meta = lead_ref[docs:, :].astype(F32)
    parts = docs // PREFIX
    high = jnp.concatenate([meta[i : i + 1] for i in range(parts)], axis=1)
    low = jnp.concatenate([meta[parts + i : parts + i + 1] for i in range(parts)], axis=1)
    return (high - 1.0) * DIGIT + low


def prep_kernel(subs, per, place_ref, cent_ref, inv_ref, centre_ref, own_prefix_ref, prior_ref):
    clusters = cent_ref.shape[0]
    half = centre_ref.shape[1]
    z, x, h = lax.axis_index("rows"), lax.axis_index("sub"), lax.axis_index("dim")
    row = lax.broadcasted_iota(jnp.int32, (subs * per, clusters), 0)
    ids = lax.broadcasted_iota(jnp.int32, (subs * per, clusters), 1)
    turn, within = row // per, row % per
    target = (z * subs + (x + turn) % subs) * per + within
    chosen = (place_ref[...] == target).astype(F32)
    inv_ref[...] = jnp.sum(chosen * ids.astype(F32), axis=1, keepdims=True)
    columns = cent_ref[:, pl.ds(pl.multiple_of(h * half, LANES), half)]
    centre_ref[...] = dot(chosen.astype(BF16), columns).astype(BF16)
    natural = (ids == target).astype(BF16)
    own_prefix_ref[...] = dot(natural, cent_ref[:, :PREFIX]).astype(BF16)
    prior_ref[...] = dot(natural[:per], columns).astype(BF16)


def centred(pick, centre, columns):
    slots = pick.shape[0]
    groups = slots // (MOST * SUBLANES)
    width = columns.shape[1]
    present = jnp.sum(pick.astype(F32), axis=1, keepdims=True)
    raw = dot(pick, columns)
    middle = centre.astype(F32).reshape(groups, 1, SUBLANES, width)
    middle = jnp.broadcast_to(middle, (groups, MOST, SUBLANES, width)).reshape(slots, width)
    return jnp.where(present > 0.0, raw - middle, 0.0).astype(BF16)


def picked(lead_ref, inv_ref):
    cid = ids_of(lead_ref)
    docs = cid.shape[1]
    groups = inv_ref.shape[0] // SUBLANES
    match = (inv_ref[...] == cid).astype(F32)
    before = lax.broadcasted_iota(jnp.int32, (docs, docs), 0) < lax.broadcasted_iota(jnp.int32, (docs, docs), 1)
    earlier = dot(match.astype(BF16), before.astype(F32).astype(BF16))
    ranked = [jnp.where(earlier == r, match, 0.0).reshape(groups, SUBLANES, docs) for r in range(MOST)]
    return jnp.stack(ranked, axis=1).reshape(groups * MOST * SUBLANES, docs).astype(BF16)


def select_kernel(lead_ref, rest_ref, inv_ref, centre_ref, *row_refs):
    docs = rest_ref.shape[0]
    pick = picked(lead_ref, inv_ref)
    groups, packed, _ = row_refs[0].shape
    for columns, at in ((lead_ref[:docs, :], 0), (rest_ref[...], PREFIX)):
        width = columns.shape[1]
        rows = centred(pick, centre_ref[:, at : at + width], columns)
        rows = rows.reshape(len(row_refs), groups, packed, width)
        for t, ref in enumerate(row_refs):
            ref[:, :, at : at + width] = rows[t]


def select_lead_kernel(lead_ref, inv_ref, centre_ref, pick_ref, *row_refs):
    docs = lead_ref.shape[0] - META
    pick = picked(lead_ref, inv_ref)
    pick_ref[...] = pick
    rows = centred(pick, centre_ref[:, :PREFIX], lead_ref[:docs, :])
    rows = rows.reshape((len(row_refs),) + row_refs[0].shape)
    for t, ref in enumerate(row_refs):
        ref[...] = rows[t]


def select_rest_kernel(pick_ref, rest_ref, centre_ref, *row_refs):
    rows = centred(pick_ref[...], centre_ref[:, PREFIX:], rest_ref[...])
    rows = rows.reshape((len(row_refs),) + row_refs[0].shape)
    for t, ref in enumerate(row_refs):
        ref[...] = rows[t]


def soft_weights(lead_ref, near_ref, cent_ref, own_prefix_ref):
    docs = lead_ref.shape[0] - META
    h = lax.axis_index("dim")
    prefix = jnp.where(h == 0, lead_ref[:docs, :], near_ref[:docs, :])
    scores = dot_nt(cent_ref[:, :PREFIX], prefix) * TEMP
    top = jnp.max(scores, axis=0, keepdims=True)
    scale = 1.0 / jnp.sum(jnp.exp(scores - top), axis=0, keepdims=True)
    own = dot_nt(own_prefix_ref[...], prefix) * TEMP
    return jnp.where(ids_of(lead_ref) >= 0.0, jnp.exp(own - top) * scale, 0.0)


def add_lead(weights, lead_ref, old_refs, new_refs):
    docs = lead_ref.shape[0] - META
    per = new_refs[0].shape[0] - SUBLANES
    sums = dot(weights.astype(BF16), lead_ref[:docs, :])
    ones = jnp.ones((SUBLANES, docs), BF16)
    for t, new in enumerate(new_refs):
        here = slice(t * per, (t + 1) * per)
        mass = dot_nt(ones, weights[here].astype(BF16))
        if old_refs:
            old = old_refs[t]
            new[:per, :] = old[:per, :] + sums[here]
            new[per:, :] = old[per:, :]
            new[per:, :per] = old[per:, :per] + mass
        else:
            new[:per, :] = sums[here]
            new[per:, :] = jnp.zeros((SUBLANES, new.shape[1]), F32)
            new[per:, :per] = mass


def add_rest(weights, rest_ref, old_refs, new_refs):
    per = new_refs[0].shape[0]
    sums = dot(weights, rest_ref[...])
    for t, new in enumerate(new_refs):
        part = sums[t * per : (t + 1) * per]
        new[...] = old_refs[t][...] + part if old_refs else part


def sums_kernel(subs, lead_ref, rest_ref, near_ref, cent_ref, own_prefix_ref, *refs):
    old, new = refs[: -2 * subs], refs[-2 * subs :]
    weights = soft_weights(lead_ref, near_ref, cent_ref, own_prefix_ref)
    add_lead(weights, lead_ref, old[:subs], new[:subs])
    add_rest(weights.astype(BF16), rest_ref, old[subs:], new[subs:])


def sums_lead_kernel(subs, lead_ref, near_ref, cent_ref, own_prefix_ref, *refs):
    old, weights_ref, new = refs[:subs], refs[subs], refs[subs + 1 :]
    weights = soft_weights(lead_ref, near_ref, cent_ref, own_prefix_ref)
    weights_ref[...] = weights.astype(BF16)
    add_lead(weights, lead_ref, old, new)


def sums_rest_kernel(subs, weights_ref, rest_ref, *refs):
    add_rest(weights_ref[...], rest_ref, refs[:subs], refs[subs:])


def gram_kernel(table, subs, *refs):
    *member_refs, gram_ref, held = refs
    z, x = lax.axis_index("rows"), lax.axis_index("sub")
    owners, groups, packed, half = held.shape
    each = len(member_refs) // subs
    for t in range(subs):
        column = member_refs[t * each : (t + 1) * each]
        for k, line in enumerate(table):
            source = sum(jnp.where(z == i, at, 0) for i, (_, at) in enumerate(line))
            row = source * subs + (x - t + subs) % subs
            if k < len(table) - 1:
                held[row] = column[k][...]
            else:
                held[row, :, :, :PREFIX] = column[k][...]
                held[row, :, :, PREFIX:] = column[k + 1][...]

    size = owners * packed
    lane = lax.broadcasted_iota(jnp.int32, (1, SUBLANES, size), 2) % SUBLANES
    same = (lane == lax.broadcasted_iota(jnp.int32, (1, SUBLANES, size), 1)).astype(F32)
    tile = min(size, 2 * LANES)
    for g in range(groups):
        mine = held[:, g].reshape(size, half)
        for start in range(0, size, tile):
            part = dot_nt(mine[start : start + tile], mine)
            part = part.reshape(tile // SUBLANES, SUBLANES, size)
            gram_ref[g, start // SUBLANES : (start + tile) // SUBLANES, :] = jnp.sum(part * same, axis=1)


def similarity_kernel(width, mine_ref, other_ref, out_ref):
    groups, slots, size = mine_ref.shape
    kept = out_ref.shape[1]
    h = lax.axis_index("dim")
    start = pl.multiple_of(h * kept, kept)
    row = lax.broadcasted_iota(jnp.int32, (slots, size), 0)
    lane = lax.broadcasted_iota(jnp.int32, (slots, size), 1)
    diagonal = row == lane // SUBLANES
    kept_row = lax.broadcasted_iota(jnp.int32, (kept, size), 0) + start
    kept_lane = lax.broadcasted_iota(jnp.int32, (kept, size), 1)
    kept_diagonal = kept_row == kept_lane // SUBLANES
    for g in range(groups):
        total = mine_ref[g] + other_ref[g]
        norms = jnp.sum(jnp.where(diagonal, total, 0.0), axis=0, keepdims=True)
        scale = lax.rsqrt(norms / width + EPS)
        spread = jnp.where(kept_diagonal, jnp.broadcast_to(scale, (kept, size)), 0.0)
        folded = spread[:, :LANES]
        for at in range(LANES, size, LANES):
            folded = folded + spread[:, at : at + LANES]
        step = SUBLANES
        while step < LANES:
            folded = folded + pltpu.roll(folded, step, 1)
            step *= 2
        row_scale = jnp.concatenate([folded] * (size // LANES), axis=1)
        own = mine_ref[g, pl.ds(start, kept), :] + other_ref[g, pl.ds(start, kept), :]
        out_ref[g] = (own / width * row_scale * scale).astype(BF16)


def centroid_kernel(*refs):
    *part_refs, prior_ref, out_ref = refs
    subs = len(part_refs) // 2
    lead = sum(ref[...] for ref in part_refs[1:subs]) + part_refs[0][...]
    rest = sum(ref[...] for ref in part_refs[subs + 1 :]) + part_refs[subs][...]
    per = rest.shape[0]
    mass = jnp.transpose(lead[per:, :LANES])[:per, :1] + SMOOTH
    prior = SMOOTH * prior_ref[...].astype(F32)
    out_ref[:, :PREFIX] = (lead[:per] + prior[:, :PREFIX]) / mass
    out_ref[:, PREFIX:] = (rest + prior[:, PREFIX:]) / mass


def shards(embeddings, centroids, cluster_id, cluster_place):
    docs, half = embeddings.shape
    clusters, width = centroids.shape
    rows, subs = lax.axis_size("rows"), lax.axis_size("sub")
    owners = rows * subs
    per = clusters // owners
    groups = per // SUBLANES
    packed = MOST * SUBLANES
    slots = owners * MOST
    table = arrivals(rows)
    z = lax.axis_index("rows")
    shape = jax.ShapeDtypeStruct

    def along(value, pairs):
        return lax.ppermute(value, "rows", pairs)

    def across(values):
        got = [values[0]]
        for t in range(1, subs):
            got.append(lax.ppermute(values[t], "sub", [(i, (i + t) % subs) for i in range(subs)]))
        return got

    def near(value):
        return lax.ppermute(value, "dim", [(0, 1), (1, 0)])

    def upward(step):
        return [(i, i + 1) for i in range(step - 1, rows - 1)]

    def downward(step):
        return [(i, i - 1) for i in range(1, rows - step + 1)]

    def send(step, held):
        if len(held) == 1:
            return (along(held[0], upward(step) + downward(step)),)
        return (along(held[0], upward(step)), along(held[1], downward(step)))

    def merged(step, held):
        if len(held) == 2 and 2 * step >= rows:
            return (jnp.where(z >= step, held[0], held[1]),)
        return held

    def slot_block(k, history):
        kinds = {}
        for i, (step, source) in enumerate(table[k]):
            side = 0 if source < i or len(history[step]) == 1 else 1
            kinds.setdefault((step, side), []).append(i)
        (step, side), *others = sorted(kinds, key=lambda kind: -len(kinds[kind]))
        value = history[step][side]
        for kind in others:
            here = functools.reduce(jnp.logical_or, [z == i for i in kinds[kind]])
            value = jnp.where(here, history[kind[0]][kind[1]], value)
        return value

    lead, rest = call(
        pack_kernel,
        "pack",
        [shape((docs + META, PREFIX), BF16), shape((docs, half - PREFIX), BF16)],
        [embeddings, cluster_id.reshape(1, docs)],
    )
    leads, rests = {0: (lead,)}, {0: (rest,)}
    sending_lead = send(1, (lead, lead))
    sending_rest = send(1, (rest, rest))

    inv, centre, own_prefix, prior = call(
        functools.partial(prep_kernel, subs, per),
        "prep",
        [
            shape((subs * per, 1), F32),
            shape((subs * per, half), BF16),
            shape((subs * per, PREFIX), BF16),
            shape((per, half), BF16),
        ],
        [cluster_place.reshape(1, clusters), centroids],
    )

    lead_sum, rest_sum = shape((per + SUBLANES, PREFIX), F32), shape((per, half - PREFIX), F32)
    sum_shapes = [lead_sum] * subs + [rest_sum] * subs
    score_flops = 2 * docs * clusters * PREFIX
    pick_flops = 2 * docs * MOST * subs * per * half

    def select(lead, rest):
        found = call(
            select_kernel, "select", [shape((groups, packed, half), BF16)] * subs, [lead, rest, inv, centre],
            flops=pick_flops,
        )
        return list(found)

    def add(lead, rest, prefix, sums):
        operands = [lead, rest, prefix, centroids, own_prefix] + sums
        return list(
            call(
                functools.partial(sums_kernel, subs), "sums", sum_shapes, operands,
                aliases={5 + i: i for i in range(len(sums))},
                flops=score_flops, transcendentals=docs * clusters,
            )
        )

    members = [[] for _ in range(subs)]

    def keep(found):
        for column, value in zip(members, found):
            column.append(value)

    prefix = near(lead)
    found = select(lead, rest)
    got = across(found)
    keep(got)
    sums = add(lead, rest, prefix, [])
    for step in range(1, rows):
        last = step == rows - 1
        leads[step] = merged(step, sending_lead)
        if not last:
            leads[step] = tied(leads[step], found)
            sending_lead = send(step + 1, leads[step])
        else:
            leads[step] = tied(leads[step], found, sums)
        lead = slot_block(step, leads)
        prefix = near(lead)
        if last:
            break
        rests[step] = merged(step, sending_rest)
        rests[step] = tied(rests[step], sums, got)
        sending_rest = send(step + 1, rests[step])
        rest = slot_block(step, rests)
        found = select(lead, rest)
        got = across(found)
        keep(got)
        sums = add(lead, rest, prefix, sums)

    half_rows = [shape((groups, packed, PREFIX), BF16)] * subs
    pick, *found = call(
        select_lead_kernel, "select_lead", [shape((subs * per * MOST, docs), BF16)] + half_rows, [lead, inv, centre],
        flops=pick_flops // 2,
    )
    keep(across(found))
    weights, *lead_sums = call(
        functools.partial(sums_lead_kernel, subs), "sums_lead", [shape((subs * per, docs), BF16)] + [lead_sum] * subs,
        [lead, prefix, centroids, own_prefix] + sums[:subs],
        aliases={4 + i: 1 + i for i in range(subs)},
        flops=score_flops, transcendentals=docs * clusters,
    )
    lead_sums = across(lead_sums)
    rests[rows - 1] = tied(merged(rows - 1, sending_rest), weights, found, pick)
    rest = slot_block(rows - 1, rests)
    half_rows = [shape((groups, packed, half - PREFIX), BF16)] * subs
    found = call(select_rest_kernel, "select_rest", half_rows, [pick, rest, centre], flops=pick_flops // 2)
    keep(across(found))
    rest_sums = call(
        functools.partial(sums_rest_kernel, subs), "sums_rest", [rest_sum] * subs, [weights, rest] + sums[subs:],
        aliases={2 + i: i for i in range(subs)},
    )
    rest_sums = across(rest_sums)

    (gram,) = call(
        functools.partial(gram_kernel, table, subs),
        "gram",
        [shape((groups, slots, slots * SUBLANES), F32)],
        [ref for column in members for ref in column],
        scratch=[pltpu.VMEM((owners, groups, packed, half), BF16)],
    )
    (tiles,) = call(
        functools.partial(similarity_kernel, width),
        "similarity",
        [shape((groups, slots // 2, slots * SUBLANES), BF16)],
        [gram, near(gram)],
    )
    tiles = tiles.reshape(groups, slots // 2, slots, SUBLANES)
    similarity = jnp.transpose(tiles, (0, 3, 1, 2)).reshape(per, slots // 2, slots)
    (new_centroids,) = call(centroid_kernel, "centroids", [shape((per, half), F32)], lead_sums + rest_sums + [prior])
    return (new_centroids, similarity)


def solution(mesh):
    in_specs = (
        P(("parts", "rows", "sub"), "dim"),
        P("parts", None),
        P(("parts", "rows", "sub"), None),
        P(),
    )
    out_specs = (P(("parts", "rows", "sub"), "dim"), P(("parts", "rows", "sub"), "dim", None))
    return jax.shard_map(shards, mesh=mesh, in_specs=in_specs, out_specs=out_specs, check_vma=False)
```

```python
import functools

import jax
import jax.numpy as jnp
from jax import lax
from jax.experimental import pallas as pl
from jax.experimental.pallas import tpu as pltpu
from jax.sharding import PartitionSpec as P

PREFIX = 256
MOST = 2

TEMP = 0.125
SMOOTH = 1.0
EPS = 1e-05

DIGIT = 32
META = 16
SUBLANES = 8
LANES = 128
F32 = jnp.float32
BF16 = jnp.bfloat16
VMEM_LIMIT = 40 * 1024 * 1024

NT = (((1,), (1,)), ((), ()))


def call(kernel, name, out_shape, operands, aliases=None, scratch=(), far=0, cost=0):
    def place(at):
        return pl.BlockSpec(memory_space=pltpu.HBM if at < far else pltpu.VMEM)

    return pl.pallas_call(
        kernel,
        out_shape=tuple(out_shape),
        in_specs=[place(at) for at in range(len(operands))],
        out_specs=tuple(pl.BlockSpec(memory_space=pltpu.VMEM) for _ in out_shape),
        input_output_aliases=aliases or {},
        scratch_shapes=list(scratch),
        compiler_params=pltpu.CompilerParams(vmem_limit_bytes=VMEM_LIMIT),
        cost_estimate=pl.CostEstimate(flops=50 * cost, bytes_accessed=cost, transcendentals=0),
        name=name,
    )(*operands)


def dot(a, b):
    return jnp.dot(a, b, preferred_element_type=F32)


def dot_nt(a, b):
    return lax.dot_general(a, b, NT, preferred_element_type=F32)


def tied(values, *others):
    leaves, tree = jax.tree.flatten(values)
    kept = lax.optimization_barrier(tuple(leaves) + tuple(jax.tree.leaves(others)))
    return jax.tree.unflatten(tree, kept[: len(leaves)])


def arrivals(rows):
    table = []
    for z in range(rows):
        line = [(0, 0, z)]
        for step in range(1, rows):
            for kind in range(2):
                source = z + step if z % 2 == kind else z - step
                if 0 <= source < rows:
                    line.append((step, kind, source))
        table.append(line)
    return [[table[z][k] for z in range(rows)] for k in range(rows)]


def pairs_of(rows, kind):
    other = list(range(rows))
    for i in range(kind, rows - 1, 2):
        other[i], other[i + 1] = i + 1, i
    return list(enumerate(other))


def pack_kernel(emb_ref, cid_ref, lead_ref, rest_ref, cid_held, sems):
    docs = emb_ref.shape[0]
    copies = [
        pltpu.make_async_copy(cid_ref, cid_held, sems.at[0]),
        pltpu.make_async_copy(emb_ref.at[:, :PREFIX], lead_ref.at[:docs, :], sems.at[1]),
        pltpu.make_async_copy(emb_ref.at[:, PREFIX:], rest_ref, sems.at[2]),
    ]
    for copy in copies:
        copy.start()
    copies[0].wait()
    cid = cid_held[...]
    high, low = (cid // DIGIT + 1).astype(F32), (cid % DIGIT).astype(F32)
    rows = []
    for digit in (high, low):
        rows += [digit[:, at : at + PREFIX] for at in range(0, docs, PREFIX)]
    rows.append(jnp.zeros((META - len(rows), PREFIX), F32))
    lead_ref[docs:, :] = jnp.concatenate(rows, axis=0).astype(BF16)
    for copy in copies[1:]:
        copy.wait()


def ids_of(lead_ref):
    docs = lead_ref.shape[0] - META
    meta = lead_ref[docs:, :].astype(F32)
    parts = docs // PREFIX
    high = jnp.concatenate([meta[i : i + 1] for i in range(parts)], axis=1)
    low = jnp.concatenate([meta[parts + i : parts + i + 1] for i in range(parts)], axis=1)
    return (high - 1.0) * DIGIT + low


def prep_kernel(
    subs, per, place_ref, cent_ref, inv_ref, centre_ref, own_prefix_ref, prior_ref, prefix_ref, place_held, columns_held, sems
):
    clusters = cent_ref.shape[0]
    half = centre_ref.shape[1]
    z, x, h = lax.axis_index("rows"), lax.axis_index("sub"), lax.axis_index("dim")
    copies = [
        pltpu.make_async_copy(place_ref, place_held, sems.at[0]),
        pltpu.make_async_copy(cent_ref.at[:, pl.ds(pl.multiple_of(h * half, LANES), half)], columns_held, sems.at[1]),
        pltpu.make_async_copy(cent_ref.at[:, :PREFIX], prefix_ref, sems.at[2]),
    ]
    for copy in copies:
        copy.start()
    row = lax.broadcasted_iota(jnp.int32, (subs * per, clusters), 0)
    ids = lax.broadcasted_iota(jnp.int32, (subs * per, clusters), 1)
    turn, within = row // per, row % per
    target = (z * subs + (x + turn) % subs) * per + within
    natural = (ids == target).astype(BF16)
    copies[0].wait()
    chosen = (place_held[...] == target).astype(F32)
    inv_ref[...] = jnp.sum(chosen * ids.astype(F32), axis=1, keepdims=True)
    copies[1].wait()
    columns = columns_held[...]
    centre_ref[...] = dot(chosen.astype(BF16), columns).astype(BF16)
    prior_ref[...] = dot(natural[:per], columns).astype(BF16)
    copies[2].wait()
    own_prefix_ref[...] = dot(natural, prefix_ref[...]).astype(BF16)


def centred(pick, centre, columns):
    slots = pick.shape[0]
    groups = slots // (MOST * SUBLANES)
    width = columns.shape[1]
    present = jnp.sum(pick.astype(F32), axis=1, keepdims=True)
    raw = dot(pick, columns)
    middle = centre.astype(F32).reshape(groups, 1, SUBLANES, width)
    middle = jnp.broadcast_to(middle, (groups, MOST, SUBLANES, width)).reshape(slots, width)
    return jnp.where(present > 0.0, raw - middle, 0.0).astype(BF16)


def picked(lead_ref, inv_ref):
    cid = ids_of(lead_ref)
    docs = cid.shape[1]
    groups = inv_ref.shape[0] // SUBLANES
    match = (inv_ref[...] == cid).astype(F32)
    before = lax.broadcasted_iota(jnp.int32, (docs, docs), 0) < lax.broadcasted_iota(jnp.int32, (docs, docs), 1)
    earlier = dot(match.astype(BF16), before.astype(F32).astype(BF16))
    ranked = [jnp.where(earlier == r, match, 0.0).reshape(groups, SUBLANES, docs) for r in range(MOST)]
    return jnp.stack(ranked, axis=1).reshape(groups * MOST * SUBLANES, docs).astype(BF16)


def select_kernel(lead_ref, rest_ref, inv_ref, centre_ref, *row_refs):
    docs = rest_ref.shape[0]
    pick = picked(lead_ref, inv_ref)
    groups, packed, _ = row_refs[0].shape
    for columns, at in ((lead_ref[:docs, :], 0), (rest_ref[...], PREFIX)):
        width = columns.shape[1]
        rows = centred(pick, centre_ref[:, at : at + width], columns)
        rows = rows.reshape(len(row_refs), groups, packed, width)
        for t, ref in enumerate(row_refs):
            ref[:, :, at : at + width] = rows[t]


def select_lead_kernel(lead_ref, inv_ref, centre_ref, pick_ref, *row_refs):
    docs = lead_ref.shape[0] - META
    pick = picked(lead_ref, inv_ref)
    pick_ref[...] = pick
    rows = centred(pick, centre_ref[:, :PREFIX], lead_ref[:docs, :])
    rows = rows.reshape((len(row_refs),) + row_refs[0].shape)
    for t, ref in enumerate(row_refs):
        ref[...] = rows[t]


def select_rest_kernel(pick_ref, rest_ref, centre_ref, *row_refs):
    rows = centred(pick_ref[...], centre_ref[:, PREFIX:], rest_ref[...])
    rows = rows.reshape((len(row_refs),) + row_refs[0].shape)
    for t, ref in enumerate(row_refs):
        ref[...] = rows[t]


def soft_weights(lead_ref, near_ref, cent_ref, own_prefix_ref):
    docs = lead_ref.shape[0] - META
    h = lax.axis_index("dim")
    prefix = jnp.where(h == 0, lead_ref[:docs, :], near_ref[:docs, :])
    scores = dot_nt(cent_ref[...], prefix) * TEMP
    top = jnp.max(scores, axis=0, keepdims=True)
    scale = 1.0 / jnp.sum(jnp.exp(scores - top), axis=0, keepdims=True)
    own = dot_nt(own_prefix_ref[...], prefix) * TEMP
    return jnp.where(ids_of(lead_ref) >= 0.0, jnp.exp(own - top) * scale, 0.0)


def add_lead(weights, lead_ref, old_refs, new_refs):
    docs = lead_ref.shape[0] - META
    per = new_refs[0].shape[0] - SUBLANES
    sums = dot(weights.astype(BF16), lead_ref[:docs, :])
    ones = jnp.ones((SUBLANES, docs), BF16)
    for t, new in enumerate(new_refs):
        here = slice(t * per, (t + 1) * per)
        mass = dot_nt(ones, weights[here].astype(BF16))
        if old_refs:
            old = old_refs[t]
            new[:per, :] = old[:per, :] + sums[here]
            new[per:, :] = old[per:, :]
            new[per:, :per] = old[per:, :per] + mass
        else:
            new[:per, :] = sums[here]
            new[per:, :] = jnp.zeros((SUBLANES, new.shape[1]), F32)
            new[per:, :per] = mass


def add_rest(weights, rest_ref, old_refs, new_refs):
    per = new_refs[0].shape[0]
    sums = dot(weights, rest_ref[...])
    for t, new in enumerate(new_refs):
        part = sums[t * per : (t + 1) * per]
        new[...] = old_refs[t][...] + part if old_refs else part


def sums_kernel(subs, lead_ref, rest_ref, near_ref, cent_ref, own_prefix_ref, *refs):
    old, new = refs[: -2 * subs], refs[-2 * subs :]
    weights = soft_weights(lead_ref, near_ref, cent_ref, own_prefix_ref)
    add_lead(weights, lead_ref, old[:subs], new[:subs])
    add_rest(weights.astype(BF16), rest_ref, old[subs:], new[subs:])


def sums_lead_kernel(subs, lead_ref, near_ref, cent_ref, own_prefix_ref, *refs):
    old, weights_ref, new = refs[:subs], refs[subs], refs[subs + 1 :]
    weights = soft_weights(lead_ref, near_ref, cent_ref, own_prefix_ref)
    weights_ref[...] = weights.astype(BF16)
    add_lead(weights, lead_ref, old, new)


def sums_rest_kernel(subs, weights_ref, rest_ref, *refs):
    add_rest(weights_ref[...], rest_ref, refs[:subs], refs[subs:])


def gram_kernel(table, subs, *refs):
    *member_refs, gram_ref, held = refs
    z, x = lax.axis_index("rows"), lax.axis_index("sub")
    owners, groups, packed, half = held.shape
    each = len(member_refs) // subs
    for t in range(subs):
        column = member_refs[t * each : (t + 1) * each]
        for k, line in enumerate(table):
            source = sum(jnp.where(z == i, at, 0) for i, (_, _, at) in enumerate(line))
            row = source * subs + (x - t + subs) % subs
            if k < len(table) - 1:
                held[row] = column[k][...]
            else:
                held[row, :, :, :PREFIX] = column[k][...]
                held[row, :, :, PREFIX:] = column[k + 1][...]

    size = owners * packed
    lane = lax.broadcasted_iota(jnp.int32, (1, SUBLANES, size), 2) % SUBLANES
    same = (lane == lax.broadcasted_iota(jnp.int32, (1, SUBLANES, size), 1)).astype(F32)
    tile = min(size, 2 * LANES)
    for g in range(groups):
        mine = held[:, g].reshape(size, half)
        for start in range(0, size, tile):
            part = dot_nt(mine[start : start + tile], mine)
            part = part.reshape(tile // SUBLANES, SUBLANES, size)
            gram_ref[g, start // SUBLANES : (start + tile) // SUBLANES, :] = jnp.sum(part * same, axis=1)


def scaled_tiles(width, mine_ref, other_ref, scaled_ref):
    groups, slots, size = mine_ref.shape
    kept = scaled_ref.shape[1]
    h = lax.axis_index("dim")
    start = pl.multiple_of(h * kept, kept)
    row = lax.broadcasted_iota(jnp.int32, (slots, size), 0)
    lane = lax.broadcasted_iota(jnp.int32, (slots, size), 1)
    diagonal = row == lane // SUBLANES
    kept_row = lax.broadcasted_iota(jnp.int32, (kept, size), 0) + start
    kept_lane = lax.broadcasted_iota(jnp.int32, (kept, size), 1)
    kept_diagonal = kept_row == kept_lane // SUBLANES
    for g in range(groups):
        total = mine_ref[g] + other_ref[g]
        norms = jnp.sum(jnp.where(diagonal, total, 0.0), axis=0, keepdims=True)
        scale = lax.rsqrt(norms / width + EPS)
        spread = jnp.where(kept_diagonal, jnp.broadcast_to(scale, (kept, size)), 0.0)
        folded = spread[:, :LANES]
        for at in range(LANES, size, LANES):
            folded = folded + spread[:, at : at + LANES]
        step = SUBLANES
        while step < LANES:
            folded = folded + pltpu.roll(folded, step, 1)
            step *= 2
        row_scale = jnp.concatenate([folded] * (size // LANES), axis=1)
        own = mine_ref[g, pl.ds(start, kept), :] + other_ref[g, pl.ds(start, kept), :]
        scaled_ref[g] = own / width * row_scale * scale


def finish_kernel(width, mine_ref, other_ref, *refs):
    *part_refs, prior_ref, new_ref, tile_ref, scaled_ref = refs
    subs = len(part_refs) // 2
    lead = sum(ref[...] for ref in part_refs[1:subs]) + part_refs[0][...]
    rest = sum(ref[...] for ref in part_refs[subs + 1 :]) + part_refs[subs][...]
    per = rest.shape[0]
    mass = jnp.transpose(lead[per:, :LANES])[:per, :1] + SMOOTH
    prior = SMOOTH * prior_ref[...].astype(F32)
    new_ref[:, :PREFIX] = (lead[:per] + prior[:, :PREFIX]) / mass
    new_ref[:, PREFIX:] = (rest + prior[:, PREFIX:]) / mass

    scaled_tiles(width, mine_ref, other_ref, scaled_ref)
    groups, kept, size = scaled_ref.shape
    slots = size // SUBLANES
    at = lax.broadcasted_iota(jnp.int32, (groups * size, per), 0)
    to = lax.broadcasted_iota(jnp.int32, (groups * size, per), 1)
    move = ((at // size == to // SUBLANES) & (at % SUBLANES == to % SUBLANES)).astype(F32).astype(BF16)
    row = lax.broadcasted_iota(jnp.int32, (slots, size), 0)
    lane = lax.broadcasted_iota(jnp.int32, (slots, size), 1)
    here = row == lane // SUBLANES
    batch = max(1, LANES // slots)

    def some(step, carry):
        spread = []
        for b in range(batch):
            i = step * batch + b
            lines = [jnp.broadcast_to(scaled_ref[g, pl.ds(i, 1), :], (slots, size)) for g in range(groups)]
            spread.append(jnp.concatenate([jnp.where(here, line, 0.0) for line in lines], axis=1))
        moved = dot(jnp.concatenate(spread, axis=0).astype(BF16), move).astype(BF16)
        for b in range(batch):
            tile_ref[step * batch + b] = moved[b * slots : (b + 1) * slots]
        return carry

    if kept == batch:
        some(0, 0)
    else:
        lax.fori_loop(0, kept // batch, some, 0)


def shards(embeddings, centroids, cluster_id, cluster_place):
    docs, half = embeddings.shape
    clusters, width = centroids.shape
    rows, subs = lax.axis_size("rows"), lax.axis_size("sub")
    owners = rows * subs
    per = clusters // owners
    groups = per // SUBLANES
    packed = MOST * SUBLANES
    slots = owners * MOST
    table = arrivals(rows)
    z = lax.axis_index("rows")
    shape = jax.ShapeDtypeStruct

    def across(values):
        got = [values[0]]
        for t in range(1, subs):
            got.append(lax.ppermute(values[t], "sub", [(i, (i + t) % subs) for i in range(subs)]))
        return got

    def near(value):
        return lax.ppermute(value, "dim", [(0, 1), (1, 0)])

    def needed(step, kind):
        return any((step, kind) in [entry[:2] for entry in line] for line in table)

    def swap(step, held):
        return [
            lax.ppermute(held[1 - kind], "rows", pairs_of(rows, kind)) if needed(step, kind) else None for kind in range(2)
        ]

    def slot_block(k, history):
        kinds = {}
        for i, (step, kind, _) in enumerate(table[k]):
            kinds.setdefault((step, kind), []).append(i)
        (step, kind), *others = sorted(kinds, key=lambda key: (-len(kinds[key]), key))
        value = history[step][kind]
        for step, kind in others:
            here = functools.reduce(jnp.logical_or, [z == i for i in kinds[step, kind]])
            value = jnp.where(here, history[step][kind], value)
        return value

    lead, rest = call(
        pack_kernel,
        "pack",
        [shape((docs + META, PREFIX), BF16), shape((docs, half - PREFIX), BF16)],
        [embeddings, cluster_id.reshape(1, docs)],
        scratch=[pltpu.VMEM((1, docs), jnp.int32), pltpu.SemaphoreType.DMA((3,))],
        far=2,
    )
    leads, rests = {0: [lead, lead]}, {0: [rest, rest]}
    sending_lead = swap(1, leads[0])
    sending_rest = swap(1, rests[0])

    inv, centre, own_prefix, prior, cent_prefix = call(
        functools.partial(prep_kernel, subs, per),
        "prep",
        [
            shape((subs * per, 1), F32),
            shape((subs * per, half), BF16),
            shape((subs * per, PREFIX), BF16),
            shape((per, half), BF16),
            shape((clusters, PREFIX), BF16),
        ],
        [cluster_place.reshape(1, clusters), centroids],
        scratch=[
            pltpu.VMEM((1, clusters), jnp.int32),
            pltpu.VMEM((clusters, half), BF16),
            pltpu.SemaphoreType.DMA((3,)),
        ],
        far=2,
        cost=4 * 1024 * 1024,
    )

    lead_sum, rest_sum = shape((per + SUBLANES, PREFIX), F32), shape((per, half - PREFIX), F32)
    sum_shapes = [lead_sum] * subs + [rest_sum] * subs
    own_cost, other_cost = 2 * 1024 * 1024, 128 * 1024

    def select(lead, rest, cost):
        found = call(select_kernel, "select", [shape((groups, packed, half), BF16)] * subs, [lead, rest, inv, centre], cost=cost)
        return list(found)

    def add(lead, rest, prefix, sums, cost):
        operands = [lead, rest, prefix, cent_prefix, own_prefix] + sums
        aliases = {5 + i: i for i in range(len(sums))}
        return list(call(functools.partial(sums_kernel, subs), "sums", sum_shapes, operands, aliases, cost=cost))

    members = []

    prefix = near(lead)
    found = select(lead, rest, own_cost)
    members.append(across(found))
    sums = add(lead, rest, prefix, [], own_cost)
    for step in range(1, rows):
        last = step == rows - 1
        leads[step] = tied(sending_lead, found, members[: step - 1], *([sums] if last else []))
        if not last:
            sending_lead = swap(step + 1, leads[step])
        lead = slot_block(step, leads)
        prefix = near(lead)
        if last:
            break
        rests[step] = tied(sending_rest, sums)
        sending_rest = swap(step + 1, rests[step])
        rest = slot_block(step, rests)
        found = select(lead, rest, own_cost)
        members.append(across(found))
        sums = add(lead, rest, prefix, sums, other_cost)

    half_rows = [shape((groups, packed, PREFIX), BF16)] * subs
    pick, *found = call(
        select_lead_kernel, "select_lead", [shape((subs * per * MOST, docs), BF16)] + half_rows, [lead, inv, centre],
        cost=other_cost,
    )
    lead_found = found
    weights, *lead_sums = call(
        functools.partial(sums_lead_kernel, subs),
        "sums_lead",
        [shape((subs * per, docs), BF16)] + [lead_sum] * subs,
        [lead, prefix, cent_prefix, own_prefix] + sums[:subs],
        {4 + i: 1 + i for i in range(subs)},
        cost=other_cost,
    )
    members.append(across(tied(lead_found, members[: rows - 1])))
    lead_sums = across(lead_sums)
    rests[rows - 1] = tied(sending_rest, weights, found, pick, members[: rows - 1])
    rest = slot_block(rows - 1, rests)
    half_rows = [shape((groups, packed, half - PREFIX), BF16)] * subs
    found = call(select_rest_kernel, "select_rest", half_rows, [pick, rest, centre], cost=other_cost)
    members.append(across(found))
    rest_sums = call(
        functools.partial(sums_rest_kernel, subs),
        "sums_rest",
        [rest_sum] * subs,
        [weights, rest] + sums[subs:],
        {2 + i: i for i in range(subs)},
    )
    rest_sums = across(rest_sums)

    (gram,) = call(
        functools.partial(gram_kernel, table, subs),
        "gram",
        [shape((groups, slots, slots * SUBLANES), F32)],
        [arrays[t] for t in range(subs) for arrays in members],
        scratch=[pltpu.VMEM((owners, groups, packed, half), BF16)],
    )
    new_centroids, tiles = call(
        functools.partial(finish_kernel, width),
        "finish",
        [shape((per, half), F32), shape((slots // 2, slots, per), BF16)],
        [gram, near(gram)] + lead_sums + rest_sums + [prior],
        scratch=[pltpu.VMEM((groups, slots // 2, slots * SUBLANES), F32)],
    )
    return (new_centroids, jnp.transpose(tiles, (2, 0, 1)))


def solution(mesh):
    in_specs = (
        P(("parts", "rows", "sub"), "dim"),
        P("parts", None),
        P(("parts", "rows", "sub"), None),
        P(),
    )
    out_specs = (P(("parts", "rows", "sub"), "dim"), P(("parts", "rows", "sub"), "dim", None))
    return jax.shard_map(shards, mesh=mesh, in_specs=in_specs, out_specs=out_specs, check_vma=False)
```

```python
import functools

import jax
import jax.numpy as jnp
from jax import lax
from jax.experimental import pallas as pl
from jax.experimental.pallas import tpu as pltpu
from jax.sharding import PartitionSpec as P

PREFIX = 256
MOST = 2

TEMP = 0.125
SMOOTH = 1.0
EPS = 1e-05

DIGIT = 32
META = 16
SUBLANES = 8
LANES = 128
F32 = jnp.float32
BF16 = jnp.bfloat16
VMEM_LIMIT = 40 * 1024 * 1024

NT = (((1,), (1,)), ((), ()))


def call(kernel, name, out_shape, operands, aliases=None, scratch=(), far=0, cost=0):
    def place(at):
        return pl.BlockSpec(memory_space=pltpu.HBM if at < far else pltpu.VMEM)

    return pl.pallas_call(
        kernel,
        out_shape=tuple(out_shape),
        in_specs=[place(at) for at in range(len(operands))],
        out_specs=tuple(pl.BlockSpec(memory_space=pltpu.VMEM) for _ in out_shape),
        input_output_aliases=aliases or {},
        scratch_shapes=list(scratch),
        compiler_params=pltpu.CompilerParams(vmem_limit_bytes=VMEM_LIMIT),
        cost_estimate=pl.CostEstimate(flops=50 * cost, bytes_accessed=cost, transcendentals=0),
        name=name,
    )(*operands)


def dot(a, b):
    return jnp.dot(a, b, preferred_element_type=F32)


def dot_nt(a, b):
    return lax.dot_general(a, b, NT, preferred_element_type=F32)


def tied(values, *others):
    leaves, tree = jax.tree.flatten(values)
    kept = lax.optimization_barrier(tuple(leaves) + tuple(jax.tree.leaves(others)))
    return jax.tree.unflatten(tree, kept[: len(leaves)])


def arrivals(rows):
    table = []
    for z in range(rows):
        line = [(0, 0, z)]
        for step in range(1, rows):
            for kind in range(2):
                source = z + step if z % 2 == kind else z - step
                if 0 <= source < rows:
                    line.append((step, kind, source))
        table.append(line)
    return [[table[z][k] for z in range(rows)] for k in range(rows)]


def pairs_of(rows, kind):
    other = list(range(rows))
    for i in range(kind, rows - 1, 2):
        other[i], other[i + 1] = i + 1, i
    return list(enumerate(other))


def pack_kernel(emb_ref, cid_ref, block_ref):
    docs, half = emb_ref.shape
    block_ref[:docs, :] = emb_ref[...]
    cid = cid_ref[...]
    high, low = (cid // DIGIT + 1).astype(F32), (cid % DIGIT).astype(F32)
    rows = []
    for digit in (high, low):
        rows += [digit[:, at : at + PREFIX] for at in range(0, docs, PREFIX)]
    rows.append(jnp.zeros((META - len(rows), PREFIX), F32))
    block_ref[docs:, :PREFIX] = jnp.concatenate(rows, axis=0).astype(BF16)
    block_ref[docs:, PREFIX:] = jnp.zeros((META, half - PREFIX), BF16)


def ids_of(lead_ref):
    docs = lead_ref.shape[0] - META
    meta = lead_ref[docs:, :PREFIX].astype(F32)
    parts = docs // PREFIX
    high = jnp.concatenate([meta[i : i + 1] for i in range(parts)], axis=1)
    low = jnp.concatenate([meta[parts + i : parts + i + 1] for i in range(parts)], axis=1)
    return (high - 1.0) * DIGIT + low


def prep_kernel(subs, per, place_ref, cent_ref, inv_ref, centre_ref, own_prefix_ref, prior_ref, prefix_ref):
    clusters = cent_ref.shape[0]
    half = centre_ref.shape[1]
    z, x, h = lax.axis_index("rows"), lax.axis_index("sub"), lax.axis_index("dim")
    row = lax.broadcasted_iota(jnp.int32, (subs * per, clusters), 0)
    ids = lax.broadcasted_iota(jnp.int32, (subs * per, clusters), 1)
    turn, within = row // per, row % per
    target = (z * subs + (x + turn) % subs) * per + within
    chosen = (place_ref[...] == target).astype(F32)
    inv_ref[...] = jnp.sum(chosen * ids.astype(F32), axis=1, keepdims=True)
    columns = cent_ref[:, pl.ds(pl.multiple_of(h * half, LANES), half)]
    centre_ref[...] = dot(chosen.astype(BF16), columns).astype(BF16)
    natural = (ids == target).astype(BF16)
    prior_ref[...] = dot(natural[:per], columns).astype(BF16)
    prefix_ref[...] = cent_ref[:, :PREFIX]
    own_prefix_ref[...] = dot(natural, prefix_ref[...]).astype(BF16)


def centred(pick, centre, columns):
    slots = pick.shape[0]
    groups = slots // (MOST * SUBLANES)
    width = columns.shape[1]
    present = jnp.sum(pick.astype(F32), axis=1, keepdims=True)
    raw = dot(pick, columns)
    middle = centre.astype(F32).reshape(groups, 1, SUBLANES, width)
    middle = jnp.broadcast_to(middle, (groups, MOST, SUBLANES, width)).reshape(slots, width)
    return jnp.where(present > 0.0, raw - middle, 0.0).astype(BF16)


def picked(lead_ref, inv_ref):
    cid = ids_of(lead_ref)
    docs = cid.shape[1]
    groups = inv_ref.shape[0] // SUBLANES
    match = (inv_ref[...] == cid).astype(F32)
    before = lax.broadcasted_iota(jnp.int32, (docs, docs), 0) < lax.broadcasted_iota(jnp.int32, (docs, docs), 1)
    earlier = dot(match.astype(BF16), before.astype(F32).astype(BF16))
    ranked = [jnp.where(earlier == r, match, 0.0).reshape(groups, SUBLANES, docs) for r in range(MOST)]
    return jnp.stack(ranked, axis=1).reshape(groups * MOST * SUBLANES, docs).astype(BF16)


def select_kernel(block_ref, inv_ref, centre_ref, *row_refs):
    docs = block_ref.shape[0] - META
    rows = centred(picked(block_ref, inv_ref), centre_ref[...], block_ref[:docs, :])
    rows = rows.reshape((len(row_refs),) + row_refs[0].shape)
    for t, ref in enumerate(row_refs):
        ref[...] = rows[t]


def select_lead_kernel(lead_ref, inv_ref, centre_ref, pick_ref, *row_refs):
    docs = lead_ref.shape[0] - META
    pick = picked(lead_ref, inv_ref)
    pick_ref[...] = pick
    rows = centred(pick, centre_ref[:, :PREFIX], lead_ref[:docs, :])
    rows = rows.reshape((len(row_refs),) + row_refs[0].shape)
    for t, ref in enumerate(row_refs):
        ref[...] = rows[t]


def select_rest_kernel(pick_ref, rest_ref, centre_ref, *row_refs):
    rows = centred(pick_ref[...], centre_ref[:, PREFIX:], rest_ref[...])
    rows = rows.reshape((len(row_refs),) + row_refs[0].shape)
    for t, ref in enumerate(row_refs):
        ref[...] = rows[t]


def soft_weights(lead_ref, near_ref, cent_ref, own_prefix_ref):
    docs = lead_ref.shape[0] - META
    h = lax.axis_index("dim")
    prefix = jnp.where(h == 0, lead_ref[:docs, :PREFIX], near_ref[...])
    scores = dot_nt(cent_ref[...], prefix) * TEMP
    top = jnp.max(scores, axis=0, keepdims=True)
    scale = 1.0 / jnp.sum(jnp.exp(scores - top), axis=0, keepdims=True)
    own = dot_nt(own_prefix_ref[...], prefix) * TEMP
    return jnp.where(ids_of(lead_ref) >= 0.0, jnp.exp(own - top) * scale, 0.0)


def add_lead(weights, lead_ref, old_refs, new_refs):
    docs = lead_ref.shape[0] - META
    per = new_refs[0].shape[0] - SUBLANES
    sums = dot(weights.astype(BF16), lead_ref[:docs, :PREFIX])
    ones = jnp.ones((SUBLANES, docs), BF16)
    for t, new in enumerate(new_refs):
        here = slice(t * per, (t + 1) * per)
        mass = dot_nt(ones, weights[here].astype(BF16))
        if old_refs:
            old = old_refs[t]
            new[:per, :] = old[:per, :] + sums[here]
            new[per:, :] = old[per:, :]
            new[per:, :per] = old[per:, :per] + mass
        else:
            new[:per, :] = sums[here]
            new[per:, :] = jnp.zeros((SUBLANES, new.shape[1]), F32)
            new[per:, :per] = mass


def add_rest(weights, rest, old_refs, new_refs):
    per = new_refs[0].shape[0]
    sums = dot(weights, rest)
    for t, new in enumerate(new_refs):
        part = sums[t * per : (t + 1) * per]
        new[...] = old_refs[t][...] + part if old_refs else part


def sums_kernel(subs, block_ref, near_ref, cent_ref, own_prefix_ref, *refs):
    old, new = refs[: -2 * subs], refs[-2 * subs :]
    docs = block_ref.shape[0] - META
    weights = soft_weights(block_ref, near_ref, cent_ref, own_prefix_ref)
    add_lead(weights, block_ref, old[:subs], new[:subs])
    add_rest(weights.astype(BF16), block_ref[:docs, PREFIX:], old[subs:], new[subs:])


def sums_lead_kernel(subs, lead_ref, near_ref, cent_ref, own_prefix_ref, *refs):
    old, weights_ref, new = refs[:subs], refs[subs], refs[subs + 1 :]
    weights = soft_weights(lead_ref, near_ref, cent_ref, own_prefix_ref)
    weights_ref[...] = weights.astype(BF16)
    add_lead(weights, lead_ref, old, new)


def sums_rest_kernel(subs, weights_ref, rest_ref, *refs):
    add_rest(weights_ref[...], rest_ref[...], refs[:subs], refs[subs:])


def gram_kernel(table, subs, *refs):
    *member_refs, gram_ref, held = refs
    z, x = lax.axis_index("rows"), lax.axis_index("sub")
    owners, groups, packed, half = held.shape
    each = len(member_refs) // subs
    for t in range(subs):
        column = member_refs[t * each : (t + 1) * each]
        for k, line in enumerate(table):
            source = sum(jnp.where(z == i, at, 0) for i, (_, _, at) in enumerate(line))
            row = source * subs + (x - t + subs) % subs
            if k < len(table) - 1:
                held[row] = column[k][...]
            else:
                held[row, :, :, :PREFIX] = column[k][...]
                held[row, :, :, PREFIX:] = column[k + 1][...]

    size = owners * packed
    lane = lax.broadcasted_iota(jnp.int32, (1, SUBLANES, size), 2) % SUBLANES
    same = (lane == lax.broadcasted_iota(jnp.int32, (1, SUBLANES, size), 1)).astype(F32)
    tile = min(size, 2 * LANES)
    for g in range(groups):
        mine = held[:, g].reshape(size, half)
        for start in range(0, size, tile):
            part = dot_nt(mine[start : start + tile], mine)
            part = part.reshape(tile // SUBLANES, SUBLANES, size)
            gram_ref[g, start // SUBLANES : (start + tile) // SUBLANES, :] = jnp.sum(part * same, axis=1)


def scaled_tiles(width, mine_ref, other_ref, scaled_ref):
    groups, slots, size = mine_ref.shape
    kept = scaled_ref.shape[1]
    h = lax.axis_index("dim")
    start = pl.multiple_of(h * kept, kept)
    row = lax.broadcasted_iota(jnp.int32, (slots, size), 0)
    lane = lax.broadcasted_iota(jnp.int32, (slots, size), 1)
    diagonal = row == lane // SUBLANES
    kept_row = lax.broadcasted_iota(jnp.int32, (kept, size), 0) + start
    kept_lane = lax.broadcasted_iota(jnp.int32, (kept, size), 1)
    kept_diagonal = kept_row == kept_lane // SUBLANES
    for g in range(groups):
        total = mine_ref[g] + other_ref[g]
        norms = jnp.sum(jnp.where(diagonal, total, 0.0), axis=0, keepdims=True)
        scale = lax.rsqrt(norms / width + EPS)
        spread = jnp.where(kept_diagonal, jnp.broadcast_to(scale, (kept, size)), 0.0)
        folded = spread[:, :LANES]
        for at in range(LANES, size, LANES):
            folded = folded + spread[:, at : at + LANES]
        step = SUBLANES
        while step < LANES:
            folded = folded + pltpu.roll(folded, step, 1)
            step *= 2
        row_scale = jnp.concatenate([folded] * (size // LANES), axis=1)
        own = mine_ref[g, pl.ds(start, kept), :] + other_ref[g, pl.ds(start, kept), :]
        scaled_ref[g] = own / width * row_scale * scale


def finish_kernel(width, mine_ref, other_ref, *refs):
    *part_refs, prior_ref, new_ref, tile_ref, scaled_ref = refs
    subs = len(part_refs) // 2
    lead = sum(ref[...] for ref in part_refs[1:subs]) + part_refs[0][...]
    rest = sum(ref[...] for ref in part_refs[subs + 1 :]) + part_refs[subs][...]
    per = rest.shape[0]
    mass = jnp.transpose(lead[per:, :LANES])[:per, :1] + SMOOTH
    prior = SMOOTH * prior_ref[...].astype(F32)
    new_ref[:, :PREFIX] = (lead[:per] + prior[:, :PREFIX]) / mass
    new_ref[:, PREFIX:] = (rest + prior[:, PREFIX:]) / mass

    scaled_tiles(width, mine_ref, other_ref, scaled_ref)
    groups, kept, size = scaled_ref.shape
    slots = size // SUBLANES
    at = lax.broadcasted_iota(jnp.int32, (groups * size, per), 0)
    to = lax.broadcasted_iota(jnp.int32, (groups * size, per), 1)
    move = ((at // size == to // SUBLANES) & (at % SUBLANES == to % SUBLANES)).astype(F32).astype(BF16)
    row = lax.broadcasted_iota(jnp.int32, (slots, size), 0)
    lane = lax.broadcasted_iota(jnp.int32, (slots, size), 1)
    here = row == lane // SUBLANES
    batch = max(1, LANES // slots)

    def some(step, carry):
        spread = []
        for b in range(batch):
            i = step * batch + b
            lines = [jnp.broadcast_to(scaled_ref[g, pl.ds(i, 1), :], (slots, size)) for g in range(groups)]
            spread.append(jnp.concatenate([jnp.where(here, line, 0.0) for line in lines], axis=1))
        moved = dot(jnp.concatenate(spread, axis=0).astype(BF16), move).astype(BF16)
        for b in range(batch):
            tile_ref[step * batch + b] = moved[b * slots : (b + 1) * slots]
        return carry

    if kept == batch:
        some(0, 0)
    else:
        lax.fori_loop(0, kept // batch, some, 0)


def shards(embeddings, centroids, cluster_id, cluster_place):
    docs, half = embeddings.shape
    clusters, width = centroids.shape
    rows, subs = lax.axis_size("rows"), lax.axis_size("sub")
    owners = rows * subs
    per = clusters // owners
    groups = per // SUBLANES
    packed = MOST * SUBLANES
    slots = owners * MOST
    table = arrivals(rows)
    z = lax.axis_index("rows")
    shape = jax.ShapeDtypeStruct

    def across(values):
        got = [values[0]]
        for t in range(1, subs):
            got.append(lax.ppermute(values[t], "sub", [(i, (i + t) % subs) for i in range(subs)]))
        return got

    def near(value):
        return lax.ppermute(value, "dim", [(0, 1), (1, 0)])

    def needed(step, kind):
        return any((step, kind) in [entry[:2] for entry in line] for line in table)

    def swap(step, held, cut=lambda value: value):
        return {
            kind: lax.ppermute(cut(held[1 - kind]), "rows", pairs_of(rows, kind))
            for kind in (1, 0)
            if needed(step, kind)
        }

    def lead_of(block):
        return block[:, :PREFIX]

    def rest_of(block):
        return block[:docs, PREFIX:]

    def slot_block(k, history, cut=lambda value: value):
        def part(step, kind):
            block = history[step][kind]
            return block if step == rows - 1 else cut(block)

        kinds = {}
        for i, (step, kind, _) in enumerate(table[k]):
            kinds.setdefault((step, kind), []).append(i)
        (step, kind), *others = sorted(kinds, key=lambda key: (-len(kinds[key]), key))
        value = part(step, kind)
        for step, kind in others:
            here = functools.reduce(jnp.logical_or, [z == i for i in kinds[step, kind]])
            value = jnp.where(here, part(step, kind), value)
        return value

    (block,) = call(
        pack_kernel, "pack", [shape((docs + META, half), BF16)], [embeddings, cluster_id.reshape(1, docs)]
    )
    history = {0: {0: block, 1: block}}
    coming = swap(1, history[0])

    inv, centre, own_prefix, prior, cent_prefix = call(
        functools.partial(prep_kernel, subs, per),
        "prep",
        [
            shape((subs * per, 1), F32),
            shape((subs * per, half), BF16),
            shape((subs * per, PREFIX), BF16),
            shape((per, half), BF16),
            shape((clusters, PREFIX), BF16),
        ],
        [cluster_place.reshape(1, clusters), centroids],
        cost=4 * 1024 * 1024,
    )

    lead_sum, rest_sum = shape((per + SUBLANES, PREFIX), F32), shape((per, half - PREFIX), F32)
    sum_shapes = [lead_sum] * subs + [rest_sum] * subs
    own_cost, other_cost = 2 * 1024 * 1024, 128 * 1024

    def select(block, cost):
        row_shapes = [shape((groups, packed, half), BF16)] * subs
        return list(call(select_kernel, "select", row_shapes, [block, inv, centre], cost=cost))

    def add(block, prefix, sums, cost):
        operands = [block, prefix, cent_prefix, own_prefix] + sums
        aliases = {4 + i: i for i in range(len(sums))}
        return list(call(functools.partial(sums_kernel, subs), "sums", sum_shapes, operands, aliases, cost=cost))

    members = []
    prefix = near(block[:docs, :PREFIX])
    found = select(block, own_cost)
    members.append(across(found))
    sums = add(block, prefix, [], own_cost)
    for step in range(1, rows - 1):
        history[step] = tied(coming, found, sums, members[: step - 1])
        if step == rows - 2:
            coming = swap(step + 1, history[step], lead_of)
            coming_rest = swap(step + 1, history[step], rest_of)
        else:
            coming = swap(step + 1, history[step])
        block = slot_block(step, history)
        prefix = near(block[:docs, :PREFIX])
        found = select(block, other_cost)
        members.append(across(found))
        sums = add(block, prefix, sums, other_cost)

    history[rows - 1] = tied(coming, found, sums, members)
    lead = slot_block(rows - 1, history, lead_of)
    prefix = near(lead[:docs])
    half_rows = [shape((groups, packed, PREFIX), BF16)] * subs
    pick, *lead_found = call(
        select_lead_kernel,
        "select_lead",
        [shape((subs * per * MOST, docs), BF16)] + half_rows,
        [lead, inv, centre],
        cost=other_cost,
    )
    members.append(across(lead_found))
    weights, *lead_sums = call(
        functools.partial(sums_lead_kernel, subs),
        "sums_lead",
        [shape((subs * per, docs), BF16)] + [lead_sum] * subs,
        [lead, prefix, cent_prefix, own_prefix] + sums[:subs],
        {4 + i: 1 + i for i in range(subs)},
        cost=other_cost,
    )
    lead_sums = across(lead_sums)
    history[rows - 1] = tied(coming_rest, prefix)
    rest = slot_block(rows - 1, history, rest_of)
    half_rows = [shape((groups, packed, half - PREFIX), BF16)] * subs
    found = call(select_rest_kernel, "select_rest", half_rows, [pick, rest, centre], cost=other_cost)
    members.append(across(found))
    rest_sums = call(
        functools.partial(sums_rest_kernel, subs),
        "sums_rest",
        [rest_sum] * subs,
        [weights, rest] + sums[subs:],
        {2 + i: i for i in range(subs)},
    )
    rest_sums = across(rest_sums)

    (gram,) = call(
        functools.partial(gram_kernel, table, subs),
        "gram",
        [shape((groups, slots, slots * SUBLANES), F32)],
        [arrays[t] for t in range(subs) for arrays in members],
        scratch=[pltpu.VMEM((owners, groups, packed, half), BF16)],
    )
    new_centroids, tiles = call(
        functools.partial(finish_kernel, width),
        "finish",
        [shape((per, half), F32), shape((slots // 2, slots, per), BF16)],
        [gram, near(gram)] + lead_sums + rest_sums + [prior],
        scratch=[pltpu.VMEM((groups, slots // 2, slots * SUBLANES), F32)],
    )
    return (new_centroids, jnp.transpose(tiles, (2, 0, 1)))


def solution(mesh):
    in_specs = (
        P(("parts", "rows", "sub"), "dim"),
        P("parts", None),
        P(("parts", "rows", "sub"), None),
        P(),
    )
    out_specs = (P(("parts", "rows", "sub"), "dim"), P(("parts", "rows", "sub"), "dim", None))
    return jax.shard_map(shards, mesh=mesh, in_specs=in_specs, out_specs=out_specs, check_vma=False)
```

```python
import functools

import jax
import jax.numpy as jnp
from jax import lax
from jax.experimental import pallas as pl
from jax.experimental.pallas import tpu as pltpu
from jax.sharding import PartitionSpec as P

PREFIX = 256
MOST = 2

TEMP = 0.125
SMOOTH = 1.0
EPS = 1e-05

DIGIT = 32
META = 16
SUBLANES = 8
LANES = 128
F32 = jnp.float32
BF16 = jnp.bfloat16
VMEM_LIMIT = 40 * 1024 * 1024

NT = (((1,), (1,)), ((), ()))


def call(kernel, name, out_shape, operands, aliases=None, scratch=(), far=0, cost=0):
    def place(at):
        return pl.BlockSpec(memory_space=pltpu.HBM if at < far else pltpu.VMEM)

    return pl.pallas_call(
        kernel,
        out_shape=tuple(out_shape),
        in_specs=[place(at) for at in range(len(operands))],
        out_specs=tuple(pl.BlockSpec(memory_space=pltpu.VMEM) for _ in out_shape),
        input_output_aliases=aliases or {},
        scratch_shapes=list(scratch),
        compiler_params=pltpu.CompilerParams(vmem_limit_bytes=VMEM_LIMIT),
        cost_estimate=pl.CostEstimate(flops=50 * cost, bytes_accessed=cost, transcendentals=0),
        name=name,
    )(*operands)


def dot(a, b):
    return jnp.dot(a, b, preferred_element_type=F32)


def dot_nt(a, b):
    return lax.dot_general(a, b, NT, preferred_element_type=F32)


def tied(values, *others):
    leaves, tree = jax.tree.flatten(values)
    kept = lax.optimization_barrier(tuple(leaves) + tuple(jax.tree.leaves(others)))
    return jax.tree.unflatten(tree, kept[: len(leaves)])


def slots_order(rows):
    return sorted(range(rows), key=lambda bits: (bits.bit_count(), bits))


def pack_kernel(emb_ref, cid_ref, block_ref):
    docs, half = emb_ref.shape
    block_ref[:docs, :] = emb_ref[...]
    cid = cid_ref[...]
    high, low = (cid // DIGIT + 1).astype(F32), (cid % DIGIT).astype(F32)
    rows = []
    for digit in (high, low):
        rows += [digit[:, at : at + PREFIX] for at in range(0, docs, PREFIX)]
    rows.append(jnp.zeros((META - len(rows), PREFIX), F32))
    block_ref[docs:, :PREFIX] = jnp.concatenate(rows, axis=0).astype(BF16)
    block_ref[docs:, PREFIX:] = jnp.zeros((META, half - PREFIX), BF16)


def ids_of(lead_ref):
    docs = lead_ref.shape[0] - META
    meta = lead_ref[docs:, :PREFIX].astype(F32)
    parts = docs // PREFIX
    high = jnp.concatenate([meta[i : i + 1] for i in range(parts)], axis=1)
    low = jnp.concatenate([meta[parts + i : parts + i + 1] for i in range(parts)], axis=1)
    return (high - 1.0) * DIGIT + low


def prep_kernel(subs, per, place_ref, cent_ref, inv_ref, centre_ref, own_prefix_ref, prior_ref, prefix_ref):
    clusters = cent_ref.shape[0]
    half = centre_ref.shape[1]
    z, x, h = lax.axis_index("rows"), lax.axis_index("sub"), lax.axis_index("dim")
    row = lax.broadcasted_iota(jnp.int32, (subs * per, clusters), 0)
    ids = lax.broadcasted_iota(jnp.int32, (subs * per, clusters), 1)
    turn, within = row // per, row % per
    target = (z * subs + (x + turn) % subs) * per + within
    chosen = (place_ref[...] == target).astype(F32)
    inv_ref[...] = jnp.sum(chosen * ids.astype(F32), axis=1, keepdims=True)
    columns = cent_ref[:, pl.ds(pl.multiple_of(h * half, LANES), half)]
    centre_ref[...] = dot(chosen.astype(BF16), columns).astype(BF16)
    natural = (ids == target).astype(BF16)
    prior_ref[...] = dot(natural[:per], columns).astype(BF16)
    prefix_ref[...] = cent_ref[:, :PREFIX]
    own_prefix_ref[...] = dot(natural, prefix_ref[...]).astype(BF16)


def centred(pick, centre, columns):
    slots = pick.shape[0]
    groups = slots // (MOST * SUBLANES)
    width = columns.shape[1]
    present = jnp.sum(pick.astype(F32), axis=1, keepdims=True)
    raw = dot(pick, columns)
    middle = centre.astype(F32).reshape(groups, 1, SUBLANES, width)
    middle = jnp.broadcast_to(middle, (groups, MOST, SUBLANES, width)).reshape(slots, width)
    return jnp.where(present > 0.0, raw - middle, 0.0).astype(BF16)


def picked(lead_ref, inv_ref):
    cid = ids_of(lead_ref)
    docs = cid.shape[1]
    groups = inv_ref.shape[0] // SUBLANES
    match = (inv_ref[...] == cid).astype(F32)
    before = lax.broadcasted_iota(jnp.int32, (docs, docs), 0) < lax.broadcasted_iota(jnp.int32, (docs, docs), 1)
    earlier = dot(match.astype(BF16), before.astype(F32).astype(BF16))
    ranked = [jnp.where(earlier == r, match, 0.0).reshape(groups, SUBLANES, docs) for r in range(MOST)]
    return jnp.stack(ranked, axis=1).reshape(groups * MOST * SUBLANES, docs).astype(BF16)


def select_kernel(block_ref, inv_ref, centre_ref, *row_refs):
    docs = block_ref.shape[0] - META
    rows = centred(picked(block_ref, inv_ref), centre_ref[...], block_ref[:docs, :])
    rows = rows.reshape((len(row_refs),) + row_refs[0].shape)
    for t, ref in enumerate(row_refs):
        ref[...] = rows[t]


def select_lead_kernel(lead_ref, inv_ref, centre_ref, pick_ref, *row_refs):
    docs = lead_ref.shape[0] - META
    pick = picked(lead_ref, inv_ref)
    pick_ref[...] = pick
    rows = centred(pick, centre_ref[:, :PREFIX], lead_ref[:docs, :])
    rows = rows.reshape((len(row_refs),) + row_refs[0].shape)
    for t, ref in enumerate(row_refs):
        ref[...] = rows[t]


def select_rest_kernel(pick_ref, rest_ref, centre_ref, *row_refs):
    rows = centred(pick_ref[...], centre_ref[:, PREFIX:], rest_ref[...])
    rows = rows.reshape((len(row_refs),) + row_refs[0].shape)
    for t, ref in enumerate(row_refs):
        ref[...] = rows[t]


def soft_weights(lead_ref, near_ref, cent_ref, own_prefix_ref):
    docs = lead_ref.shape[0] - META
    h = lax.axis_index("dim")
    prefix = jnp.where(h == 0, lead_ref[:docs, :PREFIX], near_ref[...])
    scores = dot_nt(cent_ref[...], prefix) * TEMP
    top = jnp.max(scores, axis=0, keepdims=True)
    scale = 1.0 / jnp.sum(jnp.exp(scores - top), axis=0, keepdims=True)
    own = dot_nt(own_prefix_ref[...], prefix) * TEMP
    return jnp.where(ids_of(lead_ref) >= 0.0, jnp.exp(own - top) * scale, 0.0)


def add_lead(weights, lead_ref, old_refs, new_refs):
    docs = lead_ref.shape[0] - META
    per = new_refs[0].shape[0] - SUBLANES
    sums = dot(weights.astype(BF16), lead_ref[:docs, :PREFIX])
    ones = jnp.ones((SUBLANES, docs), BF16)
    for t, new in enumerate(new_refs):
        here = slice(t * per, (t + 1) * per)
        mass = dot_nt(ones, weights[here].astype(BF16))
        if old_refs:
            old = old_refs[t]
            new[:per, :] = old[:per, :] + sums[here]
            new[per:, :] = old[per:, :]
            new[per:, :per] = old[per:, :per] + mass
        else:
            new[:per, :] = sums[here]
            new[per:, :] = jnp.zeros((SUBLANES, new.shape[1]), F32)
            new[per:, :per] = mass


def add_rest(weights, rest, old_refs, new_refs):
    per = new_refs[0].shape[0]
    sums = dot(weights, rest)
    for t, new in enumerate(new_refs):
        part = sums[t * per : (t + 1) * per]
        new[...] = old_refs[t][...] + part if old_refs else part


def sums_kernel(subs, block_ref, near_ref, cent_ref, own_prefix_ref, *refs):
    old, new = refs[: -2 * subs], refs[-2 * subs :]
    docs = block_ref.shape[0] - META
    weights = soft_weights(block_ref, near_ref, cent_ref, own_prefix_ref)
    add_lead(weights, block_ref, old[:subs], new[:subs])
    add_rest(weights.astype(BF16), block_ref[:docs, PREFIX:], old[subs:], new[subs:])


def sums_lead_kernel(subs, lead_ref, near_ref, cent_ref, own_prefix_ref, *refs):
    old, weights_ref, new = refs[:subs], refs[subs], refs[subs + 1 :]
    weights = soft_weights(lead_ref, near_ref, cent_ref, own_prefix_ref)
    weights_ref[...] = weights.astype(BF16)
    add_lead(weights, lead_ref, old, new)


def sums_rest_kernel(subs, weights_ref, rest_ref, *refs):
    add_rest(weights_ref[...], rest_ref[...], refs[:subs], refs[subs:])


def gram_kernel(order, subs, *refs):
    *member_refs, gram_ref, held = refs
    z, x = lax.axis_index("rows"), lax.axis_index("sub")
    owners, groups, packed, half = held.shape
    each = len(member_refs) // subs
    for t in range(subs):
        column = member_refs[t * each : (t + 1) * each]
        for k, bits in enumerate(order):
            row = (z ^ bits) * subs + (x - t + subs) % subs
            if k < len(order) - 1:
                held[row] = column[k][...]
            else:
                held[row, :, :, :PREFIX] = column[k][...]
                held[row, :, :, PREFIX:] = column[k + 1][...]

    size = owners * packed
    lane = lax.broadcasted_iota(jnp.int32, (1, SUBLANES, size), 2) % SUBLANES
    same = (lane == lax.broadcasted_iota(jnp.int32, (1, SUBLANES, size), 1)).astype(F32)
    tile = min(size, 2 * LANES)
    for g in range(groups):
        mine = held[:, g].reshape(size, half)
        for start in range(0, size, tile):
            part = dot_nt(mine[start : start + tile], mine)
            part = part.reshape(tile // SUBLANES, SUBLANES, size)
            gram_ref[g, start // SUBLANES : (start + tile) // SUBLANES, :] = jnp.sum(part * same, axis=1)


def scaled_tiles(width, mine_ref, other_ref, scaled_ref):
    groups, slots, size = mine_ref.shape
    kept = scaled_ref.shape[1]
    h = lax.axis_index("dim")
    start = pl.multiple_of(h * kept, kept)
    row = lax.broadcasted_iota(jnp.int32, (slots, size), 0)
    lane = lax.broadcasted_iota(jnp.int32, (slots, size), 1)
    diagonal = row == lane // SUBLANES
    kept_row = lax.broadcasted_iota(jnp.int32, (kept, size), 0) + start
    kept_lane = lax.broadcasted_iota(jnp.int32, (kept, size), 1)
    kept_diagonal = kept_row == kept_lane // SUBLANES
    for g in range(groups):
        total = mine_ref[g] + other_ref[g]
        norms = jnp.sum(jnp.where(diagonal, total, 0.0), axis=0, keepdims=True)
        scale = lax.rsqrt(norms / width + EPS)
        spread = jnp.where(kept_diagonal, jnp.broadcast_to(scale, (kept, size)), 0.0)
        folded = spread[:, :LANES]
        for at in range(LANES, size, LANES):
            folded = folded + spread[:, at : at + LANES]
        step = SUBLANES
        while step < LANES:
            folded = folded + pltpu.roll(folded, step, 1)
            step *= 2
        row_scale = jnp.concatenate([folded] * (size // LANES), axis=1)
        own = mine_ref[g, pl.ds(start, kept), :] + other_ref[g, pl.ds(start, kept), :]
        scaled_ref[g] = own / width * row_scale * scale


def finish_kernel(width, mine_ref, other_ref, *refs):
    *part_refs, prior_ref, new_ref, tile_ref, scaled_ref = refs
    subs = len(part_refs) // 2
    lead = sum(ref[...] for ref in part_refs[1:subs]) + part_refs[0][...]
    rest = sum(ref[...] for ref in part_refs[subs + 1 :]) + part_refs[subs][...]
    per = rest.shape[0]
    mass = jnp.transpose(lead[per:, :LANES])[:per, :1] + SMOOTH
    prior = SMOOTH * prior_ref[...].astype(F32)
    new_ref[:, :PREFIX] = (lead[:per] + prior[:, :PREFIX]) / mass
    new_ref[:, PREFIX:] = (rest + prior[:, PREFIX:]) / mass

    scaled_tiles(width, mine_ref, other_ref, scaled_ref)
    groups, kept, size = scaled_ref.shape
    slots = size // SUBLANES
    at = lax.broadcasted_iota(jnp.int32, (groups * size, per), 0)
    to = lax.broadcasted_iota(jnp.int32, (groups * size, per), 1)
    move = ((at // size == to // SUBLANES) & (at % SUBLANES == to % SUBLANES)).astype(F32).astype(BF16)
    row = lax.broadcasted_iota(jnp.int32, (slots, size), 0)
    lane = lax.broadcasted_iota(jnp.int32, (slots, size), 1)
    here = row == lane // SUBLANES
    batch = max(1, LANES // slots)

    def some(step, carry):
        spread = []
        for b in range(batch):
            i = step * batch + b
            lines = [jnp.broadcast_to(scaled_ref[g, pl.ds(i, 1), :], (slots, size)) for g in range(groups)]
            spread.append(jnp.concatenate([jnp.where(here, line, 0.0) for line in lines], axis=1))
        moved = dot(jnp.concatenate(spread, axis=0).astype(BF16), move).astype(BF16)
        for b in range(batch):
            tile_ref[step * batch + b] = moved[b * slots : (b + 1) * slots]
        return carry

    if kept == batch:
        some(0, 0)
    else:
        lax.fori_loop(0, kept // batch, some, 0)


def shards(embeddings, centroids, cluster_id, cluster_place):
    docs, half = embeddings.shape
    clusters, width = centroids.shape
    rows, subs = lax.axis_size("rows"), lax.axis_size("sub")
    owners = rows * subs
    per = clusters // owners
    groups = per // SUBLANES
    packed = MOST * SUBLANES
    slots = owners * MOST
    order = slots_order(rows)
    shape = jax.ShapeDtypeStruct

    def across(values):
        got = [values[0]]
        for t in range(1, subs):
            got.append(lax.ppermute(values[t], "sub", [(i, (i + t) % subs) for i in range(subs)]))
        return got

    def near(value):
        return lax.ppermute(value, "dim", [(0, 1), (1, 0)])

    def swap(value, bit):
        return lax.ppermute(value, "rows", [(i, i ^ bit) for i in range(rows)])

    (block,) = call(
        pack_kernel, "pack", [shape((docs + META, half), BF16)], [embeddings, cluster_id.reshape(1, docs)]
    )
    blocks = {0: block}

    def send(bits):
        bit = (bits & -bits or rows) // 2
        while bit:
            if bits | bit != rows - 1:
                blocks[bits | bit] = swap(blocks[bits], bit)
            bit //= 2

    send(0)

    inv, centre, own_prefix, prior, cent_prefix = call(
        functools.partial(prep_kernel, subs, per),
        "prep",
        [
            shape((subs * per, 1), F32),
            shape((subs * per, half), BF16),
            shape((subs * per, PREFIX), BF16),
            shape((per, half), BF16),
            shape((clusters, PREFIX), BF16),
        ],
        [cluster_place.reshape(1, clusters), centroids],
        cost=4 * 1024 * 1024,
    )

    lead_sum, rest_sum = shape((per + SUBLANES, PREFIX), F32), shape((per, half - PREFIX), F32)
    sum_shapes = [lead_sum] * subs + [rest_sum] * subs
    own_cost, other_cost = 2 * 1024 * 1024, 128 * 1024

    def select(block, cost):
        row_shapes = [shape((groups, packed, half), BF16)] * subs
        return list(call(select_kernel, "select", row_shapes, [block, inv, centre], cost=cost))

    def add(block, prefix, sums, cost):
        operands = [block, prefix, cent_prefix, own_prefix] + sums
        aliases = {4 + i: i for i in range(len(sums))}
        return list(call(functools.partial(sums_kernel, subs), "sums", sum_shapes, operands, aliases, cost=cost))

    members = []
    prefix = near(block[:docs, :PREFIX])
    found = select(block, own_cost)
    members.append(across(found))
    sums = add(block, prefix, [], own_cost)
    for k, bits in enumerate(order[1:-1], 1):
        block = blocks[bits] = tied(blocks[bits], found, sums, members[: k - 1])
        send(bits)
        if bits == rows - 2:
            coming, coming_rest = swap(block[:, :PREFIX], 1), swap(block[:docs, PREFIX:], 1)
        prefix = near(block[:docs, :PREFIX])
        found = select(block, other_cost)
        members.append(across(found))
        sums = add(block, prefix, sums, other_cost)

    lead = tied(coming, found, sums, members)
    prefix = near(lead[:docs])
    half_rows = [shape((groups, packed, PREFIX), BF16)] * subs
    pick, *lead_found = call(
        select_lead_kernel,
        "select_lead",
        [shape((subs * per * MOST, docs), BF16)] + half_rows,
        [lead, inv, centre],
        cost=other_cost,
    )
    members.append(across(lead_found))
    weights, *lead_sums = call(
        functools.partial(sums_lead_kernel, subs),
        "sums_lead",
        [shape((subs * per, docs), BF16)] + [lead_sum] * subs,
        [lead, prefix, cent_prefix, own_prefix] + sums[:subs],
        {4 + i: 1 + i for i in range(subs)},
        cost=other_cost,
    )
    lead_sums = across(lead_sums)
    rest = tied(coming_rest, prefix)
    half_rows = [shape((groups, packed, half - PREFIX), BF16)] * subs
    found = call(select_rest_kernel, "select_rest", half_rows, [pick, rest, centre], cost=other_cost)
    members.append(across(found))
    rest_sums = call(
        functools.partial(sums_rest_kernel, subs),
        "sums_rest",
        [rest_sum] * subs,
        [weights, rest] + sums[subs:],
        {2 + i: i for i in range(subs)},
    )
    rest_sums = across(rest_sums)

    (gram,) = call(
        functools.partial(gram_kernel, order, subs),
        "gram",
        [shape((groups, slots, slots * SUBLANES), F32)],
        [arrays[t] for t in range(subs) for arrays in members],
        scratch=[pltpu.VMEM((owners, groups, packed, half), BF16)],
    )
    new_centroids, tiles = call(
        functools.partial(finish_kernel, width),
        "finish",
        [shape((per, half), F32), shape((slots // 2, slots, per), BF16)],
        [gram, near(gram)] + lead_sums + rest_sums + [prior],
        scratch=[pltpu.VMEM((groups, slots // 2, slots * SUBLANES), F32)],
    )
    return (new_centroids, jnp.transpose(tiles, (2, 0, 1)))


def solution(mesh):
    in_specs = (
        P(("parts", "rows", "sub"), "dim"),
        P("parts", None),
        P(("parts", "rows", "sub"), None),
        P(),
    )
    out_specs = (P(("parts", "rows", "sub"), "dim"), P(("parts", "rows", "sub"), "dim", None))
    return jax.shard_map(shards, mesh=mesh, in_specs=in_specs, out_specs=out_specs, check_vma=False)
```

```python
import functools

import jax
import jax.numpy as jnp
from jax import lax
from jax.experimental import pallas as pl
from jax.experimental.pallas import tpu as pltpu
from jax.sharding import PartitionSpec as P

PREFIX = 256
MOST = 2

TEMP = 0.125
SMOOTH = 1.0
EPS = 1e-05

DIGIT = 32
META = 16
SUBLANES = 8
LANES = 128
F32 = jnp.float32
BF16 = jnp.bfloat16
VMEM_LIMIT = 40 * 1024 * 1024

NT = (((1,), (1,)), ((), ()))


def call(kernel, name, out_shape, operands, aliases=None, scratch=(), far=0, cost=0):
    def place(at):
        return pl.BlockSpec(memory_space=pltpu.HBM if at < far else pltpu.VMEM)

    return pl.pallas_call(
        kernel,
        out_shape=tuple(out_shape),
        in_specs=[place(at) for at in range(len(operands))],
        out_specs=tuple(pl.BlockSpec(memory_space=pltpu.VMEM) for _ in out_shape),
        input_output_aliases=aliases or {},
        scratch_shapes=list(scratch),
        compiler_params=pltpu.CompilerParams(vmem_limit_bytes=VMEM_LIMIT),
        cost_estimate=pl.CostEstimate(flops=50 * cost, bytes_accessed=cost, transcendentals=0),
        name=name,
    )(*operands)


def dot(a, b):
    return jnp.dot(a, b, preferred_element_type=F32)


def dot_nt(a, b):
    return lax.dot_general(a, b, NT, preferred_element_type=F32)


def tied(values, *others):
    leaves, tree = jax.tree.flatten(values)
    kept = lax.optimization_barrier(tuple(leaves) + tuple(jax.tree.leaves(others)))
    return jax.tree.unflatten(tree, kept[: len(leaves)])


def slots_order(rows):
    return sorted(range(rows), key=lambda bits: (bits.bit_count(), bits))


def pack_kernel(emb_ref, cid_ref, block_ref):
    docs, half = emb_ref.shape
    block_ref[:docs, :] = emb_ref[...]
    cid = cid_ref[...]
    high, low = (cid // DIGIT + 1).astype(F32), (cid % DIGIT).astype(F32)
    rows = []
    for digit in (high, low):
        rows += [digit[:, at : at + PREFIX] for at in range(0, docs, PREFIX)]
    rows.append(jnp.zeros((META - len(rows), PREFIX), F32))
    block_ref[docs:, :PREFIX] = jnp.concatenate(rows, axis=0).astype(BF16)
    block_ref[docs:, PREFIX:] = jnp.zeros((META, half - PREFIX), BF16)


def ids_of(lead_ref):
    docs = lead_ref.shape[0] - META
    meta = lead_ref[docs:, :PREFIX].astype(F32)
    parts = docs // PREFIX
    high = jnp.concatenate([meta[i : i + 1] for i in range(parts)], axis=1)
    low = jnp.concatenate([meta[parts + i : parts + i + 1] for i in range(parts)], axis=1)
    return (high - 1.0) * DIGIT + low


def prep_kernel(subs, per, place_ref, cent_ref, inv_ref, centre_ref, own_prefix_ref, prior_ref, prefix_ref):
    clusters = cent_ref.shape[0]
    half = centre_ref.shape[1]
    z, x, h = lax.axis_index("rows"), lax.axis_index("sub"), lax.axis_index("dim")
    row = lax.broadcasted_iota(jnp.int32, (subs * per, clusters), 0)
    ids = lax.broadcasted_iota(jnp.int32, (subs * per, clusters), 1)
    turn, within = row // per, row % per
    target = (z * subs + (x + turn) % subs) * per + within
    chosen = (place_ref[...] == target).astype(F32)
    inv_ref[...] = jnp.sum(chosen * ids.astype(F32), axis=1, keepdims=True)
    columns = cent_ref[:, pl.ds(pl.multiple_of(h * half, LANES), half)]
    centre_ref[...] = dot(chosen.astype(BF16), columns).astype(BF16)
    natural = (ids == target).astype(BF16)
    prior_ref[...] = dot(natural[:per], columns).astype(BF16)
    prefix_ref[...] = cent_ref[:, :PREFIX]
    own_prefix_ref[...] = dot(natural, prefix_ref[...]).astype(BF16)


def centred(pick, centre, columns):
    slots = pick.shape[0]
    groups = slots // (MOST * SUBLANES)
    width = columns.shape[1]
    present = jnp.sum(pick.astype(F32), axis=1, keepdims=True)
    raw = dot(pick, columns)
    middle = centre.astype(F32).reshape(groups, 1, SUBLANES, width)
    middle = jnp.broadcast_to(middle, (groups, MOST, SUBLANES, width)).reshape(slots, width)
    return jnp.where(present > 0.0, raw - middle, 0.0).astype(BF16)


def picked(lead_ref, inv_ref):
    cid = ids_of(lead_ref)
    docs = cid.shape[1]
    groups = inv_ref.shape[0] // SUBLANES
    match = (inv_ref[...] == cid).astype(F32)
    before = lax.broadcasted_iota(jnp.int32, (docs, docs), 0) < lax.broadcasted_iota(jnp.int32, (docs, docs), 1)
    earlier = dot(match.astype(BF16), before.astype(F32).astype(BF16))
    ranked = [jnp.where(earlier == r, match, 0.0).reshape(groups, SUBLANES, docs) for r in range(MOST)]
    return jnp.stack(ranked, axis=1).reshape(groups * MOST * SUBLANES, docs).astype(BF16)


def select_kernel(block_ref, inv_ref, centre_ref, *row_refs):
    docs = block_ref.shape[0] - META
    rows = centred(picked(block_ref, inv_ref), centre_ref[...], block_ref[:docs, :])
    rows = rows.reshape((len(row_refs),) + row_refs[0].shape)
    for t, ref in enumerate(row_refs):
        ref[...] = rows[t]


def select_lead_kernel(lead_ref, inv_ref, centre_ref, pick_ref, *row_refs):
    docs = lead_ref.shape[0] - META
    pick = picked(lead_ref, inv_ref)
    pick_ref[...] = pick
    rows = centred(pick, centre_ref[:, :PREFIX], lead_ref[:docs, :])
    rows = rows.reshape((len(row_refs),) + row_refs[0].shape)
    for t, ref in enumerate(row_refs):
        ref[...] = rows[t]


def select_rest_kernel(pick_ref, rest_ref, centre_ref, *row_refs):
    rows = centred(pick_ref[...], centre_ref[:, PREFIX:], rest_ref[...])
    rows = rows.reshape((len(row_refs),) + row_refs[0].shape)
    for t, ref in enumerate(row_refs):
        ref[...] = rows[t]


def soft_weights(lead_ref, near_ref, cent_ref, own_prefix_ref):
    docs = lead_ref.shape[0] - META
    h = lax.axis_index("dim")
    prefix = jnp.where(h == 0, lead_ref[:docs, :PREFIX], near_ref[:docs, :PREFIX])
    scores = dot_nt(cent_ref[...], prefix) * TEMP
    top = jnp.max(scores, axis=0, keepdims=True)
    scale = 1.0 / jnp.sum(jnp.exp(scores - top), axis=0, keepdims=True)
    own = dot_nt(own_prefix_ref[...], prefix) * TEMP
    return jnp.where(ids_of(lead_ref) >= 0.0, jnp.exp(own - top) * scale, 0.0)


def add_lead(weights, lead_ref, old_refs, new_refs):
    docs = lead_ref.shape[0] - META
    per = new_refs[0].shape[0] - SUBLANES
    sums = dot(weights.astype(BF16), lead_ref[:docs, :PREFIX])
    ones = jnp.ones((SUBLANES, docs), BF16)
    for t, new in enumerate(new_refs):
        here = slice(t * per, (t + 1) * per)
        mass = dot_nt(ones, weights[here].astype(BF16))
        if old_refs:
            old = old_refs[t]
            new[:per, :] = old[:per, :] + sums[here]
            new[per:, :] = old[per:, :]
            new[per:, :per] = old[per:, :per] + mass
        else:
            new[:per, :] = sums[here]
            new[per:, :] = jnp.zeros((SUBLANES, new.shape[1]), F32)
            new[per:, :per] = mass


def add_rest(weights, rest, old_refs, new_refs):
    per = new_refs[0].shape[0]
    sums = dot(weights, rest)
    for t, new in enumerate(new_refs):
        part = sums[t * per : (t + 1) * per]
        new[...] = old_refs[t][...] + part if old_refs else part


def sums_kernel(subs, block_ref, near_ref, cent_ref, own_prefix_ref, *refs):
    old, new = refs[: -2 * subs], refs[-2 * subs :]
    docs = block_ref.shape[0] - META
    weights = soft_weights(block_ref, near_ref, cent_ref, own_prefix_ref)
    add_lead(weights, block_ref, old[:subs], new[:subs])
    add_rest(weights.astype(BF16), block_ref[:docs, PREFIX:], old[subs:], new[subs:])


def sums_lead_kernel(subs, lead_ref, near_ref, cent_ref, own_prefix_ref, *refs):
    old, weights_ref, new = refs[:subs], refs[subs], refs[subs + 1 :]
    weights = soft_weights(lead_ref, near_ref, cent_ref, own_prefix_ref)
    weights_ref[...] = weights.astype(BF16)
    add_lead(weights, lead_ref, old, new)


def sums_rest_kernel(subs, weights_ref, rest_ref, *refs):
    add_rest(weights_ref[...], rest_ref[...], refs[:subs], refs[subs:])


def gram_kernel(order, subs, *refs):
    *member_refs, gram_ref, held = refs
    z, x = lax.axis_index("rows"), lax.axis_index("sub")
    owners, groups, packed, half = held.shape
    each = len(member_refs) // subs
    for t in range(subs):
        column = member_refs[t * each : (t + 1) * each]
        for k, bits in enumerate(order):
            row = (z ^ bits) * subs + (x - t + subs) % subs
            if k < len(order) - 1:
                held[row] = column[k][...]
            else:
                held[row, :, :, :PREFIX] = column[k][...]
                held[row, :, :, PREFIX:] = column[k + 1][...]

    size = owners * packed
    lane = lax.broadcasted_iota(jnp.int32, (1, SUBLANES, size), 2) % SUBLANES
    same = (lane == lax.broadcasted_iota(jnp.int32, (1, SUBLANES, size), 1)).astype(F32)
    tile = min(size, 2 * LANES)
    for g in range(groups):
        mine = held[:, g].reshape(size, half)
        for start in range(0, size, tile):
            part = dot_nt(mine[start : start + tile], mine)
            part = part.reshape(tile // SUBLANES, SUBLANES, size)
            gram_ref[g, start // SUBLANES : (start + tile) // SUBLANES, :] = jnp.sum(part * same, axis=1)


def scaled_tiles(width, mine_ref, other_ref, scaled_ref):
    groups, slots, size = mine_ref.shape
    kept = scaled_ref.shape[1]
    h = lax.axis_index("dim")
    start = pl.multiple_of(h * kept, kept)
    row = lax.broadcasted_iota(jnp.int32, (slots, size), 0)
    lane = lax.broadcasted_iota(jnp.int32, (slots, size), 1)
    diagonal = row == lane // SUBLANES
    kept_row = lax.broadcasted_iota(jnp.int32, (kept, size), 0) + start
    kept_lane = lax.broadcasted_iota(jnp.int32, (kept, size), 1)
    kept_diagonal = kept_row == kept_lane // SUBLANES
    for g in range(groups):
        total = mine_ref[g] + other_ref[g]
        norms = jnp.sum(jnp.where(diagonal, total, 0.0), axis=0, keepdims=True)
        scale = lax.rsqrt(norms / width + EPS)
        spread = jnp.where(kept_diagonal, jnp.broadcast_to(scale, (kept, size)), 0.0)
        folded = spread[:, :LANES]
        for at in range(LANES, size, LANES):
            folded = folded + spread[:, at : at + LANES]
        step = SUBLANES
        while step < LANES:
            folded = folded + pltpu.roll(folded, step, 1)
            step *= 2
        row_scale = jnp.concatenate([folded] * (size // LANES), axis=1)
        own = mine_ref[g, pl.ds(start, kept), :] + other_ref[g, pl.ds(start, kept), :]
        scaled_ref[g] = own / width * row_scale * scale


def finish_kernel(width, mine_ref, other_ref, *refs):
    *part_refs, prior_ref, new_ref, tile_ref, scaled_ref = refs
    subs = len(part_refs) // 2
    lead = sum(ref[...] for ref in part_refs[1:subs]) + part_refs[0][...]
    rest = sum(ref[...] for ref in part_refs[subs + 1 :]) + part_refs[subs][...]
    per = rest.shape[0]
    mass = jnp.transpose(lead[per:, :LANES])[:per, :1] + SMOOTH
    prior = SMOOTH * prior_ref[...].astype(F32)
    new_ref[:, :PREFIX] = (lead[:per] + prior[:, :PREFIX]) / mass
    new_ref[:, PREFIX:] = (rest + prior[:, PREFIX:]) / mass

    scaled_tiles(width, mine_ref, other_ref, scaled_ref)
    groups, kept, size = scaled_ref.shape
    slots = size // SUBLANES
    at = lax.broadcasted_iota(jnp.int32, (groups * size, per), 0)
    to = lax.broadcasted_iota(jnp.int32, (groups * size, per), 1)
    move = ((at // size == to // SUBLANES) & (at % SUBLANES == to % SUBLANES)).astype(F32).astype(BF16)
    row = lax.broadcasted_iota(jnp.int32, (slots, size), 0)
    lane = lax.broadcasted_iota(jnp.int32, (slots, size), 1)
    here = row == lane // SUBLANES
    batch = max(1, LANES // slots)

    def some(step, carry):
        spread = []
        for b in range(batch):
            i = step * batch + b
            lines = [jnp.broadcast_to(scaled_ref[g, pl.ds(i, 1), :], (slots, size)) for g in range(groups)]
            spread.append(jnp.concatenate([jnp.where(here, line, 0.0) for line in lines], axis=1))
        moved = dot(jnp.concatenate(spread, axis=0).astype(BF16), move).astype(BF16)
        for b in range(batch):
            tile_ref[step * batch + b] = moved[b * slots : (b + 1) * slots]
        return carry

    if kept == batch:
        some(0, 0)
    else:
        lax.fori_loop(0, kept // batch, some, 0)


def shards(embeddings, centroids, cluster_id, cluster_place):
    docs, half = embeddings.shape
    clusters, width = centroids.shape
    rows, subs = lax.axis_size("rows"), lax.axis_size("sub")
    owners = rows * subs
    per = clusters // owners
    groups = per // SUBLANES
    packed = MOST * SUBLANES
    slots = owners * MOST
    order = slots_order(rows)
    shape = jax.ShapeDtypeStruct

    def across(values):
        got = [values[0]]
        for t in range(1, subs):
            got.append(lax.ppermute(values[t], "sub", [(i, (i + t) % subs) for i in range(subs)]))
        return got

    def near(value):
        return lax.ppermute(value, "dim", [(0, 1), (1, 0)])

    def swap(value, bit):
        return lax.ppermute(value, "rows", [(i, i ^ bit) for i in range(rows)])

    (block,) = call(
        pack_kernel, "pack", [shape((docs + META, half), BF16)], [embeddings, cluster_id.reshape(1, docs)]
    )
    blocks = {0: block}

    def send(bits):
        bit = (bits & -bits or rows) // 2
        while bit:
            if bits | bit != rows - 1:
                blocks[bits | bit] = swap(blocks[bits], bit)
            bit //= 2

    send(0)

    inv, centre, own_prefix, prior, cent_prefix = call(
        functools.partial(prep_kernel, subs, per),
        "prep",
        [
            shape((subs * per, 1), F32),
            shape((subs * per, half), BF16),
            shape((subs * per, PREFIX), BF16),
            shape((per, half), BF16),
            shape((clusters, PREFIX), BF16),
        ],
        [cluster_place.reshape(1, clusters), centroids],
        cost=4 * 1024 * 1024,
    )

    lead_sum, rest_sum = shape((per + SUBLANES, PREFIX), F32), shape((per, half - PREFIX), F32)
    sum_shapes = [lead_sum] * subs + [rest_sum] * subs
    own_cost, other_cost = 2 * 1024 * 1024, 128 * 1024

    def select(block, cost):
        row_shapes = [shape((groups, packed, half), BF16)] * subs
        return list(call(select_kernel, "select", row_shapes, [block, inv, centre], cost=cost))

    def add(block, prefix, sums, cost):
        operands = [block, prefix, cent_prefix, own_prefix] + sums
        aliases = {4 + i: i for i in range(len(sums))}
        return list(call(functools.partial(sums_kernel, subs), "sums", sum_shapes, operands, aliases, cost=cost))

    members = []
    prefix = near(block)
    found = select(block, own_cost)
    members.append(across(found))
    sums = add(block, prefix, [], own_cost)
    for depth in range(1, (rows - 1).bit_count()):
        group = [bits for bits in order if bits.bit_count() == depth]
        arrived = tied([blocks[bits] for bits in group], found, sums, members)
        blocks.update(zip(group, arrived))
        for bits in group:
            send(bits)
            if bits == rows - 2:
                coming, coming_rest = swap(blocks[bits][:, :PREFIX], 1), swap(blocks[bits][:docs, PREFIX:], 1)
        for bits in group:
            prefix = near(blocks[bits])
            found = select(blocks[bits], other_cost)
            members.append(across(found))
            sums = add(blocks[bits], prefix, sums, other_cost)

    lead = tied(coming, found, sums, members[:-1])
    prefix = near(lead)
    half_rows = [shape((groups, packed, PREFIX), BF16)] * subs
    pick, *lead_found = call(
        select_lead_kernel,
        "select_lead",
        [shape((subs * per * MOST, docs), BF16)] + half_rows,
        [lead, inv, centre],
        cost=other_cost,
    )
    members.append(across(lead_found))
    weights, *lead_sums = call(
        functools.partial(sums_lead_kernel, subs),
        "sums_lead",
        [shape((subs * per, docs), BF16)] + [lead_sum] * subs,
        [lead, prefix, cent_prefix, own_prefix] + sums[:subs],
        {4 + i: 1 + i for i in range(subs)},
        cost=other_cost,
    )
    lead_sums = across(lead_sums)
    rest = tied(coming_rest, prefix, members[: rows - 1])
    half_rows = [shape((groups, packed, half - PREFIX), BF16)] * subs
    found = call(select_rest_kernel, "select_rest", half_rows, [pick, rest, centre], cost=other_cost)
    members.append(across(found))
    rest_sums = call(
        functools.partial(sums_rest_kernel, subs),
        "sums_rest",
        [rest_sum] * subs,
        [weights, rest] + sums[subs:],
        {2 + i: i for i in range(subs)},
    )
    rest_sums = across(rest_sums)

    (gram,) = call(
        functools.partial(gram_kernel, order, subs),
        "gram",
        [shape((groups, slots, slots * SUBLANES), F32)],
        [arrays[t] for t in range(subs) for arrays in members],
        scratch=[pltpu.VMEM((owners, groups, packed, half), BF16)],
    )
    new_centroids, tiles = call(
        functools.partial(finish_kernel, width),
        "finish",
        [shape((per, half), F32), shape((slots // 2, slots, per), BF16)],
        [gram, near(gram)] + lead_sums + rest_sums + [prior],
        scratch=[pltpu.VMEM((groups, slots // 2, slots * SUBLANES), F32)],
    )
    return (new_centroids, jnp.transpose(tiles, (2, 0, 1)))


def solution(mesh):
    in_specs = (
        P(("parts", "rows", "sub"), "dim"),
        P("parts", None),
        P(("parts", "rows", "sub"), None),
        P(),
    )
    out_specs = (P(("parts", "rows", "sub"), "dim"), P(("parts", "rows", "sub"), "dim", None))
    return jax.shard_map(shards, mesh=mesh, in_specs=in_specs, out_specs=out_specs, check_vma=False)
```

```python
import functools

import jax
import jax.numpy as jnp
from jax import lax
from jax.experimental import pallas as pl
from jax.experimental.pallas import tpu as pltpu
from jax.sharding import PartitionSpec as P

PREFIX = 256
MOST = 2

TEMP = 0.125
SMOOTH = 1.0
EPS = 1e-05

DIGIT = 32
META = 16
SUBLANES = 8
LANES = 128
F32 = jnp.float32
BF16 = jnp.bfloat16
VMEM_LIMIT = 40 * 1024 * 1024

NT = (((1,), (1,)), ((), ()))


def call(kernel, name, out_shape, operands, aliases=None, scratch=(), far=0, cost=0):
    def place(at):
        return pl.BlockSpec(memory_space=pltpu.HBM if at < far else pltpu.VMEM)

    return pl.pallas_call(
        kernel,
        out_shape=tuple(out_shape),
        in_specs=[place(at) for at in range(len(operands))],
        out_specs=tuple(pl.BlockSpec(memory_space=pltpu.VMEM) for _ in out_shape),
        input_output_aliases=aliases or {},
        scratch_shapes=list(scratch),
        compiler_params=pltpu.CompilerParams(vmem_limit_bytes=VMEM_LIMIT),
        cost_estimate=pl.CostEstimate(flops=50 * cost, bytes_accessed=cost, transcendentals=0),
        name=name,
    )(*operands)


def dot(a, b):
    return jnp.dot(a, b, preferred_element_type=F32)


def dot_nt(a, b):
    return lax.dot_general(a, b, NT, preferred_element_type=F32)


def tied(values, *others):
    leaves, tree = jax.tree.flatten(values)
    kept = lax.optimization_barrier(tuple(leaves) + tuple(jax.tree.leaves(others)))
    return jax.tree.unflatten(tree, kept[: len(leaves)])


def bits_by_count(rows):
    return [[bits for bits in range(rows) if bits.bit_count() == n] for n in range(1, (rows - 1).bit_count() + 1)]


def pack_kernel(emb_ref, cid_ref, lead_ref, rest_ref):
    docs = emb_ref.shape[0]
    lead_ref[:docs, :] = emb_ref[:, :PREFIX]
    rest_ref[...] = emb_ref[:, PREFIX:]
    cid = cid_ref[...]
    high, low = (cid // DIGIT + 1).astype(F32), (cid % DIGIT).astype(F32)
    rows = []
    for digit in (high, low):
        rows += [digit[:, at : at + PREFIX] for at in range(0, docs, PREFIX)]
    rows.append(jnp.zeros((META - len(rows), PREFIX), F32))
    lead_ref[docs:, :] = jnp.concatenate(rows, axis=0).astype(BF16)


def ids_of(lead_ref):
    docs = lead_ref.shape[0] - META
    meta = lead_ref[docs:, :].astype(F32)
    parts = docs // PREFIX
    high = jnp.concatenate([meta[i : i + 1] for i in range(parts)], axis=1)
    low = jnp.concatenate([meta[parts + i : parts + i + 1] for i in range(parts)], axis=1)
    return (high - 1.0) * DIGIT + low


def prep_kernel(subs, per, place_ref, cent_ref, inv_ref, centre_ref, own_prefix_ref, prior_ref, prefix_ref):
    clusters = cent_ref.shape[0]
    half = centre_ref.shape[1]
    z, x, h = lax.axis_index("rows"), lax.axis_index("sub"), lax.axis_index("dim")
    row = lax.broadcasted_iota(jnp.int32, (subs * per, clusters), 0)
    ids = lax.broadcasted_iota(jnp.int32, (subs * per, clusters), 1)
    turn, within = row // per, row % per
    target = (z * subs + (x + turn) % subs) * per + within
    chosen = (place_ref[...] == target).astype(F32)
    inv_ref[...] = jnp.sum(chosen * ids.astype(F32), axis=1, keepdims=True)
    columns = cent_ref[:, pl.ds(pl.multiple_of(h * half, LANES), half)]
    centre_ref[...] = dot(chosen.astype(BF16), columns).astype(BF16)
    natural = (ids == target).astype(BF16)
    prior_ref[...] = dot(natural[:per], columns).astype(BF16)
    prefix_ref[...] = cent_ref[:, :PREFIX]
    own_prefix_ref[...] = dot(natural, prefix_ref[...]).astype(BF16)


def centred(pick, centre, columns):
    slots = pick.shape[0]
    groups = slots // (MOST * SUBLANES)
    width = columns.shape[1]
    present = jnp.sum(pick.astype(F32), axis=1, keepdims=True)
    raw = dot(pick, columns)
    middle = centre.astype(F32).reshape(groups, 1, SUBLANES, width)
    middle = jnp.broadcast_to(middle, (groups, MOST, SUBLANES, width)).reshape(slots, width)
    return jnp.where(present > 0.0, raw - middle, 0.0).astype(BF16)


def picked(lead_ref, inv_ref):
    cid = ids_of(lead_ref)
    docs = cid.shape[1]
    groups = inv_ref.shape[0] // SUBLANES
    match = (inv_ref[...] == cid).astype(F32)
    before = lax.broadcasted_iota(jnp.int32, (docs, docs), 0) < lax.broadcasted_iota(jnp.int32, (docs, docs), 1)
    earlier = dot(match.astype(BF16), before.astype(F32).astype(BF16))
    ranked = [jnp.where(earlier == r, match, 0.0).reshape(groups, SUBLANES, docs) for r in range(MOST)]
    return jnp.stack(ranked, axis=1).reshape(groups * MOST * SUBLANES, docs).astype(BF16)


def select_kernel(lead_ref, rest_ref, inv_ref, centre_ref, *row_refs):
    docs = rest_ref.shape[0]
    pick = picked(lead_ref, inv_ref)
    groups, packed, _ = row_refs[0].shape
    for columns, at in ((lead_ref[:docs, :], 0), (rest_ref[...], PREFIX)):
        width = columns.shape[1]
        rows = centred(pick, centre_ref[:, at : at + width], columns)
        rows = rows.reshape(len(row_refs), groups, packed, width)
        for t, ref in enumerate(row_refs):
            ref[:, :, at : at + width] = rows[t]


def select_lead_kernel(count, subs, inv_ref, centre_ref, *refs):
    lead_refs, pick_refs, row_refs = refs[:count], refs[count : 2 * count], refs[2 * count :]
    for i in range(count):
        docs = lead_refs[i].shape[0] - META
        pick = picked(lead_refs[i], inv_ref)
        pick_refs[i][...] = pick
        rows = centred(pick, centre_ref[:, :PREFIX], lead_refs[i][:docs, :])
        rows = rows.reshape((subs,) + row_refs[0].shape[1:])
        for t in range(subs):
            row_refs[t][i] = rows[t]


def select_rest_kernel(count, subs, centre_ref, *refs):
    pick_refs, rest_refs, row_refs = refs[:count], refs[count : 2 * count], refs[2 * count :]
    for i in range(count):
        rows = centred(pick_refs[i][...], centre_ref[:, PREFIX:], rest_refs[i][...])
        rows = rows.reshape((subs,) + row_refs[0].shape[1:])
        for t in range(subs):
            row_refs[t][i] = rows[t]


def soft_weights(lead_ref, near_ref, cent_ref, own_prefix_ref):
    docs = lead_ref.shape[0] - META
    h = lax.axis_index("dim")
    prefix = jnp.where(h == 0, lead_ref[:docs, :], near_ref[:docs, :])
    scores = dot_nt(cent_ref[...], prefix) * TEMP
    top = jnp.max(scores, axis=0, keepdims=True)
    scale = 1.0 / jnp.sum(jnp.exp(scores - top), axis=0, keepdims=True)
    own = dot_nt(own_prefix_ref[...], prefix) * TEMP
    return jnp.where(ids_of(lead_ref) >= 0.0, jnp.exp(own - top) * scale, 0.0)


def add_lead(weights, lead_ref, old_refs, new_refs):
    docs = lead_ref.shape[0] - META
    per = new_refs[0].shape[0] - SUBLANES
    sums = dot(weights.astype(BF16), lead_ref[:docs, :])
    ones = jnp.ones((SUBLANES, docs), BF16)
    for t, new in enumerate(new_refs):
        here = slice(t * per, (t + 1) * per)
        mass = dot_nt(ones, weights[here].astype(BF16))
        if old_refs:
            old = old_refs[t]
            new[:per, :] = old[:per, :] + sums[here]
            new[per:, :] = old[per:, :]
            new[per:, :per] = old[per:, :per] + mass
        else:
            new[:per, :] = sums[here]
            new[per:, :] = jnp.zeros((SUBLANES, new.shape[1]), F32)
            new[per:, :per] = mass


def add_rest(weights, rest, old_refs, new_refs):
    per = new_refs[0].shape[0]
    sums = dot(weights, rest)
    for t, new in enumerate(new_refs):
        part = sums[t * per : (t + 1) * per]
        new[...] = old_refs[t][...] + part if old_refs else part


def sums_kernel(subs, lead_ref, rest_ref, near_ref, cent_ref, own_prefix_ref, *new):
    weights = soft_weights(lead_ref, near_ref, cent_ref, own_prefix_ref)
    add_lead(weights, lead_ref, (), new[:subs])
    add_rest(weights.astype(BF16), rest_ref[...], (), new[subs:])


def sums_lead_kernel(subs, lead_ref, near_ref, cent_ref, own_prefix_ref, *refs):
    old, weights_ref, new = refs[:subs], refs[subs], refs[subs + 1 :]
    weights = soft_weights(lead_ref, near_ref, cent_ref, own_prefix_ref)
    weights_ref[...] = weights.astype(BF16)
    add_lead(weights, lead_ref, old, new)


def sums_rest_kernel(count, subs, *refs):
    weights_refs, rest_refs, old, new = refs[:count], refs[count : 2 * count], refs[-2 * subs : -subs], refs[-subs:]
    total = sum(dot(w[...], rest[...]) for w, rest in zip(weights_refs, rest_refs))
    per = new[0].shape[0]
    for t in range(subs):
        new[t][...] = old[t][...] + total[t * per : (t + 1) * per]


def gram_kernel(groups_of_bits, subs, *refs):
    *member_refs, gram_ref, held = refs
    z, x = lax.axis_index("rows"), lax.axis_index("sub")
    owners, groups, packed, half = held.shape
    each = len(member_refs) // subs
    for t in range(subs):
        own, *chunks = member_refs[t * each : (t + 1) * each]
        column = (x - t + subs) % subs
        held[z * subs + column] = own[...]
        for k, group in enumerate(groups_of_bits):
            for i, bits in enumerate(group):
                row = (z ^ bits) * subs + column
                held[row, :, :, :PREFIX] = chunks[2 * k][i]
                held[row, :, :, PREFIX:] = chunks[2 * k + 1][i]

    size = owners * packed
    lane = lax.broadcasted_iota(jnp.int32, (1, SUBLANES, size), 2) % SUBLANES
    same = (lane == lax.broadcasted_iota(jnp.int32, (1, SUBLANES, size), 1)).astype(F32)
    tile = min(size, 2 * LANES)
    for g in range(groups):
        mine = held[:, g].reshape(size, half)
        for start in range(0, size, tile):
            part = dot_nt(mine[start : start + tile], mine)
            part = part.reshape(tile // SUBLANES, SUBLANES, size)
            gram_ref[g, start // SUBLANES : (start + tile) // SUBLANES, :] = jnp.sum(part * same, axis=1)


def scaled_tiles(width, mine_ref, other_ref, scaled_ref):
    groups, slots, size = mine_ref.shape
    kept = scaled_ref.shape[1]
    h = lax.axis_index("dim")
    start = pl.multiple_of(h * kept, kept)
    row = lax.broadcasted_iota(jnp.int32, (slots, size), 0)
    lane = lax.broadcasted_iota(jnp.int32, (slots, size), 1)
    diagonal = row == lane // SUBLANES
    kept_row = lax.broadcasted_iota(jnp.int32, (kept, size), 0) + start
    kept_lane = lax.broadcasted_iota(jnp.int32, (kept, size), 1)
    kept_diagonal = kept_row == kept_lane // SUBLANES
    for g in range(groups):
        total = mine_ref[g] + other_ref[g]
        norms = jnp.sum(jnp.where(diagonal, total, 0.0), axis=0, keepdims=True)
        scale = lax.rsqrt(norms / width + EPS)
        spread = jnp.where(kept_diagonal, jnp.broadcast_to(scale, (kept, size)), 0.0)
        folded = spread[:, :LANES]
        for at in range(LANES, size, LANES):
            folded = folded + spread[:, at : at + LANES]
        step = SUBLANES
        while step < LANES:
            folded = folded + pltpu.roll(folded, step, 1)
            step *= 2
        row_scale = jnp.concatenate([folded] * (size // LANES), axis=1)
        own = mine_ref[g, pl.ds(start, kept), :] + other_ref[g, pl.ds(start, kept), :]
        scaled_ref[g] = own / width * row_scale * scale


def finish_kernel(width, mine_ref, other_ref, *refs):
    *part_refs, prior_ref, new_ref, tile_ref, scaled_ref = refs
    subs = len(part_refs) // 2
    lead = sum(ref[...] for ref in part_refs[1:subs]) + part_refs[0][...]
    rest = sum(ref[...] for ref in part_refs[subs + 1 :]) + part_refs[subs][...]
    per = rest.shape[0]
    mass = jnp.transpose(lead[per:, :LANES])[:per, :1] + SMOOTH
    prior = SMOOTH * prior_ref[...].astype(F32)
    new_ref[:, :PREFIX] = (lead[:per] + prior[:, :PREFIX]) / mass
    new_ref[:, PREFIX:] = (rest + prior[:, PREFIX:]) / mass

    scaled_tiles(width, mine_ref, other_ref, scaled_ref)
    groups, kept, size = scaled_ref.shape
    slots = size // SUBLANES
    at = lax.broadcasted_iota(jnp.int32, (groups * size, per), 0)
    to = lax.broadcasted_iota(jnp.int32, (groups * size, per), 1)
    move = ((at // size == to // SUBLANES) & (at % SUBLANES == to % SUBLANES)).astype(F32).astype(BF16)
    row = lax.broadcasted_iota(jnp.int32, (slots, size), 0)
    lane = lax.broadcasted_iota(jnp.int32, (slots, size), 1)
    here = row == lane // SUBLANES
    batch = max(1, LANES // slots)

    def some(step, carry):
        spread = []
        for b in range(batch):
            i = step * batch + b
            lines = [jnp.broadcast_to(scaled_ref[g, pl.ds(i, 1), :], (slots, size)) for g in range(groups)]
            spread.append(jnp.concatenate([jnp.where(here, line, 0.0) for line in lines], axis=1))
        moved = dot(jnp.concatenate(spread, axis=0).astype(BF16), move).astype(BF16)
        for b in range(batch):
            tile_ref[step * batch + b] = moved[b * slots : (b + 1) * slots]
        return carry

    if kept == batch:
        some(0, 0)
    else:
        lax.fori_loop(0, kept // batch, some, 0)


def shards(embeddings, centroids, cluster_id, cluster_place):
    docs, half = embeddings.shape
    clusters, width = centroids.shape
    rows, subs = lax.axis_size("rows"), lax.axis_size("sub")
    owners = rows * subs
    per = clusters // owners
    groups = per // SUBLANES
    packed = MOST * SUBLANES
    slots = owners * MOST
    groups_of_bits = bits_by_count(rows)
    shape = jax.ShapeDtypeStruct

    def across(values):
        got = [values[0]]
        for t in range(1, subs):
            got.append(lax.ppermute(values[t], "sub", [(i, (i + t) % subs) for i in range(subs)]))
        return got

    def near(value):
        return lax.ppermute(value, "dim", [(0, 1), (1, 0)])

    def swap(value, bit):
        return lax.ppermute(value, "rows", [(i, i ^ bit) for i in range(rows)])

    def send(blocks, bits):
        bit = (bits & -bits or rows) // 2
        while bit:
            blocks[bits | bit] = swap(blocks[bits], bit)
            bit //= 2

    lead, rest = call(
        pack_kernel,
        "pack",
        [shape((docs + META, PREFIX), BF16), shape((docs, half - PREFIX), BF16)],
        [embeddings, cluster_id.reshape(1, docs)],
    )
    leads, rests = {0: lead}, {0: rest}
    send(leads, 0)

    inv, centre, own_prefix, prior, cent_prefix = call(
        functools.partial(prep_kernel, subs, per),
        "prep",
        [
            shape((subs * per, 1), F32),
            shape((subs * per, half), BF16),
            shape((subs * per, PREFIX), BF16),
            shape((per, half), BF16),
            shape((clusters, PREFIX), BF16),
        ],
        [cluster_place.reshape(1, clusters), centroids],
        cost=4 * 1024 * 1024,
    )

    lead_sum, rest_sum = shape((per + SUBLANES, PREFIX), F32), shape((per, half - PREFIX), F32)
    sum_shapes = [lead_sum] * subs + [rest_sum] * subs
    own_cost, other_cost = 2 * 1024 * 1024, 128 * 1024

    prefix = near(lead)
    found = call(
        select_kernel, "select", [shape((groups, packed, half), BF16)] * subs, [lead, rest, inv, centre], cost=own_cost
    )
    members = [across(found)]
    rests[0] = tied(rest, found)
    send(rests, 0)
    sums = call(
        functools.partial(sums_kernel, subs),
        "sums",
        sum_shapes,
        [lead, rest, prefix, cent_prefix, own_prefix],
        cost=own_cost,
    )
    lead_sums, rest_sums = list(sums[:subs]), list(sums[subs:])

    for group in groups_of_bits:
        last = group == groups_of_bits[-1]
        count = len(group)
        before = members[:-1] if last else members
        leads.update(zip(group, tied([leads[bits] for bits in group], found, lead_sums, rest_sums, before)))
        for bits in group:
            send(leads, bits)
        prefixes = [near(leads[bits]) for bits in group]
        row_shapes = [shape((count, groups, packed, PREFIX), BF16)] * subs
        found = call(
            functools.partial(select_lead_kernel, count, subs),
            "select_lead",
            [shape((subs * per * MOST, docs), BF16)] * count + row_shapes,
            [inv, centre] + [leads[bits] for bits in group],
            cost=other_cost,
        )
        picks, found = list(found[:count]), list(found[count:])
        members.append(across(found))
        weights = []
        for bits, prefix in zip(group, prefixes):
            weight, *lead_sums = call(
                functools.partial(sums_lead_kernel, subs),
                "sums_lead",
                [shape((subs * per, docs), BF16)] + [lead_sum] * subs,
                [leads[bits], prefix, cent_prefix, own_prefix] + lead_sums,
                {4 + i: 1 + i for i in range(subs)},
                cost=other_cost,
            )
            weights.append(weight)
        if last:
            lead_sums = across(lead_sums)
            before = (prefixes, members[:-1])
        else:
            before = (found, weights, members)
        rests.update(zip(group, tied([rests[bits] for bits in group], before)))
        for bits in group:
            send(rests, bits)
        row_shapes = [shape((count, groups, packed, half - PREFIX), BF16)] * subs
        found = call(
            functools.partial(select_rest_kernel, count, subs),
            "select_rest",
            row_shapes,
            [centre] + picks + [rests[bits] for bits in group],
            cost=other_cost,
        )
        members.append(across(found))
        rest_sums = call(
            functools.partial(sums_rest_kernel, count, subs),
            "sums_rest",
            [rest_sum] * subs,
            weights + [rests[bits] for bits in group] + list(rest_sums),
            {2 * count + i: i for i in range(subs)},
            cost=other_cost,
        )
    rest_sums = across(rest_sums)

    (gram,) = call(
        functools.partial(gram_kernel, groups_of_bits, subs),
        "gram",
        [shape((groups, slots, slots * SUBLANES), F32)],
        [arrays[t] for t in range(subs) for arrays in members],
        scratch=[pltpu.VMEM((owners, groups, packed, half), BF16)],
    )
    new_centroids, tiles = call(
        functools.partial(finish_kernel, width),
        "finish",
        [shape((per, half), F32), shape((slots // 2, slots, per), BF16)],
        [gram, near(gram)] + lead_sums + rest_sums + [prior],
        scratch=[pltpu.VMEM((groups, slots // 2, slots * SUBLANES), F32)],
    )
    return (new_centroids, jnp.transpose(tiles, (2, 0, 1)))


def solution(mesh):
    in_specs = (
        P(("parts", "rows", "sub"), "dim"),
        P("parts", None),
        P(("parts", "rows", "sub"), None),
        P(),
    )
    out_specs = (P(("parts", "rows", "sub"), "dim"), P(("parts", "rows", "sub"), "dim", None))
    return jax.shard_map(shards, mesh=mesh, in_specs=in_specs, out_specs=out_specs, check_vma=False)
```

```python
import functools

import jax
import jax.numpy as jnp
from jax import lax
from jax.experimental import pallas as pl
from jax.experimental.pallas import tpu as pltpu
from jax.sharding import PartitionSpec as P

PREFIX = 256
MOST = 2

TEMP = 0.125
SMOOTH = 1.0
EPS = 1e-05

DIGIT = 32
META = 16
SUBLANES = 8
LANES = 128
F32 = jnp.float32
BF16 = jnp.bfloat16
VMEM_LIMIT = 40 * 1024 * 1024

NT = (((1,), (1,)), ((), ()))


def call(kernel, name, out_shape, operands, aliases=None, scratch=(), far=0, cost=0):
    def place(at):
        return pl.BlockSpec(memory_space=pltpu.HBM if at < far else pltpu.VMEM)

    return pl.pallas_call(
        kernel,
        out_shape=tuple(out_shape),
        in_specs=[place(at) for at in range(len(operands))],
        out_specs=tuple(pl.BlockSpec(memory_space=pltpu.VMEM) for _ in out_shape),
        input_output_aliases=aliases or {},
        scratch_shapes=list(scratch),
        compiler_params=pltpu.CompilerParams(vmem_limit_bytes=VMEM_LIMIT),
        cost_estimate=pl.CostEstimate(flops=50 * cost, bytes_accessed=cost, transcendentals=0),
        name=name,
    )(*operands)


def dot(a, b):
    return jnp.dot(a, b, preferred_element_type=F32)


def dot_nt(a, b):
    return lax.dot_general(a, b, NT, preferred_element_type=F32)


def tied(values, *others):
    leaves, tree = jax.tree.flatten(values)
    kept = lax.optimization_barrier(tuple(leaves) + tuple(jax.tree.leaves(others)))
    return jax.tree.unflatten(tree, kept[: len(leaves)])


def bits_by_count(rows):
    return [[bits for bits in range(rows) if bits.bit_count() == n] for n in range(1, (rows - 1).bit_count() + 1)]


def pack_kernel(emb_ref, cid_ref, lead_ref, rest_ref):
    docs = emb_ref.shape[0]
    lead_ref[:docs, :] = emb_ref[:, :PREFIX]
    rest_ref[:docs, :] = emb_ref[:, PREFIX:]
    rest_ref[docs:, :] = jnp.zeros((META, rest_ref.shape[1]), BF16)
    cid = cid_ref[...]
    high, low = (cid // DIGIT + 1).astype(F32), (cid % DIGIT).astype(F32)
    rows = []
    for digit in (high, low):
        rows += [digit[:, at : at + PREFIX] for at in range(0, docs, PREFIX)]
    rows.append(jnp.zeros((META - len(rows), PREFIX), F32))
    lead_ref[docs:, :] = jnp.concatenate(rows, axis=0).astype(BF16)


def ids_of(lead_ref):
    docs = lead_ref.shape[0] - META
    meta = lead_ref[docs:, :].astype(F32)
    parts = docs // PREFIX
    high = jnp.concatenate([meta[i : i + 1] for i in range(parts)], axis=1)
    low = jnp.concatenate([meta[parts + i : parts + i + 1] for i in range(parts)], axis=1)
    return (high - 1.0) * DIGIT + low


def prep_kernel(subs, per, place_ref, cent_ref, inv_ref, centre_ref, own_prefix_ref, prior_ref, prefix_ref):
    clusters = cent_ref.shape[0]
    half = centre_ref.shape[1]
    z, x, h = lax.axis_index("rows"), lax.axis_index("sub"), lax.axis_index("dim")
    row = lax.broadcasted_iota(jnp.int32, (subs * per, clusters), 0)
    ids = lax.broadcasted_iota(jnp.int32, (subs * per, clusters), 1)
    turn, within = row // per, row % per
    target = (z * subs + (x + turn) % subs) * per + within
    chosen = (place_ref[...] == target).astype(F32)
    inv_ref[...] = jnp.sum(chosen * ids.astype(F32), axis=1, keepdims=True)
    columns = cent_ref[:, pl.ds(pl.multiple_of(h * half, LANES), half)]
    centre_ref[...] = dot(chosen.astype(BF16), columns).astype(BF16)
    natural = (ids == target).astype(BF16)
    prior_ref[...] = dot(natural[:per], columns).astype(BF16)
    prefix_ref[...] = cent_ref[:, :PREFIX]
    own_prefix_ref[...] = dot(natural, prefix_ref[...]).astype(BF16)


def centred(pick, centre, columns):
    slots = pick.shape[0]
    groups = slots // (MOST * SUBLANES)
    width = columns.shape[1]
    present = jnp.sum(pick.astype(F32), axis=1, keepdims=True)
    raw = dot(pick, columns)
    middle = centre.astype(F32).reshape(groups, 1, SUBLANES, width)
    middle = jnp.broadcast_to(middle, (groups, MOST, SUBLANES, width)).reshape(slots, width)
    return jnp.where(present > 0.0, raw - middle, 0.0).astype(BF16)


def picked(lead_ref, inv_ref):
    cid = ids_of(lead_ref)
    docs = cid.shape[1]
    groups = inv_ref.shape[0] // SUBLANES
    match = (inv_ref[...] == cid).astype(F32)
    before = lax.broadcasted_iota(jnp.int32, (docs, docs), 0) < lax.broadcasted_iota(jnp.int32, (docs, docs), 1)
    earlier = dot(match.astype(BF16), before.astype(F32).astype(BF16))
    ranked = [jnp.where(earlier == r, match, 0.0).reshape(groups, SUBLANES, docs) for r in range(MOST)]
    return jnp.stack(ranked, axis=1).reshape(groups * MOST * SUBLANES, docs).astype(BF16)


def select_kernel(lead_ref, rest_ref, inv_ref, centre_ref, *row_refs):
    docs = rest_ref.shape[0] - META
    pick = picked(lead_ref, inv_ref)
    groups, packed, _ = row_refs[0].shape
    for columns, at in ((lead_ref[:docs, :], 0), (rest_ref[:docs, :], PREFIX)):
        width = columns.shape[1]
        rows = centred(pick, centre_ref[:, at : at + width], columns)
        rows = rows.reshape(len(row_refs), groups, packed, width)
        for t, ref in enumerate(row_refs):
            ref[:, :, at : at + width] = rows[t]


def select_lead_kernel(count, subs, inv_ref, centre_ref, *refs):
    lead_refs, pick_refs, row_refs = refs[:count], refs[count : 2 * count], refs[2 * count :]
    for i in range(count):
        docs = lead_refs[i].shape[0] - META
        pick = picked(lead_refs[i], inv_ref)
        pick_refs[i][...] = pick
        rows = centred(pick, centre_ref[:, :PREFIX], lead_refs[i][:docs, :])
        rows = rows.reshape((subs,) + row_refs[0].shape[1:])
        for t in range(subs):
            row_refs[t][i] = rows[t]


def select_rest_kernel(count, subs, centre_ref, *refs):
    pick_refs, rest_refs, row_refs = refs[:count], refs[count : 2 * count], refs[2 * count :]
    for i in range(count):
        pick = pick_refs[i][...]
        rows = centred(pick, centre_ref[:, PREFIX:], rest_refs[i][: pick.shape[1], :])
        rows = rows.reshape((subs,) + row_refs[0].shape[1:])
        for t in range(subs):
            row_refs[t][i] = rows[t]


def soft_weights(lead_ref, near_ref, cent_ref, own_prefix_ref):
    docs = lead_ref.shape[0] - META
    h = lax.axis_index("dim")
    prefix = jnp.where(h == 0, lead_ref[:docs, :], near_ref[:docs, :])
    scores = dot_nt(cent_ref[...], prefix) * TEMP
    top = jnp.max(scores, axis=0, keepdims=True)
    scale = 1.0 / jnp.sum(jnp.exp(scores - top), axis=0, keepdims=True)
    own = dot_nt(own_prefix_ref[...], prefix) * TEMP
    return jnp.where(ids_of(lead_ref) >= 0.0, jnp.exp(own - top) * scale, 0.0)


def add_lead(weights, lead_ref, old_refs, new_refs):
    docs = lead_ref.shape[0] - META
    per = new_refs[0].shape[0] - SUBLANES
    sums = dot(weights.astype(BF16), lead_ref[:docs, :])
    ones = jnp.ones((SUBLANES, docs), BF16)
    for t, new in enumerate(new_refs):
        here = slice(t * per, (t + 1) * per)
        mass = dot_nt(ones, weights[here].astype(BF16))
        if old_refs:
            old = old_refs[t]
            new[:per, :] = old[:per, :] + sums[here]
            new[per:, :] = old[per:, :]
            new[per:, :per] = old[per:, :per] + mass
        else:
            new[:per, :] = sums[here]
            new[per:, :] = jnp.zeros((SUBLANES, new.shape[1]), F32)
            new[per:, :per] = mass


def add_rest(weights, rest, old_refs, new_refs):
    per = new_refs[0].shape[0]
    sums = dot(weights, rest)
    for t, new in enumerate(new_refs):
        part = sums[t * per : (t + 1) * per]
        new[...] = old_refs[t][...] + part if old_refs else part


def sums_kernel(subs, lead_ref, rest_ref, near_ref, cent_ref, own_prefix_ref, *new):
    weights = soft_weights(lead_ref, near_ref, cent_ref, own_prefix_ref)
    add_lead(weights, lead_ref, (), new[:subs])
    add_rest(weights.astype(BF16), rest_ref[: weights.shape[1], :], (), new[subs:])


def sums_lead_kernel(subs, lead_ref, near_ref, cent_ref, own_prefix_ref, *refs):
    old, weights_ref, new = refs[:subs], refs[subs], refs[subs + 1 :]
    weights = soft_weights(lead_ref, near_ref, cent_ref, own_prefix_ref)
    weights_ref[...] = weights.astype(BF16)
    add_lead(weights, lead_ref, old, new)


def sums_rest_kernel(count, subs, *refs):
    weights_refs, rest_refs, old, new = refs[:count], refs[count : 2 * count], refs[-2 * subs : -subs], refs[-subs:]
    total = sum(dot(w[...], rest[: w.shape[1], :]) for w, rest in zip(weights_refs, rest_refs))
    per = new[0].shape[0]
    for t in range(subs):
        new[t][...] = old[t][...] + total[t * per : (t + 1) * per]


def gram_kernel(groups_of_bits, subs, *refs):
    *member_refs, gram_ref, held = refs
    z, x = lax.axis_index("rows"), lax.axis_index("sub")
    owners, groups, packed, half = held.shape
    each = len(member_refs) // subs
    for t in range(subs):
        own, *chunks = member_refs[t * each : (t + 1) * each]
        column = (x - t + subs) % subs
        held[z * subs + column] = own[...]
        for k, group in enumerate(groups_of_bits):
            for i, bits in enumerate(group):
                row = (z ^ bits) * subs + column
                held[row, :, :, :PREFIX] = chunks[2 * k][i]
                held[row, :, :, PREFIX:] = chunks[2 * k + 1][i]

    size = owners * packed
    lane = lax.broadcasted_iota(jnp.int32, (1, SUBLANES, size), 2) % SUBLANES
    same = (lane == lax.broadcasted_iota(jnp.int32, (1, SUBLANES, size), 1)).astype(F32)
    tile = min(size, 2 * LANES)
    for g in range(groups):
        mine = held[:, g].reshape(size, half)
        for start in range(0, size, tile):
            part = dot_nt(mine[start : start + tile], mine)
            part = part.reshape(tile // SUBLANES, SUBLANES, size)
            gram_ref[g, start // SUBLANES : (start + tile) // SUBLANES, :] = jnp.sum(part * same, axis=1)


def scaled_tiles(width, mine_ref, other_ref, scaled_ref):
    groups, slots, size = mine_ref.shape
    kept = scaled_ref.shape[1]
    h = lax.axis_index("dim")
    start = pl.multiple_of(h * kept, kept)
    row = lax.broadcasted_iota(jnp.int32, (slots, size), 0)
    lane = lax.broadcasted_iota(jnp.int32, (slots, size), 1)
    diagonal = row == lane // SUBLANES
    kept_row = lax.broadcasted_iota(jnp.int32, (kept, size), 0) + start
    kept_lane = lax.broadcasted_iota(jnp.int32, (kept, size), 1)
    kept_diagonal = kept_row == kept_lane // SUBLANES
    for g in range(groups):
        total = mine_ref[g] + other_ref[g]
        norms = jnp.sum(jnp.where(diagonal, total, 0.0), axis=0, keepdims=True)
        scale = lax.rsqrt(norms / width + EPS)
        spread = jnp.where(kept_diagonal, jnp.broadcast_to(scale, (kept, size)), 0.0)
        folded = spread[:, :LANES]
        for at in range(LANES, size, LANES):
            folded = folded + spread[:, at : at + LANES]
        step = SUBLANES
        while step < LANES:
            folded = folded + pltpu.roll(folded, step, 1)
            step *= 2
        row_scale = jnp.concatenate([folded] * (size // LANES), axis=1)
        own = mine_ref[g, pl.ds(start, kept), :] + other_ref[g, pl.ds(start, kept), :]
        scaled_ref[g] = own / width * row_scale * scale


def finish_kernel(width, mine_ref, other_ref, *refs):
    *part_refs, prior_ref, new_ref, tile_ref, scaled_ref = refs
    subs = len(part_refs) // 2
    lead = sum(ref[...] for ref in part_refs[1:subs]) + part_refs[0][...]
    rest = sum(ref[...] for ref in part_refs[subs + 1 :]) + part_refs[subs][...]
    per = rest.shape[0]
    mass = jnp.transpose(lead[per:, :LANES])[:per, :1] + SMOOTH
    prior = SMOOTH * prior_ref[...].astype(F32)
    new_ref[:, :PREFIX] = (lead[:per] + prior[:, :PREFIX]) / mass
    new_ref[:, PREFIX:] = (rest + prior[:, PREFIX:]) / mass

    scaled_tiles(width, mine_ref, other_ref, scaled_ref)
    groups, kept, size = scaled_ref.shape
    slots = size // SUBLANES
    at = lax.broadcasted_iota(jnp.int32, (groups * size, per), 0)
    to = lax.broadcasted_iota(jnp.int32, (groups * size, per), 1)
    move = ((at // size == to // SUBLANES) & (at % SUBLANES == to % SUBLANES)).astype(F32).astype(BF16)
    row = lax.broadcasted_iota(jnp.int32, (slots, size), 0)
    lane = lax.broadcasted_iota(jnp.int32, (slots, size), 1)
    here = row == lane // SUBLANES
    batch = max(1, LANES // slots)

    def some(step, carry):
        spread = []
        for b in range(batch):
            i = step * batch + b
            lines = [jnp.broadcast_to(scaled_ref[g, pl.ds(i, 1), :], (slots, size)) for g in range(groups)]
            spread.append(jnp.concatenate([jnp.where(here, line, 0.0) for line in lines], axis=1))
        moved = dot(jnp.concatenate(spread, axis=0).astype(BF16), move).astype(BF16)
        for b in range(batch):
            tile_ref[step * batch + b] = moved[b * slots : (b + 1) * slots]
        return carry

    if kept == batch:
        some(0, 0)
    else:
        lax.fori_loop(0, kept // batch, some, 0)


def shards(embeddings, centroids, cluster_id, cluster_place):
    docs, half = embeddings.shape
    clusters, width = centroids.shape
    rows, subs = lax.axis_size("rows"), lax.axis_size("sub")
    owners = rows * subs
    per = clusters // owners
    groups = per // SUBLANES
    packed = MOST * SUBLANES
    slots = owners * MOST
    groups_of_bits = bits_by_count(rows)
    shape = jax.ShapeDtypeStruct

    def across(values):
        got = [values[0]]
        for t in range(1, subs):
            got.append(lax.ppermute(values[t], "sub", [(i, (i + t) % subs) for i in range(subs)]))
        return got

    def near(value):
        return lax.ppermute(value, "dim", [(0, 1), (1, 0)])

    def swap(value, bit):
        return lax.ppermute(value, "rows", [(i, i ^ bit) for i in range(rows)])

    def send(blocks, bits):
        bit = (bits & -bits or rows) // 2
        while bit:
            blocks[bits | bit] = swap(blocks[bits], bit)
            bit //= 2

    lead, rest = call(
        pack_kernel,
        "pack",
        [shape((docs + META, PREFIX), BF16), shape((docs + META, half - PREFIX), BF16)],
        [embeddings, cluster_id.reshape(1, docs)],
    )
    leads, rests = {0: lead}, {0: rest}
    send(leads, 0)

    inv, centre, own_prefix, prior, cent_prefix = call(
        functools.partial(prep_kernel, subs, per),
        "prep",
        [
            shape((subs * per, 1), F32),
            shape((subs * per, half), BF16),
            shape((subs * per, PREFIX), BF16),
            shape((per, half), BF16),
            shape((clusters, PREFIX), BF16),
        ],
        [cluster_place.reshape(1, clusters), centroids],
        cost=4 * 1024 * 1024,
    )

    lead_sum, rest_sum = shape((per + SUBLANES, PREFIX), F32), shape((per, half - PREFIX), F32)
    sum_shapes = [lead_sum] * subs + [rest_sum] * subs
    own_cost, other_cost = 2 * 1024 * 1024, 0

    prefix = near(lead)
    found = call(
        select_kernel, "select", [shape((groups, packed, half), BF16)] * subs, [lead, rest, inv, centre], cost=own_cost
    )
    members = [across(found)]
    rests[0] = tied(rest, found)
    send(rests, 0)
    sums = call(
        functools.partial(sums_kernel, subs),
        "sums",
        sum_shapes,
        [lead, rest, prefix, cent_prefix, own_prefix],
        cost=own_cost,
    )
    lead_sums, rest_sums = list(sums[:subs]), list(sums[subs:])

    for group in groups_of_bits:
        last = group == groups_of_bits[-1]
        count = len(group)
        before = members[:-1] if last else members
        leads.update(zip(group, tied([leads[bits] for bits in group], found, lead_sums, rest_sums, before)))
        for bits in group:
            send(leads, bits)
        prefixes = [near(leads[bits]) for bits in group]
        row_shapes = [shape((count, groups, packed, PREFIX), BF16)] * subs
        found = call(
            functools.partial(select_lead_kernel, count, subs),
            "select_lead",
            [shape((subs * per * MOST, docs), BF16)] * count + row_shapes,
            [inv, centre] + [leads[bits] for bits in group],
            cost=other_cost,
        )
        picks, found = list(found[:count]), list(found[count:])
        members.append(across(found))
        weights = []
        for bits, prefix in zip(group, prefixes):
            weight, *lead_sums = call(
                functools.partial(sums_lead_kernel, subs),
                "sums_lead",
                [shape((subs * per, docs), BF16)] + [lead_sum] * subs,
                [leads[bits], prefix, cent_prefix, own_prefix] + lead_sums,
                {4 + i: 1 + i for i in range(subs)},
                cost=other_cost,
            )
            weights.append(weight)
        if last:
            lead_sums = across(lead_sums)
            before = (found, members[:-1])
        else:
            before = (found, members)
        rests.update(zip(group, tied([rests[bits] for bits in group], before)))
        for bits in group:
            send(rests, bits)
        row_shapes = [shape((count, groups, packed, half - PREFIX), BF16)] * subs
        found = call(
            functools.partial(select_rest_kernel, count, subs),
            "select_rest",
            row_shapes,
            [centre] + picks + [rests[bits] for bits in group],
            cost=other_cost,
        )
        if last:
            found = tied(found, members)
        members.append(across(found))
        rest_sums = call(
            functools.partial(sums_rest_kernel, count, subs),
            "sums_rest",
            [rest_sum] * subs,
            weights + [rests[bits] for bits in group] + list(rest_sums),
            {2 * count + i: i for i in range(subs)},
            cost=other_cost,
        )
    rest_sums = across(rest_sums)

    (gram,) = call(
        functools.partial(gram_kernel, groups_of_bits, subs),
        "gram",
        [shape((groups, slots, slots * SUBLANES), F32)],
        [arrays[t] for t in range(subs) for arrays in members],
        scratch=[pltpu.VMEM((owners, groups, packed, half), BF16)],
    )
    new_centroids, tiles = call(
        functools.partial(finish_kernel, width),
        "finish",
        [shape((per, half), F32), shape((slots // 2, slots, per), BF16)],
        [gram, near(gram)] + lead_sums + rest_sums + [prior],
        scratch=[pltpu.VMEM((groups, slots // 2, slots * SUBLANES), F32)],
    )
    return (new_centroids, jnp.transpose(tiles, (2, 0, 1)))


def solution(mesh):
    in_specs = (
        P(("parts", "rows", "sub"), "dim"),
        P("parts", None),
        P(("parts", "rows", "sub"), None),
        P(),
    )
    out_specs = (P(("parts", "rows", "sub"), "dim"), P(("parts", "rows", "sub"), "dim", None))
    return jax.shard_map(shards, mesh=mesh, in_specs=in_specs, out_specs=out_specs, check_vma=False)
```

```python
import functools

import jax
import jax.numpy as jnp
from jax import lax
from jax.experimental import pallas as pl
from jax.experimental.pallas import tpu as pltpu
from jax.sharding import PartitionSpec as P

PREFIX = 256
MOST = 2

TEMP = 0.125
SMOOTH = 1.0
EPS = 1e-05

DIGIT = 32
META = 16
SUBLANES = 8
LANES = 128
F32 = jnp.float32
BF16 = jnp.bfloat16
VMEM_LIMIT = 40 * 1024 * 1024

NT = (((1,), (1,)), ((), ()))


def call(kernel, name, out_shape, operands, aliases=None, scratch=(), cost=0):
    def whole(_):
        return pl.BlockSpec(memory_space=pltpu.VMEM)

    return pl.pallas_call(
        kernel,
        out_shape=tuple(out_shape),
        in_specs=[whole(operand) for operand in operands],
        out_specs=tuple(whole(out) for out in out_shape),
        input_output_aliases=aliases or {},
        scratch_shapes=list(scratch),
        compiler_params=pltpu.CompilerParams(vmem_limit_bytes=VMEM_LIMIT),
        cost_estimate=pl.CostEstimate(flops=50 * cost, bytes_accessed=cost, transcendentals=0),
        name=name,
    )(*operands)


def dot(a, b):
    return jnp.dot(a, b, preferred_element_type=F32)


def dot_nt(a, b):
    return lax.dot_general(a, b, NT, preferred_element_type=F32)


def tied(values, *others):
    leaves, tree = jax.tree.flatten(values)
    kept = lax.optimization_barrier(tuple(leaves) + tuple(jax.tree.leaves(others)))
    return jax.tree.unflatten(tree, kept[: len(leaves)])


def bits_by_count(rows):
    return [[bits for bits in range(rows) if bits.bit_count() == n] for n in range(1, (rows - 1).bit_count() + 1)]


def pack_kernel(emb_ref, cid_ref, lead_ref, rest_ref):
    docs = emb_ref.shape[0]
    lead_ref[:docs, :] = emb_ref[:, :PREFIX]
    rest_ref[:docs, :] = emb_ref[:, PREFIX:]
    rest_ref[docs:, :] = jnp.zeros((META, rest_ref.shape[1]), BF16)
    cid = cid_ref[...]
    high, low = (cid // DIGIT + 1).astype(F32), (cid % DIGIT).astype(F32)
    rows = []
    for digit in (high, low):
        rows += [digit[:, at : at + PREFIX] for at in range(0, docs, PREFIX)]
    rows.append(jnp.zeros((META - len(rows), PREFIX), F32))
    lead_ref[docs:, :] = jnp.concatenate(rows, axis=0).astype(BF16)


def ids_of(lead_ref):
    docs = lead_ref.shape[0] - META
    meta = lead_ref[docs:, :].astype(F32)
    parts = docs // PREFIX
    high = jnp.concatenate([meta[i : i + 1] for i in range(parts)], axis=1)
    low = jnp.concatenate([meta[parts + i : parts + i + 1] for i in range(parts)], axis=1)
    return (high - 1.0) * DIGIT + low


def prep_kernel(subs, per, place_ref, cent_ref, inv_ref, centre_ref, own_prefix_ref, prior_ref, prefix_ref):
    clusters = cent_ref.shape[0]
    half = centre_ref.shape[1]
    z, x, h = lax.axis_index("rows"), lax.axis_index("sub"), lax.axis_index("dim")
    row = lax.broadcasted_iota(jnp.int32, (subs * per, clusters), 0)
    ids = lax.broadcasted_iota(jnp.int32, (subs * per, clusters), 1)
    turn, within = row // per, row % per
    target = (z * subs + (x + turn) % subs) * per + within
    chosen = (place_ref[...] == target).astype(F32)
    inv_ref[...] = jnp.sum(chosen * ids.astype(F32), axis=1, keepdims=True)
    columns = cent_ref[:, pl.ds(pl.multiple_of(h * half, LANES), half)]
    centre_ref[...] = dot(chosen.astype(BF16), columns).astype(BF16)
    natural = (ids == target).astype(BF16)
    prior_ref[...] = dot(natural[:per], columns).astype(BF16)
    prefix_ref[...] = cent_ref[:, :PREFIX]
    own_prefix_ref[...] = dot(natural, prefix_ref[...]).astype(BF16)


def centred(pick, centre, columns):
    slots = pick.shape[0]
    groups = slots // (MOST * SUBLANES)
    width = columns.shape[1]
    present = jnp.sum(pick.astype(F32), axis=1, keepdims=True)
    raw = dot(pick, columns)
    middle = centre.astype(F32).reshape(groups, 1, SUBLANES, width)
    middle = jnp.broadcast_to(middle, (groups, MOST, SUBLANES, width)).reshape(slots, width)
    return jnp.where(present > 0.0, raw - middle, 0.0).astype(BF16)


def picked(lead_ref, inv_ref):
    cid = ids_of(lead_ref)
    docs = cid.shape[1]
    groups = inv_ref.shape[0] // SUBLANES
    match = (inv_ref[...] == cid).astype(F32)
    before = lax.broadcasted_iota(jnp.int32, (docs, docs), 0) < lax.broadcasted_iota(jnp.int32, (docs, docs), 1)
    earlier = dot(match.astype(BF16), before.astype(F32).astype(BF16))
    ranked = [jnp.where(earlier == r, match, 0.0).reshape(groups, SUBLANES, docs) for r in range(MOST)]
    return jnp.stack(ranked, axis=1).reshape(groups * MOST * SUBLANES, docs).astype(BF16)


def select_kernel(lead_ref, rest_ref, inv_ref, centre_ref, *row_refs):
    docs = rest_ref.shape[0] - META
    pick = picked(lead_ref, inv_ref)
    groups, packed, _ = row_refs[0].shape
    for columns, at in ((lead_ref[:docs, :], 0), (rest_ref[:docs, :], PREFIX)):
        width = columns.shape[1]
        rows = centred(pick, centre_ref[:, at : at + width], columns)
        rows = rows.reshape(len(row_refs), groups, packed, width)
        for t, ref in enumerate(row_refs):
            ref[:, :, at : at + width] = rows[t]


def select_lead_kernel(count, subs, inv_ref, centre_ref, *refs):
    lead_refs, pick_refs, row_refs = refs[:count], refs[count : 2 * count], refs[2 * count :]
    for i in range(count):
        docs = lead_refs[i].shape[0] - META
        pick = picked(lead_refs[i], inv_ref)
        pick_refs[i][...] = pick
        rows = centred(pick, centre_ref[:, :PREFIX], lead_refs[i][:docs, :])
        rows = rows.reshape((subs,) + row_refs[0].shape[1:])
        for t in range(subs):
            row_refs[t][i] = rows[t]


def select_rest_kernel(count, subs, centre_ref, *refs):
    pick_refs, rest_refs, row_refs = refs[:count], refs[count : 2 * count], refs[2 * count :]
    for i in range(count):
        pick = pick_refs[i][...]
        rows = centred(pick, centre_ref[:, PREFIX:], rest_refs[i][: pick.shape[1], :])
        rows = rows.reshape((subs,) + row_refs[0].shape[1:])
        for t in range(subs):
            row_refs[t][i] = rows[t]


def soft_weights(lead_ref, near_ref, cent_ref, own_prefix_ref):
    docs = lead_ref.shape[0] - META
    h = lax.axis_index("dim")
    prefix = jnp.where(h == 0, lead_ref[:docs, :], near_ref[:docs, :])
    scores = dot_nt(cent_ref[...], prefix) * TEMP
    top = jnp.max(scores, axis=0, keepdims=True)
    scale = 1.0 / jnp.sum(jnp.exp(scores - top), axis=0, keepdims=True)
    own = dot_nt(own_prefix_ref[...], prefix) * TEMP
    return jnp.where(ids_of(lead_ref) >= 0.0, jnp.exp(own - top) * scale, 0.0)


def add_lead(weights, lead_ref, old_refs, new_refs):
    docs = lead_ref.shape[0] - META
    per = new_refs[0].shape[0] - SUBLANES
    sums = dot(weights.astype(BF16), lead_ref[:docs, :])
    ones = jnp.ones((SUBLANES, docs), BF16)
    for t, new in enumerate(new_refs):
        here = slice(t * per, (t + 1) * per)
        mass = dot_nt(ones, weights[here].astype(BF16))
        if old_refs:
            old = old_refs[t]
            new[:per, :] = old[:per, :] + sums[here]
            new[per:, :] = old[per:, :]
            new[per:, :per] = old[per:, :per] + mass
        else:
            new[:per, :] = sums[here]
            new[per:, :] = jnp.zeros((SUBLANES, new.shape[1]), F32)
            new[per:, :per] = mass


def add_rest(weights, rest, old_refs, new_refs):
    per = new_refs[0].shape[0]
    sums = dot(weights, rest)
    for t, new in enumerate(new_refs):
        part = sums[t * per : (t + 1) * per]
        new[...] = old_refs[t][...] + part if old_refs else part


def sums_kernel(subs, lead_ref, rest_ref, near_ref, cent_ref, own_prefix_ref, *new):
    weights = soft_weights(lead_ref, near_ref, cent_ref, own_prefix_ref)
    add_lead(weights, lead_ref, (), new[:subs])
    add_rest(weights.astype(BF16), rest_ref[: weights.shape[1], :], (), new[subs:])


def sums_lead_kernel(subs, lead_ref, near_ref, cent_ref, own_prefix_ref, *refs):
    old, weights_ref, new = refs[:subs], refs[subs], refs[subs + 1 :]
    weights = soft_weights(lead_ref, near_ref, cent_ref, own_prefix_ref)
    weights_ref[...] = weights.astype(BF16)
    add_lead(weights, lead_ref, old, new)


def last_sums_kernel(subs, lead_ref, rest_ref, near_ref, cent_ref, own_prefix_ref, *refs):
    old, new, totals = refs[: 2 * subs], refs[2 * subs : 3 * subs + 1], refs[3 * subs + 1 :]
    weights = soft_weights(lead_ref, near_ref, cent_ref, own_prefix_ref)
    add_lead(weights, lead_ref, old[:subs], new[:1] + totals[: subs - 1])
    add_rest(weights.astype(BF16), rest_ref[: weights.shape[1], :], old[subs:], new[1:2] + totals[subs - 1 :])
    for t in range(subs - 1):
        lead, rest = totals[t][...], totals[subs - 1 + t][...]
        mass = lead[-SUBLANES:]
        high = mass.astype(BF16).astype(F32)
        new[2 + t][...] = jnp.concatenate([lead[:-SUBLANES], rest, high, mass - high], axis=0).astype(BF16)


def sums_rest_kernel(count, subs, *refs):
    weights_refs, rest_refs, old, new = refs[:count], refs[count : 2 * count], refs[-2 * subs : -subs], refs[-subs:]
    total = sum(dot(w[...], rest[: w.shape[1], :]) for w, rest in zip(weights_refs, rest_refs))
    per = new[0].shape[0]
    for t in range(subs):
        new[t][...] = old[t][...] + total[t * per : (t + 1) * per]


def gram_kernel(groups_of_bits, subs, *refs):
    *member_refs, gram_ref, held = refs
    z, x = lax.axis_index("rows"), lax.axis_index("sub")
    owners, groups, packed, half = held.shape
    each = len(member_refs) // subs
    for t in range(subs):
        own, *chunks = member_refs[t * each : (t + 1) * each]
        column = (x - t + subs) % subs
        held[z * subs + column] = own[...]
        for k, group in enumerate(groups_of_bits):
            for i, bits in enumerate(group):
                row = (z ^ bits) * subs + column
                held[row, :, :, :PREFIX] = chunks[2 * k][i]
                held[row, :, :, PREFIX:] = chunks[2 * k + 1][i]

    size = owners * packed
    lane = lax.broadcasted_iota(jnp.int32, (1, SUBLANES, size), 2) % SUBLANES
    same = (lane == lax.broadcasted_iota(jnp.int32, (1, SUBLANES, size), 1)).astype(F32)
    tile = min(size, 2 * LANES)
    for g in range(groups):
        mine = held[:, g].reshape(size, half)
        for start in range(0, size, tile):
            part = dot_nt(mine[start : start + tile], mine)
            part = part.reshape(tile // SUBLANES, SUBLANES, size)
            gram_ref[g, start // SUBLANES : (start + tile) // SUBLANES, :] = jnp.sum(part * same, axis=1)


def scaled_tiles(width, mine_ref, other_ref, scaled_ref):
    groups, slots, size = mine_ref.shape
    kept = scaled_ref.shape[1]
    h = lax.axis_index("dim")
    start = pl.multiple_of(h * kept, kept)
    row = lax.broadcasted_iota(jnp.int32, (slots, size), 0)
    lane = lax.broadcasted_iota(jnp.int32, (slots, size), 1)
    diagonal = row == lane // SUBLANES
    kept_row = lax.broadcasted_iota(jnp.int32, (kept, size), 0) + start
    kept_lane = lax.broadcasted_iota(jnp.int32, (kept, size), 1)
    kept_diagonal = kept_row == kept_lane // SUBLANES
    for g in range(groups):
        total = mine_ref[g] + other_ref[g]
        norms = jnp.sum(jnp.where(diagonal, total, 0.0), axis=0, keepdims=True)
        scale = lax.rsqrt(norms / width + EPS)
        spread = jnp.where(kept_diagonal, jnp.broadcast_to(scale, (kept, size)), 0.0)
        folded = spread[:, :LANES]
        for at in range(LANES, size, LANES):
            folded = folded + spread[:, at : at + LANES]
        step = SUBLANES
        while step < LANES:
            folded = folded + pltpu.roll(folded, step, 1)
            step *= 2
        row_scale = jnp.concatenate([folded] * (size // LANES), axis=1)
        own = mine_ref[g, pl.ds(start, kept), :] + other_ref[g, pl.ds(start, kept), :]
        scaled_ref[g] = own / width * row_scale * scale


def centroid_kernel(lead_ref, rest_ref, *refs):
    *sent_refs, prior_ref, new_ref = refs
    per = prior_ref.shape[0]
    lead, mass, rest = lead_ref[:per, :], lead_ref[per:, :], rest_ref[...]
    for ref in sent_refs:
        sent = ref[...].astype(F32)
        lead = lead + sent[:per]
        rest = rest + sent[per : 2 * per]
        mass = mass + sent[2 * per : 2 * per + SUBLANES] + sent[2 * per + SUBLANES :]
    mass = jnp.transpose(mass[:, :LANES])[:per, :1] + SMOOTH
    prior = SMOOTH * prior_ref[...].astype(F32)
    new_ref[:, :PREFIX] = (lead + prior[:, :PREFIX]) / mass
    new_ref[:, PREFIX:] = (rest + prior[:, PREFIX:]) / mass


def tile_kernel(width, mine_ref, other_ref, tile_ref, scaled_ref):
    scaled_tiles(width, mine_ref, other_ref, scaled_ref)
    per = tile_ref.shape[2]
    groups, kept, size = scaled_ref.shape
    slots = size // SUBLANES
    at = lax.broadcasted_iota(jnp.int32, (groups * size, per), 0)
    to = lax.broadcasted_iota(jnp.int32, (groups * size, per), 1)
    move = ((at // size == to // SUBLANES) & (at % SUBLANES == to % SUBLANES)).astype(F32).astype(BF16)
    row = lax.broadcasted_iota(jnp.int32, (slots, size), 0)
    lane = lax.broadcasted_iota(jnp.int32, (slots, size), 1)
    here = row == lane // SUBLANES
    batch = max(1, LANES // slots)

    def some(step, carry):
        spread = []
        for b in range(batch):
            i = step * batch + b
            lines = [jnp.broadcast_to(scaled_ref[g, pl.ds(i, 1), :], (slots, size)) for g in range(groups)]
            spread.append(jnp.concatenate([jnp.where(here, line, 0.0) for line in lines], axis=1))
        moved = dot(jnp.concatenate(spread, axis=0).astype(BF16), move).astype(BF16)
        for b in range(batch):
            tile_ref[step * batch + b] = moved[b * slots : (b + 1) * slots]
        return carry

    if kept == batch:
        some(0, 0)
    else:
        lax.fori_loop(0, kept // batch, some, 0)


def shards(embeddings, centroids, cluster_id, cluster_place):
    docs, half = embeddings.shape
    clusters, width = centroids.shape
    rows, subs = lax.axis_size("rows"), lax.axis_size("sub")
    owners = rows * subs
    per = clusters // owners
    groups = per // SUBLANES
    packed = MOST * SUBLANES
    slots = owners * MOST
    groups_of_bits = bits_by_count(rows)
    shape = jax.ShapeDtypeStruct

    def across(values):
        got = [values[0]]
        for t in range(1, subs):
            got.append(lax.ppermute(values[t], "sub", [(i, (i + t) % subs) for i in range(subs)]))
        return got

    def near(value):
        return lax.ppermute(value, "dim", [(0, 1), (1, 0)])

    def swap(value, bit):
        return lax.ppermute(value, "rows", [(i, i ^ bit) for i in range(rows)])

    def send(blocks, bits):
        bit = (bits & -bits or rows) // 2
        while bit:
            blocks[bits | bit] = swap(blocks[bits], bit)
            bit //= 2

    lead, rest = call(
        pack_kernel,
        "pack",
        [shape((docs + META, PREFIX), BF16), shape((docs + META, half - PREFIX), BF16)],
        [embeddings, cluster_id.reshape(1, docs)],
    )
    leads, rests = {0: lead}, {0: rest}
    send(leads, 0)

    inv, centre, own_prefix, prior, cent_prefix = call(
        functools.partial(prep_kernel, subs, per),
        "prep",
        [
            shape((subs * per, 1), F32),
            shape((subs * per, half), BF16),
            shape((subs * per, PREFIX), BF16),
            shape((per, half), BF16),
            shape((clusters, PREFIX), BF16),
        ],
        [cluster_place.reshape(1, clusters), centroids],
        cost=4 * 1024 * 1024,
    )

    lead_sum, rest_sum = shape((per + SUBLANES, PREFIX), F32), shape((per, half - PREFIX), F32)
    sum_shapes = [lead_sum] * subs + [rest_sum] * subs
    own_cost = 2 * 1024 * 1024

    prefix = near(lead)
    found = call(
        select_kernel, "select", [shape((groups, packed, half), BF16)] * subs, [lead, rest, inv, centre], cost=own_cost
    )
    members = [across(found)]
    rests[0] = tied(rest, found)
    send(rests, 0)
    sums = call(
        functools.partial(sums_kernel, subs),
        "sums",
        sum_shapes,
        [lead, rest, prefix, cent_prefix, own_prefix],
        cost=own_cost,
    )
    lead_sums, rest_sums = list(sums[:subs]), list(sums[subs:])

    for group in groups_of_bits:
        last = group == groups_of_bits[-1]
        count = len(group)
        before = members[:-1] if last else members
        leads.update(zip(group, tied([leads[bits] for bits in group], found, lead_sums, rest_sums, before)))
        for bits in group:
            send(leads, bits)
        prefixes = [near(leads[bits]) for bits in group]
        row_shapes = [shape((count, groups, packed, PREFIX), BF16)] * subs
        found = call(
            functools.partial(select_lead_kernel, count, subs),
            "select_lead",
            [shape((subs * per * MOST, docs), BF16)] * count + row_shapes,
            [inv, centre] + [leads[bits] for bits in group],
        )
        picks, found = list(found[:count]), list(found[count:])
        members.append(across(found))
        if last:
            before = (found, members[:-1])
        else:
            before = (found, members)
            weights = []
            for bits, prefix in zip(group, prefixes):
                weight, *lead_sums = call(
                    functools.partial(sums_lead_kernel, subs),
                    "sums_lead",
                    [shape((subs * per, docs), BF16)] + [lead_sum] * subs,
                    [leads[bits], prefix, cent_prefix, own_prefix] + lead_sums,
                    {4 + i: 1 + i for i in range(subs)},
                )
                weights.append(weight)
        rests.update(zip(group, tied([rests[bits] for bits in group], before)))
        for bits in group:
            send(rests, bits)
        row_shapes = [shape((count, groups, packed, half - PREFIX), BF16)] * subs
        found = call(
            functools.partial(select_rest_kernel, count, subs),
            "select_rest",
            row_shapes,
            [centre] + picks + [rests[bits] for bits in group],
        )
        members.append(across(found))
        if last:
            break
        rest_sums = call(
            functools.partial(sums_rest_kernel, count, subs),
            "sums_rest",
            [rest_sum] * subs,
            weights + [rests[bits] for bits in group] + list(rest_sums),
            {2 * count + i: i for i in range(subs)},
        )

    (bits,), (prefix,) = group, prefixes
    lead, rest, *sent = call(
        functools.partial(last_sums_kernel, subs),
        "last_sums",
        [lead_sum, rest_sum] + [shape((2 * per + 2 * SUBLANES, PREFIX), BF16)] * (subs - 1),
        [leads[bits], rests[bits], prefix, cent_prefix, own_prefix] + list(lead_sums) + list(tied(rest_sums, members[:-1])),
        {5: 0, 5 + subs: 1},
        scratch=[pltpu.VMEM(total.shape, F32) for total in [lead_sum] * (subs - 1) + [rest_sum] * (subs - 1)],
    )
    _, *sent = across([None] + sent)

    (gram,) = call(
        functools.partial(gram_kernel, groups_of_bits, subs),
        "gram",
        [shape((groups, slots, slots * SUBLANES), F32)],
        [arrays[t] for t in range(subs) for arrays in members],
        scratch=[pltpu.VMEM((owners, groups, packed, half), BF16)],
    )
    (tiles,) = call(
        functools.partial(tile_kernel, width),
        "tiles",
        [shape((slots // 2, slots, per), BF16)],
        [gram, near(gram)],
        scratch=[pltpu.VMEM((groups, slots // 2, slots * SUBLANES), F32)],
    )
    (new_centroids,) = call(centroid_kernel, "centroids", [shape((per, half), F32)], [lead, rest] + sent + [prior])
    return (new_centroids, jnp.transpose(tiles, (2, 0, 1)))


def solution(mesh):
    in_specs = (
        P(("parts", "rows", "sub"), "dim"),
        P("parts", None),
        P(("parts", "rows", "sub"), None),
        P(),
    )
    out_specs = (P(("parts", "rows", "sub"), "dim"), P(("parts", "rows", "sub"), "dim", None))
    return jax.shard_map(shards, mesh=mesh, in_specs=in_specs, out_specs=out_specs, check_vma=False)
```

```python
import functools

import jax
import jax.numpy as jnp
from jax import lax
from jax.experimental import pallas as pl
from jax.experimental.pallas import tpu as pltpu
from jax.sharding import PartitionSpec as P

PREFIX = 256
MOST = 2

TEMP = 0.125
SMOOTH = 1.0
EPS = 1e-05

DIGIT = 32
META = 16
SUBLANES = 8
LANES = 128
F32 = jnp.float32
BF16 = jnp.bfloat16
VMEM_LIMIT = 40 * 1024 * 1024

NT = (((1,), (1,)), ((), ()))


def call(kernel, name, out_shape, operands, aliases=None, scratch=(), cost=0):
    def whole(_):
        return pl.BlockSpec(memory_space=pltpu.VMEM)

    return pl.pallas_call(
        kernel,
        out_shape=tuple(out_shape),
        in_specs=[whole(operand) for operand in operands],
        out_specs=tuple(whole(out) for out in out_shape),
        input_output_aliases=aliases or {},
        scratch_shapes=list(scratch),
        compiler_params=pltpu.CompilerParams(vmem_limit_bytes=VMEM_LIMIT),
        cost_estimate=pl.CostEstimate(flops=50 * cost, bytes_accessed=cost, transcendentals=0),
        name=name,
    )(*operands)


def dot(a, b):
    return jnp.dot(a, b, preferred_element_type=F32)


def dot_nt(a, b):
    return lax.dot_general(a, b, NT, preferred_element_type=F32)


def tied(values, *others):
    leaves, tree = jax.tree.flatten(values)
    kept = lax.optimization_barrier(tuple(leaves) + tuple(jax.tree.leaves(others)))
    return jax.tree.unflatten(tree, kept[: len(leaves)])


def bits_by_count(rows):
    return [[bits for bits in range(rows) if bits.bit_count() == n] for n in range(1, (rows - 1).bit_count() + 1)]


def pack_kernel(emb_ref, cid_ref, lead_ref, rest_ref):
    docs = emb_ref.shape[0]
    lead_ref[:docs, :] = emb_ref[:, :PREFIX]
    rest_ref[:docs, :] = emb_ref[:, PREFIX:]
    rest_ref[docs:, :] = jnp.zeros((META, rest_ref.shape[1]), BF16)
    cid = cid_ref[...]
    high, low = (cid // DIGIT + 1).astype(F32), (cid % DIGIT).astype(F32)
    rows = []
    for digit in (high, low):
        rows += [digit[:, at : at + PREFIX] for at in range(0, docs, PREFIX)]
    rows.append(jnp.zeros((META - len(rows), PREFIX), F32))
    lead_ref[docs:, :] = jnp.concatenate(rows, axis=0).astype(BF16)


def ids_of(lead_ref):
    docs = lead_ref.shape[0] - META
    meta = lead_ref[docs:, :].astype(F32)
    parts = docs // PREFIX
    high = jnp.concatenate([meta[i : i + 1] for i in range(parts)], axis=1)
    low = jnp.concatenate([meta[parts + i : parts + i + 1] for i in range(parts)], axis=1)
    return (high - 1.0) * DIGIT + low


def prep_kernel(subs, per, place_ref, cent_ref, inv_ref, centre_ref, own_prefix_ref, prior_ref, prefix_ref):
    clusters = cent_ref.shape[0]
    half = centre_ref.shape[1]
    z, x, h = lax.axis_index("rows"), lax.axis_index("sub"), lax.axis_index("dim")
    row = lax.broadcasted_iota(jnp.int32, (subs * per, clusters), 0)
    ids = lax.broadcasted_iota(jnp.int32, (subs * per, clusters), 1)
    turn, within = row // per, row % per
    target = (z * subs + (x + turn) % subs) * per + within
    chosen = (place_ref[...] == target).astype(F32)
    inv_ref[...] = jnp.sum(chosen * ids.astype(F32), axis=1, keepdims=True)
    columns = cent_ref[:, pl.ds(pl.multiple_of(h * half, LANES), half)]
    centre_ref[...] = dot(chosen.astype(BF16), columns).astype(BF16)
    natural = (ids == target).astype(BF16)
    prior_ref[...] = dot(natural[:per], columns).astype(BF16)
    prefix_ref[...] = cent_ref[:, :PREFIX]
    own_prefix_ref[...] = dot(natural, prefix_ref[...]).astype(BF16)


def centred(pick, centre, columns):
    slots = pick.shape[0]
    groups = slots // (MOST * SUBLANES)
    width = columns.shape[1]
    present = jnp.sum(pick.astype(F32), axis=1, keepdims=True)
    raw = dot(pick, columns)
    middle = centre.astype(F32).reshape(groups, 1, SUBLANES, width)
    middle = jnp.broadcast_to(middle, (groups, MOST, SUBLANES, width)).reshape(slots, width)
    return jnp.where(present > 0.0, raw - middle, 0.0).astype(BF16)


def picked(lead_ref, inv_ref):
    cid = ids_of(lead_ref)
    docs = cid.shape[1]
    groups = inv_ref.shape[0] // SUBLANES
    match = (inv_ref[...] == cid).astype(F32)
    before = lax.broadcasted_iota(jnp.int32, (docs, docs), 0) < lax.broadcasted_iota(jnp.int32, (docs, docs), 1)
    earlier = dot(match.astype(BF16), before.astype(F32).astype(BF16))
    ranked = [jnp.where(earlier == r, match, 0.0).reshape(groups, SUBLANES, docs) for r in range(MOST)]
    return jnp.stack(ranked, axis=1).reshape(groups * MOST * SUBLANES, docs).astype(BF16)


def select_kernel(lead_ref, rest_ref, inv_ref, centre_ref, *row_refs):
    docs = rest_ref.shape[0] - META
    pick = picked(lead_ref, inv_ref)
    groups, packed, _ = row_refs[0].shape
    for columns, at in ((lead_ref[:docs, :], 0), (rest_ref[:docs, :], PREFIX)):
        width = columns.shape[1]
        rows = centred(pick, centre_ref[:, at : at + width], columns)
        rows = rows.reshape(len(row_refs), groups, packed, width)
        for t, ref in enumerate(row_refs):
            ref[:, :, at : at + width] = rows[t]


def select_lead_kernel(count, subs, inv_ref, centre_ref, *refs):
    lead_refs, pick_refs, row_refs = refs[:count], refs[count : 2 * count], refs[2 * count :]
    for i in range(count):
        docs = lead_refs[i].shape[0] - META
        pick = picked(lead_refs[i], inv_ref)
        pick_refs[i][...] = pick
        rows = centred(pick, centre_ref[:, :PREFIX], lead_refs[i][:docs, :])
        rows = rows.reshape((subs,) + row_refs[0].shape[1:])
        for t in range(subs):
            row_refs[t][i] = rows[t]


def select_rest_kernel(count, subs, centre_ref, *refs):
    pick_refs, rest_refs, row_refs = refs[:count], refs[count : 2 * count], refs[2 * count :]
    for i in range(count):
        pick = pick_refs[i][...]
        rows = centred(pick, centre_ref[:, PREFIX:], rest_refs[i][: pick.shape[1], :])
        rows = rows.reshape((subs,) + row_refs[0].shape[1:])
        for t in range(subs):
            row_refs[t][i] = rows[t]


def soft_weights(lead_ref, near_refs, cent_ref, own_prefix_ref):
    docs = lead_ref.shape[0] - META
    h = lax.axis_index("dim")
    near = jnp.concatenate([ref[...] for ref in near_refs], axis=0)[:docs]
    prefix = jnp.where(h == 0, lead_ref[:docs, :], near)
    scores = dot_nt(cent_ref[...], prefix) * TEMP
    top = jnp.max(scores, axis=0, keepdims=True)
    scale = 1.0 / jnp.sum(jnp.exp(scores - top), axis=0, keepdims=True)
    own = dot_nt(own_prefix_ref[...], prefix) * TEMP
    return jnp.where(ids_of(lead_ref) >= 0.0, jnp.exp(own - top) * scale, 0.0)


def add_lead(weights, lead_ref, old_refs, new_refs):
    docs = lead_ref.shape[0] - META
    per = new_refs[0].shape[0] - SUBLANES
    sums = dot(weights.astype(BF16), lead_ref[:docs, :])
    ones = jnp.ones((SUBLANES, docs), BF16)
    for t, new in enumerate(new_refs):
        here = slice(t * per, (t + 1) * per)
        mass = dot_nt(ones, weights[here].astype(BF16))
        if old_refs:
            old = old_refs[t]
            new[:per, :] = old[:per, :] + sums[here]
            new[per:, :] = old[per:, :]
            new[per:, :per] = old[per:, :per] + mass
        else:
            new[:per, :] = sums[here]
            new[per:, :] = jnp.zeros((SUBLANES, new.shape[1]), F32)
            new[per:, :per] = mass


def add_rest(weights, rest, old_refs, new_refs):
    per = new_refs[0].shape[0]
    sums = dot(weights, rest)
    for t, new in enumerate(new_refs):
        part = sums[t * per : (t + 1) * per]
        new[...] = old_refs[t][...] + part if old_refs else part


def sums_kernel(subs, lead_ref, rest_ref, near_ref, cent_ref, own_prefix_ref, *new):
    weights = soft_weights(lead_ref, [near_ref], cent_ref, own_prefix_ref)
    add_lead(weights, lead_ref, (), new[:subs])
    add_rest(weights.astype(BF16), rest_ref[: weights.shape[1], :], (), new[subs:])


def sums_lead_kernel(subs, lead_ref, near_ref, cent_ref, own_prefix_ref, *refs):
    old, weights_ref, new = refs[:subs], refs[subs], refs[subs + 1 :]
    weights = soft_weights(lead_ref, [near_ref], cent_ref, own_prefix_ref)
    weights_ref[...] = weights.astype(BF16)
    add_lead(weights, lead_ref, old, new)


def last_sums_lead_kernel(subs, lead_ref, low_ref, high_ref, cent_ref, own_prefix_ref, *refs):
    old, weights_ref, new, totals = refs[:subs], refs[subs], refs[subs + 1 : 2 * subs + 1], refs[2 * subs + 1 :]
    weights = soft_weights(lead_ref, [low_ref, high_ref], cent_ref, own_prefix_ref)
    weights_ref[...] = weights.astype(BF16)
    add_lead(weights, lead_ref, old, new[:1] + totals)
    for sent, total in zip(new[1:], totals):
        whole = total[...]
        mass = whole[-SUBLANES:]
        high = mass.astype(BF16).astype(F32)
        sent[...] = jnp.concatenate([whole[:-SUBLANES], high, mass - high], axis=0).astype(BF16)


def sums_rest_kernel(count, subs, *refs):
    weights_refs, rest_refs, old, new = refs[:count], refs[count : 2 * count], refs[-2 * subs : -subs], refs[-subs:]
    total = sum(dot(w[...], rest[: w.shape[1], :]) for w, rest in zip(weights_refs, rest_refs))
    per = old[0].shape[0]
    for t in range(subs):
        part = old[t][...] + total[t * per : (t + 1) * per]
        padding = jnp.zeros((new[t].shape[0] - per, part.shape[1]), F32)
        new[t][...] = jnp.concatenate([part, padding], axis=0).astype(new[t].dtype) if padding.shape[0] else part


def gram_kernel(groups_of_bits, subs, parts, *refs):
    member_refs, gram_refs, held = refs[: -parts - 1], refs[-parts - 1 : -1], refs[-1]
    z, x = lax.axis_index("rows"), lax.axis_index("sub")
    owners, groups, packed, half = held.shape
    each = len(member_refs) // subs
    for t in range(subs):
        own, *chunks = member_refs[t * each : (t + 1) * each]
        column = (x - t + subs) % subs
        held[z * subs + column] = own[...]
        for k, group in enumerate(groups_of_bits):
            for i, bits in enumerate(group):
                row = (z ^ bits) * subs + column
                held[row, :, :, :PREFIX] = chunks[2 * k][i]
                held[row, :, :, PREFIX:] = chunks[2 * k + 1][i]

    size = owners * packed
    lane = lax.broadcasted_iota(jnp.int32, (1, SUBLANES, size), 2) % SUBLANES
    same = (lane == lax.broadcasted_iota(jnp.int32, (1, SUBLANES, size), 1)).astype(F32)
    tile = min(size, 2 * LANES)
    for g in range(groups):
        mine = held[:, g].reshape(size, half)
        for start in range(0, size, tile):
            part = dot_nt(mine[start : start + tile], mine)
            part = part.reshape(tile // SUBLANES, SUBLANES, size)
            at = slice(start // SUBLANES, (start + tile) // SUBLANES)
            gram_refs[g * parts // groups][g % (groups // parts), at, :] = jnp.sum(part * same, axis=1)


def scaled_tiles(width, mine_refs, other_refs, scaled_ref):
    groups, kept, size = scaled_ref.shape
    slots = mine_refs[0].shape[1]
    each = groups // len(mine_refs)
    h = lax.axis_index("dim")
    start = pl.multiple_of(h * kept, kept)
    row = lax.broadcasted_iota(jnp.int32, (slots, size), 0)
    lane = lax.broadcasted_iota(jnp.int32, (slots, size), 1)
    diagonal = row == lane // SUBLANES
    kept_row = lax.broadcasted_iota(jnp.int32, (kept, size), 0) + start
    kept_lane = lax.broadcasted_iota(jnp.int32, (kept, size), 1)
    kept_diagonal = kept_row == kept_lane // SUBLANES
    for g in range(groups):
        mine_ref, other_ref, at = mine_refs[g // each], other_refs[g // each], g % each
        total = mine_ref[at] + other_ref[at]
        norms = jnp.sum(jnp.where(diagonal, total, 0.0), axis=0, keepdims=True)
        scale = lax.rsqrt(norms / width + EPS)
        spread = jnp.where(kept_diagonal, jnp.broadcast_to(scale, (kept, size)), 0.0)
        folded = spread[:, :LANES]
        for lanes in range(LANES, size, LANES):
            folded = folded + spread[:, lanes : lanes + LANES]
        step = SUBLANES
        while step < LANES:
            folded = folded + pltpu.roll(folded, step, 1)
            step *= 2
        row_scale = jnp.concatenate([folded] * (size // LANES), axis=1)
        own = mine_ref[at, pl.ds(start, kept), :] + other_ref[at, pl.ds(start, kept), :]
        scaled_ref[g] = own / width * row_scale * scale


def finish_kernel(width, subs, parts, *refs):
    mine_refs, other_refs, refs = refs[:parts], refs[parts : 2 * parts], refs[2 * parts :]
    lead_refs, rest_refs = refs[:subs], refs[subs : 2 * subs]
    prior_ref, new_ref, tile_ref, scaled_ref = refs[2 * subs :]
    per = prior_ref.shape[0]
    lead, mass = lead_refs[0][:per, :], lead_refs[0][per:, :]
    for ref in lead_refs[1:]:
        sent = ref[...].astype(F32)
        lead = lead + sent[:per]
        mass = mass + sent[per : per + SUBLANES] + sent[per + SUBLANES :]
    rest = rest_refs[0][...]
    for ref in rest_refs[1:]:
        rest = rest + ref[...].astype(F32)[:per]
    mass = jnp.transpose(mass[:, :LANES])[:per, :1] + SMOOTH
    prior = SMOOTH * prior_ref[...].astype(F32)
    new_ref[:, :PREFIX] = (lead + prior[:, :PREFIX]) / mass
    new_ref[:, PREFIX:] = (rest + prior[:, PREFIX:]) / mass

    scaled_tiles(width, mine_refs, other_refs, scaled_ref)
    groups, kept, size = scaled_ref.shape
    slots = size // SUBLANES
    at = lax.broadcasted_iota(jnp.int32, (groups * size, per), 0)
    to = lax.broadcasted_iota(jnp.int32, (groups * size, per), 1)
    move = ((at // size == to // SUBLANES) & (at % SUBLANES == to % SUBLANES)).astype(F32).astype(BF16)
    row = lax.broadcasted_iota(jnp.int32, (slots, size), 0)
    lane = lax.broadcasted_iota(jnp.int32, (slots, size), 1)
    here = row == lane // SUBLANES
    batch = max(1, LANES // slots)

    def some(step, carry):
        spread = []
        for b in range(batch):
            i = step * batch + b
            lines = [jnp.broadcast_to(scaled_ref[g, pl.ds(i, 1), :], (slots, size)) for g in range(groups)]
            spread.append(jnp.concatenate([jnp.where(here, line, 0.0) for line in lines], axis=1))
        moved = dot(jnp.concatenate(spread, axis=0).astype(BF16), move).astype(BF16)
        for b in range(batch):
            tile_ref[step * batch + b] = moved[b * slots : (b + 1) * slots]
        return carry

    if kept == batch:
        some(0, 0)
    else:
        lax.fori_loop(0, kept // batch, some, 0)


def shards(embeddings, centroids, cluster_id, cluster_place):
    docs, half = embeddings.shape
    clusters, width = centroids.shape
    rows, subs = lax.axis_size("rows"), lax.axis_size("sub")
    owners = rows * subs
    per = clusters // owners
    groups = per // SUBLANES
    packed = MOST * SUBLANES
    slots = owners * MOST
    groups_of_bits = bits_by_count(rows)
    shape = jax.ShapeDtypeStruct

    def across(values):
        got = [values[0]]
        for t in range(1, subs):
            got.append(lax.ppermute(values[t], "sub", [(i, (i + t) % subs) for i in range(subs)]))
        return got

    def near(value):
        return lax.ppermute(value, "dim", [(0, 1), (1, 0)])

    def swap(value, bit):
        return lax.ppermute(value, "rows", [(i, i ^ bit) for i in range(rows)])

    def send(blocks, bits):
        bit = (bits & -bits or rows) // 2
        while bit:
            blocks[bits | bit] = swap(blocks[bits], bit)
            bit //= 2

    lead, rest = call(
        pack_kernel,
        "pack",
        [shape((docs + META, PREFIX), BF16), shape((docs + META, half - PREFIX), BF16)],
        [embeddings, cluster_id.reshape(1, docs)],
    )
    leads, rests = {0: lead}, {0: rest}
    send(leads, 0)

    inv, centre, own_prefix, prior, cent_prefix = call(
        functools.partial(prep_kernel, subs, per),
        "prep",
        [
            shape((subs * per, 1), F32),
            shape((subs * per, half), BF16),
            shape((subs * per, PREFIX), BF16),
            shape((per, half), BF16),
            shape((clusters, PREFIX), BF16),
        ],
        [cluster_place.reshape(1, clusters), centroids],
        cost=4 * 1024 * 1024,
    )

    lead_sum, rest_sum = shape((per + SUBLANES, PREFIX), F32), shape((per, half - PREFIX), F32)
    sent_lead, sent_rest = shape((per + 2 * SUBLANES, PREFIX), BF16), shape((per + 2 * SUBLANES, half - PREFIX), BF16)
    sum_shapes = [lead_sum] * subs + [rest_sum] * subs
    own_cost = 2 * 1024 * 1024

    prefix = near(lead)
    found = call(
        select_kernel, "select", [shape((groups, packed, half), BF16)] * subs, [lead, rest, inv, centre], cost=own_cost
    )
    members = [across(found)]
    rests[0] = tied(rest, found)
    send(rests, 0)
    sums = call(
        functools.partial(sums_kernel, subs),
        "sums",
        sum_shapes,
        [lead, rest, prefix, cent_prefix, own_prefix],
        cost=own_cost,
    )
    lead_sums, rest_sums = list(sums[:subs]), list(sums[subs:])

    for group in groups_of_bits:
        last = group == groups_of_bits[-1]
        count = len(group)
        before = members[:-1] if last else members
        leads.update(zip(group, tied([leads[bits] for bits in group], found, lead_sums, rest_sums, before)))
        for bits in group:
            send(leads, bits)
        if last:
            lead = leads[group[0]]
            halves = [near(lead[: docs // 2]), near(lead[docs // 2 : docs])]
        row_shapes = [shape((count, groups, packed, PREFIX), BF16)] * subs
        found = call(
            functools.partial(select_lead_kernel, count, subs),
            "select_lead",
            [shape((subs * per * MOST, docs), BF16)] * count + row_shapes,
            [inv, centre] + [leads[bits] for bits in group],
        )
        picks, found = list(found[:count]), list(found[count:])
        weights = []
        if last:
            found = tied(found, members)
            weight, *lead_sums = call(
                functools.partial(last_sums_lead_kernel, subs),
                "sums_lead",
                [shape((subs * per, docs), BF16), lead_sum] + [sent_lead] * (subs - 1),
                [lead] + halves + [cent_prefix, own_prefix] + lead_sums,
                {5: 1},
                scratch=[pltpu.VMEM(lead_sum.shape, F32)] * (subs - 1),
            )
            weights.append(weight)
            members.append(across(found))
            lead_sums = across(lead_sums)
            before = (found, weights)
        else:
            members.append(across(found))
            before = (found, members)
        rests.update(zip(group, tied([rests[bits] for bits in group], before)))
        for bits in group:
            send(rests, bits)
        row_shapes = [shape((count, groups, packed, half - PREFIX), BF16)] * subs
        found = call(
            functools.partial(select_rest_kernel, count, subs),
            "select_rest",
            row_shapes,
            [centre] + picks + [rests[bits] for bits in group],
        )
        members.append(across(found))
        if last:
            rest_sums = tied(rest_sums, members[:-1])
        else:
            for bits in group:
                prefix = near(tied(leads[bits], rests[bits]))
                weight, *lead_sums = call(
                    functools.partial(sums_lead_kernel, subs),
                    "sums_lead",
                    [shape((subs * per, docs), BF16)] + [lead_sum] * subs,
                    [leads[bits], prefix, cent_prefix, own_prefix] + lead_sums,
                    {4 + i: 1 + i for i in range(subs)},
                )
                weights.append(weight)
        rest_sums = call(
            functools.partial(sums_rest_kernel, count, subs),
            "sums_rest",
            [rest_sum] + [sent_rest if last else rest_sum] * (subs - 1),
            weights + [rests[bits] for bits in group] + list(rest_sums),
            {2 * count + i: i for i in range(1 if last else subs)},
        )
    members = tied(members, rest_sums)
    rest_sums = across(rest_sums)

    parts = 2 if groups % 2 == 0 else 1
    grams = call(
        functools.partial(gram_kernel, groups_of_bits, subs, parts),
        "gram",
        [shape((groups // parts, slots, slots * SUBLANES), F32)] * parts,
        [arrays[t] for t in range(subs) for arrays in members],
        scratch=[pltpu.VMEM((owners, groups, packed, half), BF16)],
    )
    new_centroids, tiles = call(
        functools.partial(finish_kernel, width, subs, parts),
        "finish",
        [shape((per, half), F32), shape((slots // 2, slots, per), BF16)],
        list(grams) + [near(gram) for gram in grams] + lead_sums + rest_sums + [prior],
        scratch=[pltpu.VMEM((groups, slots // 2, slots * SUBLANES), F32)],
    )
    return (new_centroids, jnp.transpose(tiles, (2, 0, 1)))


def solution(mesh):
    in_specs = (
        P(("parts", "rows", "sub"), "dim"),
        P("parts", None),
        P(("parts", "rows", "sub"), None),
        P(),
    )
    out_specs = (P(("parts", "rows", "sub"), "dim"), P(("parts", "rows", "sub"), "dim", None))
    return jax.shard_map(shards, mesh=mesh, in_specs=in_specs, out_specs=out_specs, check_vma=False)
```

```python
import functools

import jax
import jax.numpy as jnp
from jax import lax
from jax.experimental import pallas as pl
from jax.experimental.pallas import tpu as pltpu
from jax.sharding import PartitionSpec as P

PREFIX = 256
MOST = 2

TEMP = 0.125
SMOOTH = 1.0
EPS = 1e-05

DIGIT = 32
META = 16
SUBLANES = 8
LANES = 128
F32 = jnp.float32
BF16 = jnp.bfloat16
VMEM_LIMIT = 40 * 1024 * 1024

NT = (((1,), (1,)), ((), ()))


def call(kernel, name, out_shape, operands, aliases=None, scratch=(), cost=0):
    def whole(_):
        return pl.BlockSpec(memory_space=pltpu.VMEM)

    return pl.pallas_call(
        kernel,
        out_shape=tuple(out_shape),
        in_specs=[whole(operand) for operand in operands],
        out_specs=tuple(whole(out) for out in out_shape),
        input_output_aliases=aliases or {},
        scratch_shapes=list(scratch),
        compiler_params=pltpu.CompilerParams(vmem_limit_bytes=VMEM_LIMIT),
        cost_estimate=pl.CostEstimate(flops=50 * cost, bytes_accessed=cost, transcendentals=0),
        name=name,
    )(*operands)


def dot(a, b):
    return jnp.dot(a, b, preferred_element_type=F32)


def dot_nt(a, b):
    return lax.dot_general(a, b, NT, preferred_element_type=F32)


def tied(values, *others):
    leaves, tree = jax.tree.flatten(values)
    kept = lax.optimization_barrier(tuple(leaves) + tuple(jax.tree.leaves(others)))
    return jax.tree.unflatten(tree, kept[: len(leaves)])


def bits_by_count(rows):
    return [[bits for bits in range(rows) if bits.bit_count() == n] for n in range(1, (rows - 1).bit_count() + 1)]


def pack_kernel(emb_ref, cid_ref, lead_ref, rest_ref):
    docs = emb_ref.shape[0]
    lead_ref[:docs, :] = emb_ref[:, :PREFIX]
    rest_ref[:docs, :] = emb_ref[:, PREFIX:]
    rest_ref[docs:, :] = jnp.zeros((META, rest_ref.shape[1]), BF16)
    cid = cid_ref[...]
    high, low = (cid // DIGIT + 1).astype(F32), (cid % DIGIT).astype(F32)
    rows = []
    for digit in (high, low):
        rows += [digit[:, at : at + PREFIX] for at in range(0, docs, PREFIX)]
    rows.append(jnp.zeros((META - len(rows), PREFIX), F32))
    lead_ref[docs:, :] = jnp.concatenate(rows, axis=0).astype(BF16)


def ids_of(lead_ref):
    docs = lead_ref.shape[0] - META
    meta = lead_ref[docs:, :].astype(F32)
    parts = docs // PREFIX
    high = jnp.concatenate([meta[i : i + 1] for i in range(parts)], axis=1)
    low = jnp.concatenate([meta[parts + i : parts + i + 1] for i in range(parts)], axis=1)
    return (high - 1.0) * DIGIT + low


def prep_kernel(subs, per, place_ref, cent_ref, inv_ref, centre_ref, own_prefix_ref, prior_ref, prefix_ref):
    clusters = cent_ref.shape[0]
    half = centre_ref.shape[1]
    z, x, h = lax.axis_index("rows"), lax.axis_index("sub"), lax.axis_index("dim")
    row = lax.broadcasted_iota(jnp.int32, (subs * per, clusters), 0)
    ids = lax.broadcasted_iota(jnp.int32, (subs * per, clusters), 1)
    turn, within = row // per, row % per
    target = (z * subs + (x + turn) % subs) * per + within
    chosen = (place_ref[...] == target).astype(F32)
    inv_ref[...] = jnp.sum(chosen * ids.astype(F32), axis=1, keepdims=True)
    columns = cent_ref[:, pl.ds(pl.multiple_of(h * half, LANES), half)]
    centre_ref[...] = dot(chosen.astype(BF16), columns).astype(BF16)
    natural = (ids == target).astype(BF16)
    prior_ref[...] = dot(natural[:per], columns).astype(BF16)
    prefix_ref[...] = cent_ref[:, :PREFIX]
    own_prefix_ref[...] = dot(natural, prefix_ref[...]).astype(BF16)


def centred(pick, centre, columns):
    slots = pick.shape[0]
    groups = slots // (MOST * SUBLANES)
    width = columns.shape[1]
    present = jnp.sum(pick.astype(F32), axis=1, keepdims=True)
    raw = dot(pick, columns)
    middle = centre.astype(F32).reshape(groups, 1, SUBLANES, width)
    middle = jnp.broadcast_to(middle, (groups, MOST, SUBLANES, width)).reshape(slots, width)
    return jnp.where(present > 0.0, raw - middle, 0.0).astype(BF16)


def picked(lead_ref, inv_ref):
    cid = ids_of(lead_ref)
    docs = cid.shape[1]
    groups = inv_ref.shape[0] // SUBLANES
    match = (inv_ref[...] == cid).astype(F32)
    before = lax.broadcasted_iota(jnp.int32, (docs, docs), 0) < lax.broadcasted_iota(jnp.int32, (docs, docs), 1)
    earlier = dot(match.astype(BF16), before.astype(F32).astype(BF16))
    ranked = [jnp.where(earlier == r, match, 0.0).reshape(groups, SUBLANES, docs) for r in range(MOST)]
    return jnp.stack(ranked, axis=1).reshape(groups * MOST * SUBLANES, docs).astype(BF16)


def select_kernel(lead_ref, rest_ref, inv_ref, centre_ref, *row_refs):
    docs = rest_ref.shape[0] - META
    pick = picked(lead_ref, inv_ref)
    groups, packed, _ = row_refs[0].shape
    for columns, at in ((lead_ref[:docs, :], 0), (rest_ref[:docs, :], PREFIX)):
        width = columns.shape[1]
        rows = centred(pick, centre_ref[:, at : at + width], columns)
        rows = rows.reshape(len(row_refs), groups, packed, width)
        for t, ref in enumerate(row_refs):
            ref[:, :, at : at + width] = rows[t]


def select_lead_kernel(count, subs, inv_ref, centre_ref, *refs):
    lead_refs, pick_refs, row_refs = refs[:count], refs[count : 2 * count], refs[2 * count :]
    for i in range(count):
        docs = lead_refs[i].shape[0] - META
        pick = picked(lead_refs[i], inv_ref)
        pick_refs[i][...] = pick
        rows = centred(pick, centre_ref[:, :PREFIX], lead_refs[i][:docs, :])
        rows = rows.reshape((subs,) + row_refs[0].shape[1:])
        for t in range(subs):
            row_refs[t][i] = rows[t]


def select_rest_kernel(count, subs, centre_ref, *refs):
    pick_refs, rest_refs, row_refs = refs[:count], refs[count : 2 * count], refs[2 * count :]
    for i in range(count):
        pick = pick_refs[i][...]
        rows = centred(pick, centre_ref[:, PREFIX:], rest_refs[i][: pick.shape[1], :])
        rows = rows.reshape((subs,) + row_refs[0].shape[1:])
        for t in range(subs):
            row_refs[t][i] = rows[t]


def soft_weights(lead_ref, near_refs, cent_ref, own_prefix_ref):
    docs = lead_ref.shape[0] - META
    h = lax.axis_index("dim")
    near = jnp.concatenate([ref[...] for ref in near_refs], axis=0)[:docs]
    prefix = jnp.where(h == 0, lead_ref[:docs, :], near)
    scores = dot_nt(cent_ref[...], prefix) * TEMP
    top = jnp.max(scores, axis=0, keepdims=True)
    scale = 1.0 / jnp.sum(jnp.exp(scores - top), axis=0, keepdims=True)
    own = dot_nt(own_prefix_ref[...], prefix) * TEMP
    return jnp.where(ids_of(lead_ref) >= 0.0, jnp.exp(own - top) * scale, 0.0)


def add_lead(weights, lead_ref, old_refs, new_refs):
    docs = lead_ref.shape[0] - META
    per = new_refs[0].shape[0] - SUBLANES
    sums = dot(weights.astype(BF16), lead_ref[:docs, :])
    ones = jnp.ones((SUBLANES, docs), BF16)
    for t, new in enumerate(new_refs):
        here = slice(t * per, (t + 1) * per)
        mass = dot_nt(ones, weights[here].astype(BF16))
        if old_refs:
            old = old_refs[t]
            new[:per, :] = old[:per, :] + sums[here]
            new[per:, :] = old[per:, :]
            new[per:, :per] = old[per:, :per] + mass
        else:
            new[:per, :] = sums[here]
            new[per:, :] = jnp.zeros((SUBLANES, new.shape[1]), F32)
            new[per:, :per] = mass


def add_rest(weights, rest, old_refs, new_refs):
    per = new_refs[0].shape[0]
    sums = dot(weights, rest)
    for t, new in enumerate(new_refs):
        part = sums[t * per : (t + 1) * per]
        new[...] = old_refs[t][...] + part if old_refs else part


def sums_kernel(subs, lead_ref, rest_ref, near_ref, cent_ref, own_prefix_ref, *new):
    weights = soft_weights(lead_ref, [near_ref], cent_ref, own_prefix_ref)
    add_lead(weights, lead_ref, (), new[:subs])
    add_rest(weights.astype(BF16), rest_ref[: weights.shape[1], :], (), new[subs:])


def sums_lead_kernel(subs, lead_ref, near_ref, cent_ref, own_prefix_ref, *refs):
    old, weights_ref, new = refs[:subs], refs[subs], refs[subs + 1 :]
    weights = soft_weights(lead_ref, [near_ref], cent_ref, own_prefix_ref)
    weights_ref[...] = weights.astype(BF16)
    add_lead(weights, lead_ref, old, new)


def last_sums_lead_kernel(subs, lead_ref, low_ref, high_ref, cent_ref, own_prefix_ref, *refs):
    old, weights_ref, new, totals = refs[:subs], refs[subs], refs[subs + 1 : 2 * subs + 1], refs[2 * subs + 1 :]
    weights = soft_weights(lead_ref, [low_ref, high_ref], cent_ref, own_prefix_ref)
    weights_ref[...] = weights.astype(BF16)
    add_lead(weights, lead_ref, old, new[:1] + totals)
    for sent, total in zip(new[1:], totals):
        whole = total[...]
        mass = whole[-SUBLANES:]
        high = mass.astype(BF16).astype(F32)
        sent[...] = jnp.concatenate([whole[:-SUBLANES], high, mass - high], axis=0).astype(BF16)


def sums_rest_kernel(count, subs, *refs):
    weights_refs, rest_refs, old, new = refs[:count], refs[count : 2 * count], refs[-2 * subs : -subs], refs[-subs:]
    total = sum(dot(w[...], rest[: w.shape[1], :]) for w, rest in zip(weights_refs, rest_refs))
    per = old[0].shape[0]
    for t in range(subs):
        part = old[t][...] + total[t * per : (t + 1) * per]
        padding = jnp.zeros((new[t].shape[0] - per, part.shape[1]), F32)
        new[t][...] = jnp.concatenate([part, padding], axis=0).astype(new[t].dtype) if padding.shape[0] else part


def gram_kernel(groups_of_bits, subs, parts, *refs):
    member_refs, gram_refs, held = refs[: -parts - 1], refs[-parts - 1 : -1], refs[-1]
    z, x = lax.axis_index("rows"), lax.axis_index("sub")
    owners, groups, packed, half = held.shape
    each = len(member_refs) // subs
    for t in range(subs):
        own, *chunks = member_refs[t * each : (t + 1) * each]
        column = (x - t + subs) % subs
        held[z * subs + column] = own[...]
        for k, group in enumerate(groups_of_bits):
            for i, bits in enumerate(group):
                row = (z ^ bits) * subs + column
                held[row, :, :, :PREFIX] = chunks[2 * k][i]
                held[row, :, :, PREFIX:] = chunks[2 * k + 1][i]

    size = owners * packed
    lane = lax.broadcasted_iota(jnp.int32, (1, SUBLANES, size), 2) % SUBLANES
    same = (lane == lax.broadcasted_iota(jnp.int32, (1, SUBLANES, size), 1)).astype(F32)
    tile = min(size, 2 * LANES)
    for g in range(groups):
        mine = held[:, g].reshape(size, half)
        for start in range(0, size, tile):
            part = dot_nt(mine[start : start + tile], mine)
            part = part.reshape(tile // SUBLANES, SUBLANES, size)
            at = slice(start // SUBLANES, (start + tile) // SUBLANES)
            gram_refs[g * parts // groups][g % (groups // parts), at, :] = jnp.sum(part * same, axis=1)


def scaled_tiles(width, mine_refs, other_refs, scaled_ref):
    groups, kept, size = scaled_ref.shape
    slots = mine_refs[0].shape[1]
    each = groups // len(mine_refs)
    h = lax.axis_index("dim")
    start = pl.multiple_of(h * kept, kept)
    row = lax.broadcasted_iota(jnp.int32, (slots, size), 0)
    lane = lax.broadcasted_iota(jnp.int32, (slots, size), 1)
    diagonal = row == lane // SUBLANES
    kept_row = lax.broadcasted_iota(jnp.int32, (kept, size), 0) + start
    kept_lane = lax.broadcasted_iota(jnp.int32, (kept, size), 1)
    kept_diagonal = kept_row == kept_lane // SUBLANES
    for g in range(groups):
        mine_ref, other_ref, at = mine_refs[g // each], other_refs[g // each], g % each
        total = mine_ref[at] + other_ref[at]
        norms = jnp.sum(jnp.where(diagonal, total, 0.0), axis=0, keepdims=True)
        scale = lax.rsqrt(norms / width + EPS)
        spread = jnp.where(kept_diagonal, jnp.broadcast_to(scale, (kept, size)), 0.0)
        folded = spread[:, :LANES]
        for lanes in range(LANES, size, LANES):
            folded = folded + spread[:, lanes : lanes + LANES]
        step = SUBLANES
        while step < LANES:
            folded = folded + pltpu.roll(folded, step, 1)
            step *= 2
        row_scale = jnp.concatenate([folded] * (size // LANES), axis=1)
        own = mine_ref[at, pl.ds(start, kept), :] + other_ref[at, pl.ds(start, kept), :]
        scaled_ref[g] = own / width * row_scale * scale


def finish_kernel(width, subs, parts, *refs):
    mine_refs, other_refs, refs = refs[:parts], refs[parts : 2 * parts], refs[2 * parts :]
    lead_refs, rest_refs = refs[:subs], refs[subs : 2 * subs]
    prior_ref, new_ref, tile_ref, scaled_ref = refs[2 * subs :]
    per = prior_ref.shape[0]
    lead, mass = lead_refs[0][:per, :], lead_refs[0][per:, :]
    for ref in lead_refs[1:]:
        sent = ref[...].astype(F32)
        lead = lead + sent[:per]
        mass = mass + sent[per : per + SUBLANES] + sent[per + SUBLANES :]
    rest = rest_refs[0][...]
    for ref in rest_refs[1:]:
        rest = rest + ref[...].astype(F32)[:per]
    mass = jnp.transpose(mass[:, :LANES])[:per, :1] + SMOOTH
    prior = SMOOTH * prior_ref[...].astype(F32)
    new_ref[:, :PREFIX] = (lead + prior[:, :PREFIX]) / mass
    new_ref[:, PREFIX:] = (rest + prior[:, PREFIX:]) / mass

    scaled_tiles(width, mine_refs, other_refs, scaled_ref)
    groups, kept, size = scaled_ref.shape
    slots = size // SUBLANES
    at = lax.broadcasted_iota(jnp.int32, (groups * size, per), 0)
    to = lax.broadcasted_iota(jnp.int32, (groups * size, per), 1)
    move = ((at // size == to // SUBLANES) & (at % SUBLANES == to % SUBLANES)).astype(F32).astype(BF16)
    row = lax.broadcasted_iota(jnp.int32, (slots, size), 0)
    lane = lax.broadcasted_iota(jnp.int32, (slots, size), 1)
    here = row == lane // SUBLANES
    batch = max(1, LANES // slots)

    def some(step, carry):
        spread = []
        for b in range(batch):
            i = step * batch + b
            lines = [jnp.broadcast_to(scaled_ref[g, pl.ds(i, 1), :], (slots, size)) for g in range(groups)]
            spread.append(jnp.concatenate([jnp.where(here, line, 0.0) for line in lines], axis=1))
        moved = dot(jnp.concatenate(spread, axis=0).astype(BF16), move).astype(BF16)
        for b in range(batch):
            tile_ref[step * batch + b] = moved[b * slots : (b + 1) * slots]
        return carry

    if kept == batch:
        some(0, 0)
    else:
        lax.fori_loop(0, kept // batch, some, 0)


def shards(embeddings, centroids, cluster_id, cluster_place):
    docs, half = embeddings.shape
    clusters, width = centroids.shape
    rows, subs = lax.axis_size("rows"), lax.axis_size("sub")
    owners = rows * subs
    per = clusters // owners
    groups = per // SUBLANES
    packed = MOST * SUBLANES
    slots = owners * MOST
    groups_of_bits = bits_by_count(rows)
    shape = jax.ShapeDtypeStruct

    def across(values):
        got = [values[0]]
        for t in range(1, subs):
            got.append(lax.ppermute(values[t], "sub", [(i, (i + t) % subs) for i in range(subs)]))
        return got

    def near(value):
        return lax.ppermute(value, "dim", [(0, 1), (1, 0)])

    def swap(value, bit):
        return lax.ppermute(value, "rows", [(i, i ^ bit) for i in range(rows)])

    def send(blocks, bits, value):
        bit = (bits & -bits or rows) // 2
        while bit:
            blocks[bits | bit] = swap(value, bit)
            bit //= 2

    lead, rest = call(
        pack_kernel,
        "pack",
        [shape((docs + META, PREFIX), BF16), shape((docs + META, half - PREFIX), BF16)],
        [embeddings, cluster_id.reshape(1, docs)],
    )
    leads, rests = {0: lead}, {0: rest}
    send(leads, 0, lead)

    inv, centre, own_prefix, prior, cent_prefix = call(
        functools.partial(prep_kernel, subs, per),
        "prep",
        [
            shape((subs * per, 1), F32),
            shape((subs * per, half), BF16),
            shape((subs * per, PREFIX), BF16),
            shape((per, half), BF16),
            shape((clusters, PREFIX), BF16),
        ],
        [cluster_place.reshape(1, clusters), centroids],
        cost=4 * 1024 * 1024,
    )

    lead_sum, rest_sum = shape((per + SUBLANES, PREFIX), F32), shape((per, half - PREFIX), F32)
    sent_lead, sent_rest = shape((per + 2 * SUBLANES, PREFIX), BF16), shape((per + 2 * SUBLANES, half - PREFIX), BF16)
    sum_shapes = [lead_sum] * subs + [rest_sum] * subs
    own_cost = 2 * 1024 * 1024

    prefix = near(lead)
    found = call(
        select_kernel, "select", [shape((groups, packed, half), BF16)] * subs, [lead, rest, inv, centre], cost=own_cost
    )
    members = [across(found)]
    rests[0] = tied(rest, found)
    send(rests, 0, rests[0])
    sums = call(
        functools.partial(sums_kernel, subs),
        "sums",
        sum_shapes,
        [lead, rest, prefix, cent_prefix, own_prefix],
        cost=own_cost,
    )
    lead_sums, rest_sums = list(sums[:subs]), list(sums[subs:])

    for group in groups_of_bits:
        last = group == groups_of_bits[-1]
        count = len(group)
        before = members[:-1] if last else members
        leads.update(zip(group, tied([leads[bits] for bits in group], found, lead_sums, rest_sums, before)))
        if last:
            lead = leads[group[0]]
            halves = [near(lead[: docs // 2]), near(lead[docs // 2 : docs])]
        row_shapes = [shape((count, groups, packed, PREFIX), BF16)] * subs
        found = call(
            functools.partial(select_lead_kernel, count, subs),
            "select_lead",
            [shape((subs * per * MOST, docs), BF16)] * count + row_shapes,
            [inv, centre] + [leads[bits] for bits in group],
        )
        picks, found = list(found[:count]), list(found[count:])
        weights = []
        if last:
            found = tied(found, members)
            weight, *lead_sums = call(
                functools.partial(last_sums_lead_kernel, subs),
                "sums_lead",
                [shape((subs * per, docs), BF16), lead_sum] + [sent_lead] * (subs - 1),
                [lead] + halves + [cent_prefix, own_prefix] + lead_sums,
                {5: 1},
                scratch=[pltpu.VMEM(lead_sum.shape, F32)] * (subs - 1),
            )
            weights.append(weight)
            members.append(across(found))
            lead_sums = across(lead_sums)
            before = (found, weights)
        else:
            members.append(across(found))
            before = (found, members)
            for bits in group:
                prefix = near(leads[bits])
                weight, *lead_sums = call(
                    functools.partial(sums_lead_kernel, subs),
                    "sums_lead",
                    [shape((subs * per, docs), BF16)] + [lead_sum] * subs,
                    [leads[bits], prefix, cent_prefix, own_prefix] + lead_sums,
                    {4 + i: 1 + i for i in range(subs)},
                )
                weights.append(weight)
        rests.update(zip(group, tied([rests[bits] for bits in group], before)))
        for bits in group:
            send(leads, bits, tied(leads[bits], rests[bits]))
        row_shapes = [shape((count, groups, packed, half - PREFIX), BF16)] * subs
        found = call(
            functools.partial(select_rest_kernel, count, subs),
            "select_rest",
            row_shapes,
            [centre] + picks + [rests[bits] for bits in group],
        )
        members.append(across(found))
        for bits in group:
            rests[bits] = tied(rests[bits], found)
            send(rests, bits, rests[bits])
        if last:
            rest_sums = tied(rest_sums, members[:-1])
        rest_sums = call(
            functools.partial(sums_rest_kernel, count, subs),
            "sums_rest",
            [rest_sum] + [sent_rest if last else rest_sum] * (subs - 1),
            weights + [rests[bits] for bits in group] + list(rest_sums),
            {2 * count + i: i for i in range(1 if last else subs)},
        )
    members = tied(members, rest_sums)
    rest_sums = across(rest_sums)

    parts = 2 if groups % 2 == 0 else 1
    grams = call(
        functools.partial(gram_kernel, groups_of_bits, subs, parts),
        "gram",
        [shape((groups // parts, slots, slots * SUBLANES), F32)] * parts,
        [arrays[t] for t in range(subs) for arrays in members],
        scratch=[pltpu.VMEM((owners, groups, packed, half), BF16)],
    )
    new_centroids, tiles = call(
        functools.partial(finish_kernel, width, subs, parts),
        "finish",
        [shape((per, half), F32), shape((slots // 2, slots, per), BF16)],
        list(grams) + [near(gram) for gram in grams] + lead_sums + rest_sums + [prior],
        scratch=[pltpu.VMEM((groups, slots // 2, slots * SUBLANES), F32)],
    )
    return (new_centroids, jnp.transpose(tiles, (2, 0, 1)))


def solution(mesh):
    in_specs = (
        P(("parts", "rows", "sub"), "dim"),
        P("parts", None),
        P(("parts", "rows", "sub"), None),
        P(),
    )
    out_specs = (P(("parts", "rows", "sub"), "dim"), P(("parts", "rows", "sub"), "dim", None))
    return jax.shard_map(shards, mesh=mesh, in_specs=in_specs, out_specs=out_specs, check_vma=False)
```

```python
import functools

import jax
import jax.numpy as jnp
from jax import lax
from jax.experimental import pallas as pl
from jax.experimental.pallas import tpu as pltpu
from jax.sharding import PartitionSpec as P

PREFIX = 256
MOST = 2

TEMP = 0.125
SMOOTH = 1.0
EPS = 1e-05

DIGIT = 32
META = 16
SUBLANES = 8
LANES = 128
F32 = jnp.float32
BF16 = jnp.bfloat16
VMEM_LIMIT = 40 * 1024 * 1024

NT = (((1,), (1,)), ((), ()))


def call(kernel, name, out_shape, operands, aliases=None, scratch=(), cost=0):
    def whole(_):
        return pl.BlockSpec(memory_space=pltpu.VMEM)

    return pl.pallas_call(
        kernel,
        out_shape=tuple(out_shape),
        in_specs=[whole(operand) for operand in operands],
        out_specs=tuple(whole(out) for out in out_shape),
        input_output_aliases=aliases or {},
        scratch_shapes=list(scratch),
        compiler_params=pltpu.CompilerParams(vmem_limit_bytes=VMEM_LIMIT),
        cost_estimate=pl.CostEstimate(flops=50 * cost, bytes_accessed=cost, transcendentals=0),
        name=name,
    )(*operands)


def dot(a, b):
    return jnp.dot(a, b, preferred_element_type=F32)


def dot_nt(a, b):
    return lax.dot_general(a, b, NT, preferred_element_type=F32)


def tied(values, *others):
    leaves, tree = jax.tree.flatten(values)
    kept = lax.optimization_barrier(tuple(leaves) + tuple(jax.tree.leaves(others)))
    return jax.tree.unflatten(tree, kept[: len(leaves)])


def bits_by_count(rows):
    return [[bits for bits in range(rows) if bits.bit_count() == n] for n in range(1, (rows - 1).bit_count() + 1)]


def pack_kernel(emb_ref, cid_ref, lead_ref, rest_ref):
    docs = emb_ref.shape[0]
    lead_ref[:docs, :] = emb_ref[:, :PREFIX]
    rest_ref[:docs, :] = emb_ref[:, PREFIX:]
    rest_ref[docs:, :] = jnp.zeros((rest_ref.shape[0] - docs, rest_ref.shape[1]), BF16)
    cid = cid_ref[...]
    high, low = (cid // DIGIT + 1).astype(F32), (cid % DIGIT).astype(F32)
    rows = []
    for digit in (high, low):
        rows += [digit[:, at : at + PREFIX] for at in range(0, docs, PREFIX)]
    rows.append(jnp.zeros((META - len(rows), PREFIX), F32))
    lead_ref[docs:, :] = jnp.concatenate(rows, axis=0).astype(BF16)


def ids_of(lead_ref):
    docs = lead_ref.shape[0] - META
    meta = lead_ref[docs:, :].astype(F32)
    parts = docs // PREFIX
    high = jnp.concatenate([meta[i : i + 1] for i in range(parts)], axis=1)
    low = jnp.concatenate([meta[parts + i : parts + i + 1] for i in range(parts)], axis=1)
    return (high - 1.0) * DIGIT + low


def prep_kernel(subs, per, place_ref, cent_ref, inv_ref, centre_ref, own_prefix_ref, prior_ref, prefix_ref):
    clusters = cent_ref.shape[0]
    half = centre_ref.shape[1]
    z, x, h = lax.axis_index("rows"), lax.axis_index("sub"), lax.axis_index("dim")
    row = lax.broadcasted_iota(jnp.int32, (subs * per, clusters), 0)
    ids = lax.broadcasted_iota(jnp.int32, (subs * per, clusters), 1)
    turn, within = row // per, row % per
    target = (z * subs + (x + turn) % subs) * per + within
    chosen = (place_ref[...] == target).astype(F32)
    inv_ref[...] = jnp.sum(chosen * ids.astype(F32), axis=1, keepdims=True)
    columns = cent_ref[:, pl.ds(pl.multiple_of(h * half, LANES), half)]
    centre_ref[...] = dot(chosen.astype(BF16), columns).astype(BF16)
    natural = (ids == target).astype(BF16)
    prior_ref[...] = dot(natural[:per], columns).astype(BF16)
    prefix_ref[...] = cent_ref[:, :PREFIX]
    own_prefix_ref[...] = dot(natural, prefix_ref[...]).astype(BF16)


def centred(pick, centre, columns):
    slots = pick.shape[0]
    groups = slots // (MOST * SUBLANES)
    width = columns.shape[1]
    present = jnp.sum(pick.astype(F32), axis=1, keepdims=True)
    raw = dot(pick, columns)
    middle = centre.astype(F32).reshape(groups, 1, SUBLANES, width)
    middle = jnp.broadcast_to(middle, (groups, MOST, SUBLANES, width)).reshape(slots, width)
    return jnp.where(present > 0.0, raw - middle, 0.0).astype(BF16)


def picked(lead_ref, inv_ref):
    cid = ids_of(lead_ref)
    docs = cid.shape[1]
    groups = inv_ref.shape[0] // SUBLANES
    match = (inv_ref[...] == cid).astype(F32)
    before = lax.broadcasted_iota(jnp.int32, (docs, docs), 0) < lax.broadcasted_iota(jnp.int32, (docs, docs), 1)
    earlier = dot(match.astype(BF16), before.astype(F32).astype(BF16))
    ranked = [jnp.where(earlier == r, match, 0.0).reshape(groups, SUBLANES, docs) for r in range(MOST)]
    return jnp.stack(ranked, axis=1).reshape(groups * MOST * SUBLANES, docs).astype(BF16)


def select_kernel(lead_ref, rest_ref, inv_ref, centre_ref, *row_refs):
    docs = lead_ref.shape[0] - META
    pick = picked(lead_ref, inv_ref)
    groups, packed, _ = row_refs[0].shape
    for columns, at in ((lead_ref[:docs, :], 0), (rest_ref[:docs, :], PREFIX)):
        width = columns.shape[1]
        rows = centred(pick, centre_ref[:, at : at + width], columns)
        rows = rows.reshape(len(row_refs), groups, packed, width)
        for t, ref in enumerate(row_refs):
            ref[:, :, at : at + width] = rows[t]


def select_lead_kernel(count, subs, inv_ref, centre_ref, *refs):
    lead_refs, pick_refs, row_refs = refs[:count], refs[count : 2 * count], refs[2 * count :]
    for i in range(count):
        docs = lead_refs[i].shape[0] - META
        pick = picked(lead_refs[i], inv_ref)
        pick_refs[i][...] = pick
        rows = centred(pick, centre_ref[:, :PREFIX], lead_refs[i][:docs, :])
        rows = rows.reshape((subs,) + row_refs[0].shape[1:])
        for t in range(subs):
            row_refs[t][i] = rows[t]


def select_rest_kernel(count, subs, centre_ref, *refs):
    pick_refs, rest_refs, row_refs = refs[:count], refs[count : 2 * count], refs[2 * count :]
    for i in range(count):
        pick = pick_refs[i][...]
        rows = centred(pick, centre_ref[:, PREFIX:], rest_refs[i][: pick.shape[1], :])
        rows = rows.reshape((subs,) + row_refs[0].shape[1:])
        for t in range(subs):
            row_refs[t][i] = rows[t]


def soft_weights(lead_ref, near_refs, cent_ref, own_prefix_ref):
    docs = lead_ref.shape[0] - META
    h = lax.axis_index("dim")
    near = jnp.concatenate([ref[...] for ref in near_refs], axis=0)[:docs]
    prefix = jnp.where(h == 0, lead_ref[:docs, :], near)
    scores = dot_nt(cent_ref[...], prefix) * TEMP
    top = jnp.max(scores, axis=0, keepdims=True)
    scale = 1.0 / jnp.sum(jnp.exp(scores - top), axis=0, keepdims=True)
    own = dot_nt(own_prefix_ref[...], prefix) * TEMP
    return jnp.where(ids_of(lead_ref) >= 0.0, jnp.exp(own - top) * scale, 0.0)


def add_lead(weights, lead_ref, old_refs, new_refs):
    docs = lead_ref.shape[0] - META
    per = new_refs[0].shape[0] - SUBLANES
    sums = dot(weights.astype(BF16), lead_ref[:docs, :])
    ones = jnp.ones((SUBLANES, docs), BF16)
    for t, new in enumerate(new_refs):
        here = slice(t * per, (t + 1) * per)
        mass = dot_nt(ones, weights[here].astype(BF16))
        if old_refs:
            old = old_refs[t]
            new[:per, :] = old[:per, :] + sums[here]
            new[per:, :] = old[per:, :]
            new[per:, :per] = old[per:, :per] + mass
        else:
            new[:per, :] = sums[here]
            new[per:, :] = jnp.zeros((SUBLANES, new.shape[1]), F32)
            new[per:, :per] = mass


def add_rest(weights, rest, old_refs, new_refs):
    per = new_refs[0].shape[0]
    sums = dot(weights, rest)
    for t, new in enumerate(new_refs):
        part = sums[t * per : (t + 1) * per]
        new[...] = old_refs[t][...] + part if old_refs else part


def sums_kernel(subs, lead_ref, rest_ref, near_ref, cent_ref, own_prefix_ref, *new):
    weights = soft_weights(lead_ref, [near_ref], cent_ref, own_prefix_ref)
    add_lead(weights, lead_ref, (), new[:subs])
    add_rest(weights.astype(BF16), rest_ref[: weights.shape[1], :], (), new[subs:])


def sums_lead_kernel(subs, lead_ref, near_ref, cent_ref, own_prefix_ref, *refs):
    old, weights_ref, new = refs[:subs], refs[subs], refs[subs + 1 :]
    weights = soft_weights(lead_ref, [near_ref], cent_ref, own_prefix_ref)
    weights_ref[...] = weights.astype(BF16)
    add_lead(weights, lead_ref, old, new)


def last_sums_lead_kernel(subs, lead_ref, low_ref, high_ref, cent_ref, own_prefix_ref, *refs):
    old, weights_ref, new, totals = refs[:subs], refs[subs], refs[subs + 1 : 2 * subs + 1], refs[2 * subs + 1 :]
    weights = soft_weights(lead_ref, [low_ref, high_ref], cent_ref, own_prefix_ref)
    weights_ref[...] = weights.astype(BF16)
    add_lead(weights, lead_ref, old, new[:1] + totals)
    for sent, total in zip(new[1:], totals):
        whole = total[...]
        mass = whole[-SUBLANES:]
        high = mass.astype(BF16).astype(F32)
        sent[...] = jnp.concatenate([whole[:-SUBLANES], high, mass - high], axis=0).astype(BF16)


def sums_rest_kernel(count, subs, *refs):
    weights_refs, rest_refs, old, new = refs[:count], refs[count : 2 * count], refs[-2 * subs : -subs], refs[-subs:]
    total = sum(dot(w[...], rest[: w.shape[1], :]) for w, rest in zip(weights_refs, rest_refs))
    per = old[0].shape[0]
    for t in range(subs):
        part = old[t][...] + total[t * per : (t + 1) * per]
        padding = jnp.zeros((new[t].shape[0] - per, part.shape[1]), F32)
        new[t][...] = jnp.concatenate([part, padding], axis=0).astype(new[t].dtype) if padding.shape[0] else part


def gram_kernel(groups_of_bits, subs, parts, *refs):
    member_refs, gram_refs, held = refs[: -parts - 1], refs[-parts - 1 : -1], refs[-1]
    z, x = lax.axis_index("rows"), lax.axis_index("sub")
    owners, groups, packed, half = held.shape
    each = len(member_refs) // subs
    for t in range(subs):
        own, *chunks = member_refs[t * each : (t + 1) * each]
        column = (x - t + subs) % subs
        held[z * subs + column] = own[...]
        for k, group in enumerate(groups_of_bits):
            for i, bits in enumerate(group):
                row = (z ^ bits) * subs + column
                held[row, :, :, :PREFIX] = chunks[2 * k][i]
                held[row, :, :, PREFIX:] = chunks[2 * k + 1][i]

    size = owners * packed
    lane = lax.broadcasted_iota(jnp.int32, (1, SUBLANES, size), 2) % SUBLANES
    same = (lane == lax.broadcasted_iota(jnp.int32, (1, SUBLANES, size), 1)).astype(F32)
    tile = min(size, 2 * LANES)
    for g in range(groups):
        mine = held[:, g].reshape(size, half)
        for start in range(0, size, tile):
            part = dot_nt(mine[start : start + tile], mine)
            part = part.reshape(tile // SUBLANES, SUBLANES, size)
            at = slice(start // SUBLANES, (start + tile) // SUBLANES)
            gram_refs[g * parts // groups][g % (groups // parts), at, :] = jnp.sum(part * same, axis=1)


def scaled_tiles(width, mine_refs, other_refs, scaled_ref):
    groups, kept, size = scaled_ref.shape
    slots = mine_refs[0].shape[1]
    each = groups // len(mine_refs)
    h = lax.axis_index("dim")
    start = pl.multiple_of(h * kept, kept)
    row = lax.broadcasted_iota(jnp.int32, (slots, size), 0)
    lane = lax.broadcasted_iota(jnp.int32, (slots, size), 1)
    diagonal = row == lane // SUBLANES
    kept_row = lax.broadcasted_iota(jnp.int32, (kept, size), 0) + start
    kept_lane = lax.broadcasted_iota(jnp.int32, (kept, size), 1)
    kept_diagonal = kept_row == kept_lane // SUBLANES
    for g in range(groups):
        mine_ref, other_ref, at = mine_refs[g // each], other_refs[g // each], g % each
        total = mine_ref[at] + other_ref[at]
        norms = jnp.sum(jnp.where(diagonal, total, 0.0), axis=0, keepdims=True)
        scale = lax.rsqrt(norms / width + EPS)
        spread = jnp.where(kept_diagonal, jnp.broadcast_to(scale, (kept, size)), 0.0)
        folded = spread[:, :LANES]
        for lanes in range(LANES, size, LANES):
            folded = folded + spread[:, lanes : lanes + LANES]
        step = SUBLANES
        while step < LANES:
            folded = folded + pltpu.roll(folded, step, 1)
            step *= 2
        row_scale = jnp.concatenate([folded] * (size // LANES), axis=1)
        own = mine_ref[at, pl.ds(start, kept), :] + other_ref[at, pl.ds(start, kept), :]
        scaled_ref[g] = own / width * row_scale * scale


def finish_kernel(width, subs, parts, *refs):
    mine_refs, other_refs, refs = refs[:parts], refs[parts : 2 * parts], refs[2 * parts :]
    lead_refs, rest_refs = refs[:subs], refs[subs : 2 * subs]
    prior_ref, new_ref, tile_ref, scaled_ref = refs[2 * subs :]
    per = prior_ref.shape[0]
    lead, mass = lead_refs[0][:per, :], lead_refs[0][per:, :]
    for ref in lead_refs[1:]:
        sent = ref[...].astype(F32)
        lead = lead + sent[:per]
        mass = mass + sent[per : per + SUBLANES] + sent[per + SUBLANES :]
    rest = rest_refs[0][...]
    for ref in rest_refs[1:]:
        rest = rest + ref[...].astype(F32)[:per]
    mass = jnp.transpose(mass[:, :LANES])[:per, :1] + SMOOTH
    prior = SMOOTH * prior_ref[...].astype(F32)
    new_ref[:, :PREFIX] = (lead + prior[:, :PREFIX]) / mass
    new_ref[:, PREFIX:] = (rest + prior[:, PREFIX:]) / mass

    scaled_tiles(width, mine_refs, other_refs, scaled_ref)
    groups, kept, size = scaled_ref.shape
    slots = size // SUBLANES
    at = lax.broadcasted_iota(jnp.int32, (groups * size, per), 0)
    to = lax.broadcasted_iota(jnp.int32, (groups * size, per), 1)
    move = ((at // size == to // SUBLANES) & (at % SUBLANES == to % SUBLANES)).astype(F32).astype(BF16)
    row = lax.broadcasted_iota(jnp.int32, (slots, size), 0)
    lane = lax.broadcasted_iota(jnp.int32, (slots, size), 1)
    here = row == lane // SUBLANES
    batch = max(1, LANES // slots)

    def some(step, carry):
        spread = []
        for b in range(batch):
            i = step * batch + b
            lines = [jnp.broadcast_to(scaled_ref[g, pl.ds(i, 1), :], (slots, size)) for g in range(groups)]
            spread.append(jnp.concatenate([jnp.where(here, line, 0.0) for line in lines], axis=1))
        moved = dot(jnp.concatenate(spread, axis=0).astype(BF16), move).astype(BF16)
        for b in range(batch):
            tile_ref[step * batch + b] = moved[b * slots : (b + 1) * slots]
        return carry

    if kept == batch:
        some(0, 0)
    else:
        lax.fori_loop(0, kept // batch, some, 0)


def shards(embeddings, centroids, cluster_id, cluster_place):
    docs, half = embeddings.shape
    clusters, width = centroids.shape
    rows, subs = lax.axis_size("rows"), lax.axis_size("sub")
    owners = rows * subs
    per = clusters // owners
    groups = per // SUBLANES
    packed = MOST * SUBLANES
    slots = owners * MOST
    groups_of_bits = bits_by_count(rows)
    shape = jax.ShapeDtypeStruct

    def across(values):
        got = [values[0]]
        for t in range(1, subs):
            got.append(lax.ppermute(values[t], "sub", [(i, (i + t) % subs) for i in range(subs)]))
        return got

    def near(value):
        return lax.ppermute(value, "dim", [(0, 1), (1, 0)])

    def swap(value, bit):
        return lax.ppermute(value, "rows", [(i, i ^ bit) for i in range(rows)])

    def send(blocks, bits, value):
        bit = (bits & -bits or rows) // 2
        while bit:
            blocks[bits | bit] = swap(value, bit)
            value = value[: docs + META]
            bit //= 2

    lead, rest = call(
        pack_kernel,
        "pack",
        [shape((docs + META, PREFIX), BF16), shape((docs + 2 * META, half - PREFIX), BF16)],
        [embeddings, cluster_id.reshape(1, docs)],
    )
    leads, rests = {0: lead}, {0: rest}
    send(leads, 0, lead)

    inv, centre, own_prefix, prior, cent_prefix = call(
        functools.partial(prep_kernel, subs, per),
        "prep",
        [
            shape((subs * per, 1), F32),
            shape((subs * per, half), BF16),
            shape((subs * per, PREFIX), BF16),
            shape((per, half), BF16),
            shape((clusters, PREFIX), BF16),
        ],
        [cluster_place.reshape(1, clusters), centroids],
        cost=4 * 1024 * 1024,
    )

    lead_sum, rest_sum = shape((per + SUBLANES, PREFIX), F32), shape((per, half - PREFIX), F32)
    sent_lead, sent_rest = shape((per + 2 * SUBLANES, PREFIX), BF16), shape((per + 2 * SUBLANES, half - PREFIX), BF16)
    sum_shapes = [lead_sum] * subs + [rest_sum] * subs
    own_cost = 2 * 1024 * 1024

    prefix = near(lead)
    found = call(
        select_kernel, "select", [shape((groups, packed, half), BF16)] * subs, [lead, rest, inv, centre], cost=own_cost
    )
    members = [across(found)]
    rests[0] = tied(rest, found)
    send(rests, 0, rests[0])
    sums = call(
        functools.partial(sums_kernel, subs),
        "sums",
        sum_shapes,
        [lead, rest, prefix, cent_prefix, own_prefix],
        cost=own_cost,
    )
    lead_sums, rest_sums = list(sums[:subs]), list(sums[subs:])

    for group in groups_of_bits:
        last = group == groups_of_bits[-1]
        count = len(group)
        before = members[:-1] if last else members
        leads.update(zip(group, tied([leads[bits] for bits in group], found, lead_sums, rest_sums, before)))
        if last:
            lead = leads[group[0]]
            halves = [near(lead[: docs // 2]), near(lead[docs // 2 : docs])]
        row_shapes = [shape((count, groups, packed, PREFIX), BF16)] * subs
        found = call(
            functools.partial(select_lead_kernel, count, subs),
            "select_lead",
            [shape((subs * per * MOST, docs), BF16)] * count + row_shapes,
            [inv, centre] + [leads[bits] for bits in group],
        )
        picks, found = list(found[:count]), list(found[count:])
        weights = []
        if last:
            found = tied(found, members)
            weight, *lead_sums = call(
                functools.partial(last_sums_lead_kernel, subs),
                "sums_lead",
                [shape((subs * per, docs), BF16), lead_sum] + [sent_lead] * (subs - 1),
                [lead] + halves + [cent_prefix, own_prefix] + lead_sums,
                {5: 1},
                scratch=[pltpu.VMEM(lead_sum.shape, F32)] * (subs - 1),
            )
            weights.append(weight)
            members.append(across(tied(found, weights)))
            lead_sums = across(lead_sums)
            before = (found, weights)
        else:
            members.append(across(found))
            before = (found, members)
            for bits in group:
                prefix = near(leads[bits])
                weight, *lead_sums = call(
                    functools.partial(sums_lead_kernel, subs),
                    "sums_lead",
                    [shape((subs * per, docs), BF16)] + [lead_sum] * subs,
                    [leads[bits], prefix, cent_prefix, own_prefix] + lead_sums,
                    {4 + i: 1 + i for i in range(subs)},
                )
                weights.append(weight)
        rests.update(zip(group, tied([rests[bits] for bits in group], before)))
        for bits in group:
            send(leads, bits, tied(leads[bits], rests[bits]))
        row_shapes = [shape((count, groups, packed, half - PREFIX), BF16)] * subs
        found = call(
            functools.partial(select_rest_kernel, count, subs),
            "select_rest",
            row_shapes,
            [centre] + picks + [rests[bits] for bits in group],
        )
        if last:
            found = tied(found, lead_sums)
        members.append(across(found))
        if last:
            rest_sums = tied(rest_sums, members[:-1])
        rest_sums = call(
            functools.partial(sums_rest_kernel, count, subs),
            "sums_rest",
            [rest_sum] + [sent_rest if last else rest_sum] * (subs - 1),
            weights + [rests[bits] for bits in group] + list(rest_sums),
            {2 * count + i: i for i in range(1 if last else subs)},
        )
        for bits in group:
            rests[bits] = tied(rests[bits], weights[:1])
            send(rests, bits, rests[bits])
    members = tied(members, rest_sums)
    rest_sums = across(rest_sums)

    parts = 2 if groups % 2 == 0 else 1
    grams = call(
        functools.partial(gram_kernel, groups_of_bits, subs, parts),
        "gram",
        [shape((groups // parts, slots, slots * SUBLANES), F32)] * parts,
        [arrays[t] for t in range(subs) for arrays in members],
        scratch=[pltpu.VMEM((owners, groups, packed, half), BF16)],
    )
    new_centroids, tiles = call(
        functools.partial(finish_kernel, width, subs, parts),
        "finish",
        [shape((per, half), F32), shape((slots // 2, slots, per), BF16)],
        list(grams) + [near(gram) for gram in grams] + lead_sums + rest_sums + [prior],
        scratch=[pltpu.VMEM((groups, slots // 2, slots * SUBLANES), F32)],
    )
    return (new_centroids, jnp.transpose(tiles, (2, 0, 1)))


def solution(mesh):
    in_specs = (
        P(("parts", "rows", "sub"), "dim"),
        P("parts", None),
        P(("parts", "rows", "sub"), None),
        P(),
    )
    out_specs = (P(("parts", "rows", "sub"), "dim"), P(("parts", "rows", "sub"), "dim", None))
    return jax.shard_map(shards, mesh=mesh, in_specs=in_specs, out_specs=out_specs, check_vma=False)
```

```python
import functools

import jax
import jax.numpy as jnp
from jax import lax
from jax.experimental import pallas as pl
from jax.experimental.pallas import tpu as pltpu
from jax.sharding import PartitionSpec as P

PREFIX = 256
MOST = 2

TEMP = 0.125
SMOOTH = 1.0
EPS = 1e-05

DIGIT = 32
META = 16
SUBLANES = 8
LANES = 128
F32 = jnp.float32
BF16 = jnp.bfloat16
VMEM_LIMIT = 40 * 1024 * 1024

NT = (((1,), (1,)), ((), ()))


def call(kernel, name, out_shape, operands, aliases=None, scratch=(), cost=0):
    def whole(_):
        return pl.BlockSpec(memory_space=pltpu.VMEM)

    return pl.pallas_call(
        kernel,
        out_shape=tuple(out_shape),
        in_specs=[whole(operand) for operand in operands],
        out_specs=tuple(whole(out) for out in out_shape),
        input_output_aliases=aliases or {},
        scratch_shapes=list(scratch),
        compiler_params=pltpu.CompilerParams(vmem_limit_bytes=VMEM_LIMIT),
        cost_estimate=pl.CostEstimate(flops=50 * cost, bytes_accessed=cost, transcendentals=0),
        name=name,
    )(*operands)


def dot(a, b):
    return jnp.dot(a, b, preferred_element_type=F32)


def dot_nt(a, b):
    return lax.dot_general(a, b, NT, preferred_element_type=F32)


def tied(values, *others):
    leaves, tree = jax.tree.flatten(values)
    kept = lax.optimization_barrier(tuple(leaves) + tuple(jax.tree.leaves(others)))
    return jax.tree.unflatten(tree, kept[: len(leaves)])


def bits_by_count(rows):
    return [[bits for bits in range(rows) if bits.bit_count() == n] for n in range(1, (rows - 1).bit_count() + 1)]


def pack_kernel(emb_ref, cid_ref, lead_ref, rest_ref):
    docs = emb_ref.shape[0]
    lead_ref[:docs, :] = emb_ref[:, :PREFIX]
    rest_ref[:docs, :] = emb_ref[:, PREFIX:]
    rest_ref[docs:, :] = jnp.zeros((rest_ref.shape[0] - docs, rest_ref.shape[1]), BF16)
    cid = cid_ref[...]
    high, low = (cid // DIGIT + 1).astype(F32), (cid % DIGIT).astype(F32)
    rows = []
    for digit in (high, low):
        rows += [digit[:, at : at + PREFIX] for at in range(0, docs, PREFIX)]
    rows.append(jnp.zeros((META - len(rows), PREFIX), F32))
    lead_ref[docs:, :] = jnp.concatenate(rows, axis=0).astype(BF16)


def ids_of(lead_ref):
    docs = lead_ref.shape[0] - META
    meta = lead_ref[docs:, :].astype(F32)
    parts = docs // PREFIX
    high = jnp.concatenate([meta[i : i + 1] for i in range(parts)], axis=1)
    low = jnp.concatenate([meta[parts + i : parts + i + 1] for i in range(parts)], axis=1)
    return (high - 1.0) * DIGIT + low


def prep_kernel(subs, per, place_ref, cent_ref, inv_ref, centre_ref, own_prefix_ref, prior_ref, prefix_ref):
    clusters = cent_ref.shape[0]
    half = centre_ref.shape[1]
    z, x, h = lax.axis_index("rows"), lax.axis_index("sub"), lax.axis_index("dim")
    row = lax.broadcasted_iota(jnp.int32, (subs * per, clusters), 0)
    ids = lax.broadcasted_iota(jnp.int32, (subs * per, clusters), 1)
    turn, within = row // per, row % per
    target = (z * subs + (x + turn) % subs) * per + within
    chosen = (place_ref[...] == target).astype(F32)
    inv_ref[...] = jnp.sum(chosen * ids.astype(F32), axis=1, keepdims=True)
    columns = cent_ref[:, pl.ds(pl.multiple_of(h * half, LANES), half)]
    centre_ref[...] = dot(chosen.astype(BF16), columns).astype(BF16)
    natural = (ids == target).astype(BF16)
    prior_ref[...] = dot(natural[:per], columns).astype(BF16)
    prefix_ref[...] = cent_ref[:, :PREFIX]
    own_prefix_ref[...] = dot(natural, prefix_ref[...]).astype(BF16)


def centred(pick, centre, columns):
    slots = pick.shape[0]
    groups = slots // (MOST * SUBLANES)
    width = columns.shape[1]
    present = jnp.sum(pick.astype(F32), axis=1, keepdims=True)
    raw = dot(pick, columns)
    middle = centre.astype(F32).reshape(groups, 1, SUBLANES, width)
    middle = jnp.broadcast_to(middle, (groups, MOST, SUBLANES, width)).reshape(slots, width)
    return jnp.where(present > 0.0, raw - middle, 0.0).astype(BF16)


def picked(lead_ref, inv_ref):
    cid = ids_of(lead_ref)
    docs = cid.shape[1]
    groups = inv_ref.shape[0] // SUBLANES
    match = (inv_ref[...] == cid).astype(F32)
    before = lax.broadcasted_iota(jnp.int32, (docs, docs), 0) < lax.broadcasted_iota(jnp.int32, (docs, docs), 1)
    earlier = dot(match.astype(BF16), before.astype(F32).astype(BF16))
    ranked = [jnp.where(earlier == r, match, 0.0).reshape(groups, SUBLANES, docs) for r in range(MOST)]
    return jnp.stack(ranked, axis=1).reshape(groups * MOST * SUBLANES, docs).astype(BF16)


def select_kernel(lead_ref, rest_ref, inv_ref, centre_ref, *row_refs):
    docs = lead_ref.shape[0] - META
    pick = picked(lead_ref, inv_ref)
    groups, packed, _ = row_refs[0].shape
    for columns, at in ((lead_ref[:docs, :], 0), (rest_ref[:docs, :], PREFIX)):
        width = columns.shape[1]
        rows = centred(pick, centre_ref[:, at : at + width], columns)
        rows = rows.reshape(len(row_refs), groups, packed, width)
        for t, ref in enumerate(row_refs):
            ref[:, :, at : at + width] = rows[t]


def select_lead_kernel(count, subs, inv_ref, centre_ref, *refs):
    lead_refs, pick_refs, row_refs = refs[:count], refs[count : 2 * count], refs[2 * count :]
    for i in range(count):
        docs = lead_refs[i].shape[0] - META
        pick = picked(lead_refs[i], inv_ref)
        pick_refs[i][...] = pick
        rows = centred(pick, centre_ref[:, :PREFIX], lead_refs[i][:docs, :])
        rows = rows.reshape((subs,) + row_refs[0].shape[1:])
        for t in range(subs):
            row_refs[t][i] = rows[t]


def select_rest_kernel(count, subs, centre_ref, *refs):
    pick_refs, rest_refs, row_refs = refs[:count], refs[count : 2 * count], refs[2 * count :]
    for i in range(count):
        pick = pick_refs[i][...]
        rows = centred(pick, centre_ref[:, PREFIX:], rest_refs[i][: pick.shape[1], :])
        rows = rows.reshape((subs,) + row_refs[0].shape[1:])
        for t in range(subs):
            row_refs[t][i] = rows[t]


def soft_weights(lead_ref, near_refs, cent_ref, own_prefix_ref):
    docs = lead_ref.shape[0] - META
    h = lax.axis_index("dim")
    near = jnp.concatenate([ref[...] for ref in near_refs], axis=0)[:docs]
    prefix = jnp.where(h == 0, lead_ref[:docs, :], near)
    scores = dot_nt(cent_ref[...], prefix) * TEMP
    top = jnp.max(scores, axis=0, keepdims=True)
    scale = 1.0 / jnp.sum(jnp.exp(scores - top), axis=0, keepdims=True)
    own = dot_nt(own_prefix_ref[...], prefix) * TEMP
    return jnp.where(ids_of(lead_ref) >= 0.0, jnp.exp(own - top) * scale, 0.0)


def add_lead(weights, lead_ref, old_refs, new_refs):
    docs = lead_ref.shape[0] - META
    per = new_refs[0].shape[0] - SUBLANES
    sums = dot(weights.astype(BF16), lead_ref[:docs, :])
    ones = jnp.ones((SUBLANES, docs), BF16)
    for t, new in enumerate(new_refs):
        here = slice(t * per, (t + 1) * per)
        mass = dot_nt(ones, weights[here].astype(BF16))
        if old_refs:
            old = old_refs[t]
            new[:per, :] = old[:per, :] + sums[here]
            new[per:, :] = old[per:, :]
            new[per:, :per] = old[per:, :per] + mass
        else:
            new[:per, :] = sums[here]
            new[per:, :] = jnp.zeros((SUBLANES, new.shape[1]), F32)
            new[per:, :per] = mass


def add_rest(weights, rest, old_refs, new_refs):
    per = new_refs[0].shape[0]
    sums = dot(weights, rest)
    for t, new in enumerate(new_refs):
        part = sums[t * per : (t + 1) * per]
        new[...] = old_refs[t][...] + part if old_refs else part


def sums_kernel(subs, lead_ref, rest_ref, near_ref, cent_ref, own_prefix_ref, *new):
    weights = soft_weights(lead_ref, [near_ref], cent_ref, own_prefix_ref)
    add_lead(weights, lead_ref, (), new[:subs])
    add_rest(weights.astype(BF16), rest_ref[: weights.shape[1], :], (), new[subs:])


def sums_lead_kernel(subs, lead_ref, near_ref, cent_ref, own_prefix_ref, *refs):
    old, weights_ref, new = refs[:subs], refs[subs], refs[subs + 1 :]
    weights = soft_weights(lead_ref, [near_ref], cent_ref, own_prefix_ref)
    weights_ref[...] = weights.astype(BF16)
    add_lead(weights, lead_ref, old, new)


def last_sums_lead_kernel(subs, lead_ref, low_ref, high_ref, cent_ref, own_prefix_ref, *refs):
    old, weights_ref, new, totals = refs[:subs], refs[subs], refs[subs + 1 : 2 * subs + 1], refs[2 * subs + 1 :]
    weights = soft_weights(lead_ref, [low_ref, high_ref], cent_ref, own_prefix_ref)
    weights_ref[...] = weights.astype(BF16)
    add_lead(weights, lead_ref, old, new[:1] + totals)
    for sent, total in zip(new[1:], totals):
        whole = total[...]
        mass = whole[-SUBLANES:]
        high = mass.astype(BF16).astype(F32)
        sent[...] = jnp.concatenate([whole[:-SUBLANES], high, mass - high], axis=0).astype(BF16)


def sums_rest_kernel(count, subs, *refs):
    weights_refs, rest_refs, old, new = refs[:count], refs[count : 2 * count], refs[-2 * subs : -subs], refs[-subs:]
    total = sum(dot(w[...], rest[: w.shape[1], :]) for w, rest in zip(weights_refs, rest_refs))
    per = old[0].shape[0]
    for t in range(subs):
        part = old[t][...] + total[t * per : (t + 1) * per]
        padding = jnp.zeros((new[t].shape[0] - per, part.shape[1]), F32)
        new[t][...] = jnp.concatenate([part, padding], axis=0).astype(new[t].dtype) if padding.shape[0] else part


def gram_kernel(groups_of_bits, subs, parts, *refs):
    member_refs, gram_refs, held = refs[: -parts - 1], refs[-parts - 1 : -1], refs[-1]
    z, x = lax.axis_index("rows"), lax.axis_index("sub")
    owners, groups, packed, half = held.shape
    each = len(member_refs) // subs
    for t in range(subs):
        own, *chunks = member_refs[t * each : (t + 1) * each]
        column = (x - t + subs) % subs
        held[z * subs + column] = own[...]
        for k, group in enumerate(groups_of_bits):
            for i, bits in enumerate(group):
                row = (z ^ bits) * subs + column
                held[row, :, :, :PREFIX] = chunks[2 * k][i]
                held[row, :, :, PREFIX:] = chunks[2 * k + 1][i]

    size = owners * packed
    lane = lax.broadcasted_iota(jnp.int32, (1, SUBLANES, size), 2) % SUBLANES
    same = (lane == lax.broadcasted_iota(jnp.int32, (1, SUBLANES, size), 1)).astype(F32)
    tile = min(size, 2 * LANES)
    for g in range(groups):
        mine = held[:, g].reshape(size, half)
        for start in range(0, size, tile):
            part = dot_nt(mine[start : start + tile], mine)
            part = part.reshape(tile // SUBLANES, SUBLANES, size)
            at = slice(start // SUBLANES, (start + tile) // SUBLANES)
            gram_refs[g * parts // groups][g % (groups // parts), at, :] = jnp.sum(part * same, axis=1)


def scaled_tiles(width, mine_refs, other_refs, scaled_ref):
    groups, kept, size = scaled_ref.shape
    slots = mine_refs[0].shape[1]
    each = groups // len(mine_refs)
    h = lax.axis_index("dim")
    start = pl.multiple_of(h * kept, kept)
    row = lax.broadcasted_iota(jnp.int32, (slots, size), 0)
    lane = lax.broadcasted_iota(jnp.int32, (slots, size), 1)
    diagonal = row == lane // SUBLANES
    kept_row = lax.broadcasted_iota(jnp.int32, (kept, size), 0) + start
    kept_lane = lax.broadcasted_iota(jnp.int32, (kept, size), 1)
    kept_diagonal = kept_row == kept_lane // SUBLANES
    for g in range(groups):
        mine_ref, other_ref, at = mine_refs[g // each], other_refs[g // each], g % each
        total = mine_ref[at] + other_ref[at]
        norms = jnp.sum(jnp.where(diagonal, total, 0.0), axis=0, keepdims=True)
        scale = lax.rsqrt(norms / width + EPS)
        spread = jnp.where(kept_diagonal, jnp.broadcast_to(scale, (kept, size)), 0.0)
        folded = spread[:, :LANES]
        for lanes in range(LANES, size, LANES):
            folded = folded + spread[:, lanes : lanes + LANES]
        step = SUBLANES
        while step < LANES:
            folded = folded + pltpu.roll(folded, step, 1)
            step *= 2
        row_scale = jnp.concatenate([folded] * (size // LANES), axis=1)
        own = mine_ref[at, pl.ds(start, kept), :] + other_ref[at, pl.ds(start, kept), :]
        scaled_ref[g] = own / width * row_scale * scale


def finish_kernel(width, subs, parts, *refs):
    mine_refs, other_refs, refs = refs[:parts], refs[parts : 2 * parts], refs[2 * parts :]
    lead_refs, rest_refs = refs[:subs], refs[subs : 2 * subs]
    prior_ref, new_ref, tile_ref, scaled_ref = refs[2 * subs :]
    per = prior_ref.shape[0]
    lead, mass = lead_refs[0][:per, :], lead_refs[0][per:, :]
    for ref in lead_refs[1:]:
        sent = ref[...].astype(F32)
        lead = lead + sent[:per]
        mass = mass + sent[per : per + SUBLANES] + sent[per + SUBLANES :]
    rest = rest_refs[0][...]
    for ref in rest_refs[1:]:
        rest = rest + ref[...].astype(F32)[:per]
    mass = jnp.transpose(mass[:, :LANES])[:per, :1] + SMOOTH
    prior = SMOOTH * prior_ref[...].astype(F32)
    new_ref[:, :PREFIX] = (lead + prior[:, :PREFIX]) / mass
    new_ref[:, PREFIX:] = (rest + prior[:, PREFIX:]) / mass

    scaled_tiles(width, mine_refs, other_refs, scaled_ref)
    groups, kept, size = scaled_ref.shape
    slots = size // SUBLANES
    at = lax.broadcasted_iota(jnp.int32, (groups * size, per), 0)
    to = lax.broadcasted_iota(jnp.int32, (groups * size, per), 1)
    move = ((at // size == to // SUBLANES) & (at % SUBLANES == to % SUBLANES)).astype(F32).astype(BF16)
    row = lax.broadcasted_iota(jnp.int32, (slots, size), 0)
    lane = lax.broadcasted_iota(jnp.int32, (slots, size), 1)
    here = row == lane // SUBLANES
    batch = max(1, LANES // slots)

    def some(step, carry):
        spread = []
        for b in range(batch):
            i = step * batch + b
            lines = [jnp.broadcast_to(scaled_ref[g, pl.ds(i, 1), :], (slots, size)) for g in range(groups)]
            spread.append(jnp.concatenate([jnp.where(here, line, 0.0) for line in lines], axis=1))
        moved = dot(jnp.concatenate(spread, axis=0).astype(BF16), move).astype(BF16)
        for b in range(batch):
            tile_ref[step * batch + b] = moved[b * slots : (b + 1) * slots]
        return carry

    if kept == batch:
        some(0, 0)
    else:
        lax.fori_loop(0, kept // batch, some, 0)


def shards(embeddings, centroids, cluster_id, cluster_place):
    docs, half = embeddings.shape
    clusters, width = centroids.shape
    rows, subs = lax.axis_size("rows"), lax.axis_size("sub")
    owners = rows * subs
    per = clusters // owners
    groups = per // SUBLANES
    packed = MOST * SUBLANES
    slots = owners * MOST
    groups_of_bits = bits_by_count(rows)
    shape = jax.ShapeDtypeStruct

    def across(values):
        got = [values[0]]
        for t in range(1, subs):
            got.append(lax.ppermute(values[t], "sub", [(i, (i + t) % subs) for i in range(subs)]))
        return got

    def near(value):
        return lax.ppermute(value, "dim", [(0, 1), (1, 0)])

    def swap(value, bit):
        return lax.ppermute(value, "rows", [(i, i ^ bit) for i in range(rows)])

    def send(blocks, bits, value):
        bit = (bits & -bits or rows) // 2
        while bit:
            blocks[bits | bit] = swap(value, bit)
            value = value[: docs + META]
            bit //= 2

    lead, rest = call(
        pack_kernel,
        "pack",
        [shape((docs + META, PREFIX), BF16), shape((docs + 2 * META, half - PREFIX), BF16)],
        [embeddings, cluster_id.reshape(1, docs)],
    )
    leads, rests = {0: lead}, {0: rest}
    send(leads, 0, lead)

    inv, centre, own_prefix, prior, cent_prefix = call(
        functools.partial(prep_kernel, subs, per),
        "prep",
        [
            shape((subs * per, 1), F32),
            shape((subs * per, half), BF16),
            shape((subs * per, PREFIX), BF16),
            shape((per, half), BF16),
            shape((clusters, PREFIX), BF16),
        ],
        [cluster_place.reshape(1, clusters), centroids],
        cost=4 * 1024 * 1024,
    )

    lead_sum, rest_sum = shape((per + SUBLANES, PREFIX), F32), shape((per, half - PREFIX), F32)
    sent_lead, sent_rest = shape((per + 2 * SUBLANES, PREFIX), BF16), shape((per + 2 * SUBLANES, half - PREFIX), BF16)
    sum_shapes = [lead_sum] * subs + [rest_sum] * subs
    own_cost = 2 * 1024 * 1024

    prefix = near(lead)
    found = call(
        select_kernel, "select", [shape((groups, packed, half), BF16)] * subs, [lead, rest, inv, centre], cost=own_cost
    )
    members = [across(found)]
    rests[0] = tied(rest, found)
    send(rests, 0, rests[0])
    sums = call(
        functools.partial(sums_kernel, subs),
        "sums",
        sum_shapes,
        [lead, rest, prefix, cent_prefix, own_prefix],
        cost=own_cost,
    )
    lead_sums, rest_sums = list(sums[:subs]), list(sums[subs:])

    for group in groups_of_bits:
        last = group == groups_of_bits[-1]
        count = len(group)
        before = members[:-1] if last else members
        leads.update(zip(group, tied([leads[bits] for bits in group], found, lead_sums, rest_sums, before)))
        if last:
            lead = leads[group[0]]
            halves = [near(lead[: docs // 2]), near(lead[docs // 2 : docs])]
        row_shapes = [shape((count, groups, packed, PREFIX), BF16)] * subs
        found = call(
            functools.partial(select_lead_kernel, count, subs),
            "select_lead",
            [shape((subs * per * MOST, docs), BF16)] * count + row_shapes,
            [inv, centre] + [leads[bits] for bits in group],
        )
        picks, found = list(found[:count]), list(found[count:])
        weights = []
        if last:
            found = tied(found, members)
            weight, *lead_sums = call(
                functools.partial(last_sums_lead_kernel, subs),
                "sums_lead",
                [shape((subs * per, docs), BF16), lead_sum] + [sent_lead] * (subs - 1),
                [tied(lead, picks)] + halves + [cent_prefix, own_prefix] + lead_sums,
                {5: 1},
                scratch=[pltpu.VMEM(lead_sum.shape, F32)] * (subs - 1),
            )
            weights.append(weight)
            members.append(across(found))
            lead_sums = across(lead_sums)
            before = (found, weights)
        else:
            members.append(across(found))
            before = (found, members)
            for bits in group:
                prefix = near(leads[bits])
                weight, *lead_sums = call(
                    functools.partial(sums_lead_kernel, subs),
                    "sums_lead",
                    [shape((subs * per, docs), BF16)] + [lead_sum] * subs,
                    [leads[bits], prefix, cent_prefix, own_prefix] + lead_sums,
                    {4 + i: 1 + i for i in range(subs)},
                )
                weights.append(weight)
        rests.update(zip(group, tied([rests[bits] for bits in group], before)))
        for bits in group:
            send(leads, bits, tied(leads[bits], rests[bits]))
        row_shapes = [shape((count, groups, packed, half - PREFIX), BF16)] * subs
        found = call(
            functools.partial(select_rest_kernel, count, subs),
            "select_rest",
            row_shapes,
            [centre] + picks + [rests[bits] for bits in group],
        )
        if last:
            found = tied(found, lead_sums, members)
        members.append(across(found))
        if last:
            rest_sums = tied(rest_sums, members[:-1])
        rest_sums = call(
            functools.partial(sums_rest_kernel, count, subs),
            "sums_rest",
            [rest_sum] + [sent_rest if last else rest_sum] * (subs - 1),
            weights + [rests[bits] for bits in group] + list(rest_sums),
            {2 * count + i: i for i in range(1 if last else subs)},
        )
        for bits in group:
            rests[bits] = tied(rests[bits], weights[:1])
            send(rests, bits, rests[bits])
    members = tied(members, rest_sums)
    rest_sums = across(rest_sums)

    parts = 2 if groups % 2 == 0 else 1
    grams = call(
        functools.partial(gram_kernel, groups_of_bits, subs, parts),
        "gram",
        [shape((groups // parts, slots, slots * SUBLANES), F32)] * parts,
        [arrays[t] for t in range(subs) for arrays in members],
        scratch=[pltpu.VMEM((owners, groups, packed, half), BF16)],
    )
    new_centroids, tiles = call(
        functools.partial(finish_kernel, width, subs, parts),
        "finish",
        [shape((per, half), F32), shape((slots // 2, slots, per), BF16)],
        list(grams) + [near(gram) for gram in grams] + lead_sums + rest_sums + [prior],
        scratch=[pltpu.VMEM((groups, slots // 2, slots * SUBLANES), F32)],
    )
    return (new_centroids, jnp.transpose(tiles, (2, 0, 1)))


def solution(mesh):
    in_specs = (
        P(("parts", "rows", "sub"), "dim"),
        P("parts", None),
        P(("parts", "rows", "sub"), None),
        P(),
    )
    out_specs = (P(("parts", "rows", "sub"), "dim"), P(("parts", "rows", "sub"), "dim", None))
    return jax.shard_map(shards, mesh=mesh, in_specs=in_specs, out_specs=out_specs, check_vma=False)
```

```python
import functools

import jax
import jax.numpy as jnp
from jax import lax
from jax.experimental import pallas as pl
from jax.experimental.pallas import tpu as pltpu
from jax.sharding import PartitionSpec as P

PREFIX = 256
MOST = 2

TEMP = 0.125
SMOOTH = 1.0
EPS = 1e-05

DIGIT = 32
META = 16
SUBLANES = 8
LANES = 128
F32 = jnp.float32
BF16 = jnp.bfloat16
VMEM_LIMIT = 40 * 1024 * 1024

NT = (((1,), (1,)), ((), ()))


def call(kernel, name, out_shape, operands, aliases=None, scratch=(), cost=0):
    def whole(_):
        return pl.BlockSpec(memory_space=pltpu.VMEM)

    return pl.pallas_call(
        kernel,
        out_shape=tuple(out_shape),
        in_specs=[whole(operand) for operand in operands],
        out_specs=tuple(whole(out) for out in out_shape),
        input_output_aliases=aliases or {},
        scratch_shapes=list(scratch),
        compiler_params=pltpu.CompilerParams(vmem_limit_bytes=VMEM_LIMIT),
        cost_estimate=pl.CostEstimate(flops=50 * cost, bytes_accessed=cost, transcendentals=0),
        name=name,
    )(*operands)


def dot(a, b):
    return jnp.dot(a, b, preferred_element_type=F32)


def dot_nt(a, b):
    return lax.dot_general(a, b, NT, preferred_element_type=F32)


def tied(values, *others):
    leaves, tree = jax.tree.flatten(values)
    kept = lax.optimization_barrier(tuple(leaves) + tuple(jax.tree.leaves(others)))
    return jax.tree.unflatten(tree, kept[: len(leaves)])


def bits_by_count(rows):
    return [[bits for bits in range(rows) if bits.bit_count() == n] for n in range(1, (rows - 1).bit_count() + 1)]


def pack_kernel(emb_ref, cid_ref, lead_ref, rest_ref):
    docs = emb_ref.shape[0]
    lead_ref[:docs, :] = emb_ref[:, :PREFIX]
    rest_ref[:docs, :] = emb_ref[:, PREFIX:]
    rest_ref[docs:, :] = jnp.zeros((rest_ref.shape[0] - docs, rest_ref.shape[1]), BF16)
    cid = cid_ref[...]
    high, low = (cid // DIGIT + 1).astype(F32), (cid % DIGIT).astype(F32)
    rows = []
    for digit in (high, low):
        rows += [digit[:, at : at + PREFIX] for at in range(0, docs, PREFIX)]
    rows.append(jnp.zeros((META - len(rows), PREFIX), F32))
    lead_ref[docs:, :] = jnp.concatenate(rows, axis=0).astype(BF16)


def ids_of(lead_ref):
    docs = lead_ref.shape[0] - META
    meta = lead_ref[docs:, :].astype(F32)
    parts = docs // PREFIX
    high = jnp.concatenate([meta[i : i + 1] for i in range(parts)], axis=1)
    low = jnp.concatenate([meta[parts + i : parts + i + 1] for i in range(parts)], axis=1)
    return (high - 1.0) * DIGIT + low


def prep_kernel(subs, per, place_ref, cent_ref, inv_ref, centre_ref, own_prefix_ref, prior_ref, prefix_ref):
    clusters = cent_ref.shape[0]
    half = centre_ref.shape[1]
    z, x, h = lax.axis_index("rows"), lax.axis_index("sub"), lax.axis_index("dim")
    row = lax.broadcasted_iota(jnp.int32, (subs * per, clusters), 0)
    ids = lax.broadcasted_iota(jnp.int32, (subs * per, clusters), 1)
    turn, within = row // per, row % per
    target = (z * subs + (x + turn) % subs) * per + within
    chosen = (place_ref[...] == target).astype(F32)
    inv_ref[...] = jnp.sum(chosen * ids.astype(F32), axis=1, keepdims=True)
    columns = cent_ref[:, pl.ds(pl.multiple_of(h * half, LANES), half)]
    centre_ref[...] = dot(chosen.astype(BF16), columns).astype(BF16)
    natural = (ids == target).astype(BF16)
    prior_ref[...] = dot(natural[:per], columns).astype(BF16)
    prefix_ref[...] = cent_ref[:, :PREFIX]
    own_prefix_ref[...] = dot(natural, prefix_ref[...]).astype(BF16)


def centred(pick, centre, columns):
    slots = pick.shape[0]
    groups = slots // (MOST * SUBLANES)
    width = columns.shape[1]
    present = jnp.sum(pick.astype(F32), axis=1, keepdims=True)
    raw = dot(pick, columns)
    middle = centre.astype(F32).reshape(groups, 1, SUBLANES, width)
    middle = jnp.broadcast_to(middle, (groups, MOST, SUBLANES, width)).reshape(slots, width)
    return jnp.where(present > 0.0, raw - middle, 0.0).astype(BF16)


def picked(lead_ref, inv_ref):
    cid = ids_of(lead_ref)
    docs = cid.shape[1]
    groups = inv_ref.shape[0] // SUBLANES
    match = (inv_ref[...] == cid).astype(F32)
    before = lax.broadcasted_iota(jnp.int32, (docs, docs), 0) < lax.broadcasted_iota(jnp.int32, (docs, docs), 1)
    earlier = dot(match.astype(BF16), before.astype(F32).astype(BF16))
    ranked = [jnp.where(earlier == r, match, 0.0).reshape(groups, SUBLANES, docs) for r in range(MOST)]
    return jnp.stack(ranked, axis=1).reshape(groups * MOST * SUBLANES, docs).astype(BF16)


def select_kernel(lead_ref, rest_ref, inv_ref, centre_ref, *row_refs):
    docs = lead_ref.shape[0] - META
    pick = picked(lead_ref, inv_ref)
    groups, packed, _ = row_refs[0].shape
    for columns, at in ((lead_ref[:docs, :], 0), (rest_ref[:docs, :], PREFIX)):
        width = columns.shape[1]
        rows = centred(pick, centre_ref[:, at : at + width], columns)
        rows = rows.reshape(len(row_refs), groups, packed, width)
        for t, ref in enumerate(row_refs):
            ref[:, :, at : at + width] = rows[t]


def select_lead_kernel(count, subs, inv_ref, centre_ref, *refs):
    lead_refs, pick_refs, row_refs = refs[:count], refs[count : 2 * count], refs[2 * count :]
    for i in range(count):
        docs = lead_refs[i].shape[0] - META
        pick = picked(lead_refs[i], inv_ref)
        pick_refs[i][...] = pick
        rows = centred(pick, centre_ref[:, :PREFIX], lead_refs[i][:docs, :])
        rows = rows.reshape((subs,) + row_refs[0].shape[1:])
        for t in range(subs):
            row_refs[t][i] = rows[t]


def select_rest_kernel(count, subs, centre_ref, *refs):
    pick_refs, rest_refs, row_refs = refs[:count], refs[count : 2 * count], refs[2 * count :]
    for i in range(count):
        pick = pick_refs[i][...]
        rows = centred(pick, centre_ref[:, PREFIX:], rest_refs[i][: pick.shape[1], :])
        rows = rows.reshape((subs,) + row_refs[0].shape[1:])
        for t in range(subs):
            row_refs[t][i] = rows[t]


def soft_weights(lead_ref, near_refs, cent_ref, own_prefix_ref):
    docs = lead_ref.shape[0] - META
    h = lax.axis_index("dim")
    near = jnp.concatenate([ref[...] for ref in near_refs], axis=0)[:docs]
    prefix = jnp.where(h == 0, lead_ref[:docs, :], near)
    scores = dot_nt(cent_ref[...], prefix) * TEMP
    top = jnp.max(scores, axis=0, keepdims=True)
    scale = 1.0 / jnp.sum(jnp.exp(scores - top), axis=0, keepdims=True)
    own = dot_nt(own_prefix_ref[...], prefix) * TEMP
    return jnp.where(ids_of(lead_ref) >= 0.0, jnp.exp(own - top) * scale, 0.0)


def add_lead(weights, lead_ref, old_refs, new_refs):
    docs = lead_ref.shape[0] - META
    per = new_refs[0].shape[0] - SUBLANES
    sums = dot(weights.astype(BF16), lead_ref[:docs, :])
    ones = jnp.ones((SUBLANES, docs), BF16)
    for t, new in enumerate(new_refs):
        here = slice(t * per, (t + 1) * per)
        mass = dot_nt(ones, weights[here].astype(BF16))
        if old_refs:
            old = old_refs[t]
            new[:per, :] = old[:per, :] + sums[here]
            new[per:, :] = old[per:, :]
            new[per:, :per] = old[per:, :per] + mass
        else:
            new[:per, :] = sums[here]
            new[per:, :] = jnp.zeros((SUBLANES, new.shape[1]), F32)
            new[per:, :per] = mass


def add_rest(weights, rest, old_refs, new_refs):
    per = new_refs[0].shape[0]
    sums = dot(weights, rest)
    for t, new in enumerate(new_refs):
        part = sums[t * per : (t + 1) * per]
        new[...] = old_refs[t][...] + part if old_refs else part


def sums_kernel(subs, lead_ref, rest_ref, near_ref, cent_ref, own_prefix_ref, *new):
    weights = soft_weights(lead_ref, [near_ref], cent_ref, own_prefix_ref)
    add_lead(weights, lead_ref, (), new[:subs])
    add_rest(weights.astype(BF16), rest_ref[: weights.shape[1], :], (), new[subs:])


def sums_lead_kernel(subs, lead_ref, near_ref, cent_ref, own_prefix_ref, *refs):
    old, weights_ref, new = refs[:subs], refs[subs], refs[subs + 1 :]
    weights = soft_weights(lead_ref, [near_ref], cent_ref, own_prefix_ref)
    weights_ref[...] = weights.astype(BF16)
    add_lead(weights, lead_ref, old, new)


def last_lead_kernel(subs, lead_ref, low_ref, high_ref, cent_ref, own_prefix_ref, inv_ref, centre_ref, *refs):
    old, new, totals = refs[:subs], refs[subs : 2 * subs + 3], refs[2 * subs + 3 :]
    weights_ref, pick_ref, sums_ref, rows_ref, *sent_refs = new
    docs = lead_ref.shape[0] - META
    pick = picked(lead_ref, inv_ref)
    pick_ref[...] = pick
    rows = centred(pick, centre_ref[:, :PREFIX], lead_ref[:docs, :])
    slots = rows.shape[0] // subs
    rows_ref[0] = rows[:slots].reshape(rows_ref.shape[1:])
    weights = soft_weights(lead_ref, [low_ref, high_ref], cent_ref, own_prefix_ref)
    weights_ref[...] = weights.astype(BF16)
    add_lead(weights, lead_ref, old, (sums_ref,) + tuple(totals))
    for t, (sent, total) in enumerate(zip(sent_refs, totals), 1):
        whole = total[...]
        mass = whole[-SUBLANES:]
        high = mass.astype(BF16).astype(F32)
        sent[:slots, :] = rows[t * slots : (t + 1) * slots]
        sent[slots:, :] = jnp.concatenate([whole[:-SUBLANES], high, mass - high], axis=0).astype(BF16)


def sums_rest_kernel(count, subs, *refs):
    weights_refs, rest_refs, old, new = refs[:count], refs[count : 2 * count], refs[-2 * subs : -subs], refs[-subs:]
    total = sum(dot(w[...], rest[: w.shape[1], :]) for w, rest in zip(weights_refs, rest_refs))
    per = old[0].shape[0]
    for t in range(subs):
        part = old[t][...] + total[t * per : (t + 1) * per]
        padding = jnp.zeros((new[t].shape[0] - per, part.shape[1]), F32)
        new[t][...] = jnp.concatenate([part, padding], axis=0).astype(new[t].dtype) if padding.shape[0] else part


def gram_kernel(groups_of_bits, subs, parts, *refs):
    member_refs, gram_refs, held = refs[: -parts - 1], refs[-parts - 1 : -1], refs[-1]
    z, x = lax.axis_index("rows"), lax.axis_index("sub")
    owners, groups, packed, half = held.shape
    each = len(member_refs) // subs
    for t in range(subs):
        own, *chunks = member_refs[t * each : (t + 1) * each]
        column = (x - t + subs) % subs
        held[z * subs + column] = own[...]
        for k, group in enumerate(groups_of_bits):
            for i, bits in enumerate(group):
                row = (z ^ bits) * subs + column
                lead = chunks[2 * k]
                held[row, :, :, :PREFIX] = lead[i] if len(lead.shape) == 4 else lead[: groups * packed, :].reshape(
                    groups, packed, PREFIX
                )
                held[row, :, :, PREFIX:] = chunks[2 * k + 1][i]

    size = owners * packed
    lane = lax.broadcasted_iota(jnp.int32, (1, SUBLANES, size), 2) % SUBLANES
    same = (lane == lax.broadcasted_iota(jnp.int32, (1, SUBLANES, size), 1)).astype(F32)
    tile = min(size, 2 * LANES)
    for g in range(groups):
        mine = held[:, g].reshape(size, half)
        for start in range(0, size, tile):
            part = dot_nt(mine[start : start + tile], mine)
            part = part.reshape(tile // SUBLANES, SUBLANES, size)
            at = slice(start // SUBLANES, (start + tile) // SUBLANES)
            gram_refs[g * parts // groups][g % (groups // parts), at, :] = jnp.sum(part * same, axis=1)


def scaled_tiles(width, mine_refs, other_refs, scaled_ref):
    groups, kept, size = scaled_ref.shape
    slots = mine_refs[0].shape[1]
    each = groups // len(mine_refs)
    h = lax.axis_index("dim")
    start = pl.multiple_of(h * kept, kept)
    row = lax.broadcasted_iota(jnp.int32, (slots, size), 0)
    lane = lax.broadcasted_iota(jnp.int32, (slots, size), 1)
    diagonal = row == lane // SUBLANES
    kept_row = lax.broadcasted_iota(jnp.int32, (kept, size), 0) + start
    kept_lane = lax.broadcasted_iota(jnp.int32, (kept, size), 1)
    kept_diagonal = kept_row == kept_lane // SUBLANES
    for g in range(groups):
        mine_ref, other_ref, at = mine_refs[g // each], other_refs[g // each], g % each
        total = mine_ref[at] + other_ref[at]
        norms = jnp.sum(jnp.where(diagonal, total, 0.0), axis=0, keepdims=True)
        scale = lax.rsqrt(norms / width + EPS)
        spread = jnp.where(kept_diagonal, jnp.broadcast_to(scale, (kept, size)), 0.0)
        folded = spread[:, :LANES]
        for lanes in range(LANES, size, LANES):
            folded = folded + spread[:, lanes : lanes + LANES]
        step = SUBLANES
        while step < LANES:
            folded = folded + pltpu.roll(folded, step, 1)
            step *= 2
        row_scale = jnp.concatenate([folded] * (size // LANES), axis=1)
        own = mine_ref[at, pl.ds(start, kept), :] + other_ref[at, pl.ds(start, kept), :]
        scaled_ref[g] = own / width * row_scale * scale


def finish_kernel(width, subs, parts, *refs):
    mine_refs, other_refs, refs = refs[:parts], refs[parts : 2 * parts], refs[2 * parts :]
    lead_refs, rest_refs = refs[:subs], refs[subs : 2 * subs]
    prior_ref, new_ref, tile_ref, scaled_ref = refs[2 * subs :]
    per = prior_ref.shape[0]
    lead, mass = lead_refs[0][:per, :], lead_refs[0][per:, :]
    for ref in lead_refs[1:]:
        sent = ref[...].astype(F32)[-per - 2 * SUBLANES :]
        lead = lead + sent[:per]
        mass = mass + sent[per : per + SUBLANES] + sent[per + SUBLANES :]
    rest = rest_refs[0][...]
    for ref in rest_refs[1:]:
        rest = rest + ref[...].astype(F32)[:per]
    mass = jnp.transpose(mass[:, :LANES])[:per, :1] + SMOOTH
    prior = SMOOTH * prior_ref[...].astype(F32)
    new_ref[:, :PREFIX] = (lead + prior[:, :PREFIX]) / mass
    new_ref[:, PREFIX:] = (rest + prior[:, PREFIX:]) / mass

    scaled_tiles(width, mine_refs, other_refs, scaled_ref)
    groups, kept, size = scaled_ref.shape
    slots = size // SUBLANES
    at = lax.broadcasted_iota(jnp.int32, (groups * size, per), 0)
    to = lax.broadcasted_iota(jnp.int32, (groups * size, per), 1)
    move = ((at // size == to // SUBLANES) & (at % SUBLANES == to % SUBLANES)).astype(F32).astype(BF16)
    row = lax.broadcasted_iota(jnp.int32, (slots, size), 0)
    lane = lax.broadcasted_iota(jnp.int32, (slots, size), 1)
    here = row == lane // SUBLANES
    batch = max(1, LANES // slots)

    def some(step, carry):
        spread = []
        for b in range(batch):
            i = step * batch + b
            lines = [jnp.broadcast_to(scaled_ref[g, pl.ds(i, 1), :], (slots, size)) for g in range(groups)]
            spread.append(jnp.concatenate([jnp.where(here, line, 0.0) for line in lines], axis=1))
        moved = dot(jnp.concatenate(spread, axis=0).astype(BF16), move).astype(BF16)
        for b in range(batch):
            tile_ref[step * batch + b] = moved[b * slots : (b + 1) * slots]
        return carry

    if kept == batch:
        some(0, 0)
    else:
        lax.fori_loop(0, kept // batch, some, 0)


def shards(embeddings, centroids, cluster_id, cluster_place):
    docs, half = embeddings.shape
    clusters, width = centroids.shape
    rows, subs = lax.axis_size("rows"), lax.axis_size("sub")
    owners = rows * subs
    per = clusters // owners
    groups = per // SUBLANES
    packed = MOST * SUBLANES
    slots = owners * MOST
    groups_of_bits = bits_by_count(rows)
    shape = jax.ShapeDtypeStruct

    def across(values):
        got = [values[0]]
        for t in range(1, subs):
            got.append(lax.ppermute(values[t], "sub", [(i, (i + t) % subs) for i in range(subs)]))
        return got

    def near(value):
        return lax.ppermute(value, "dim", [(0, 1), (1, 0)])

    def swap(value, bit):
        return lax.ppermute(value, "rows", [(i, i ^ bit) for i in range(rows)])

    def send(blocks, bits, value):
        bit = (bits & -bits or rows) // 2
        while bit:
            blocks[bits | bit] = swap(value, bit)
            value = value[: docs + META]
            bit //= 2

    lead, rest = call(
        pack_kernel,
        "pack",
        [shape((docs + META, PREFIX), BF16), shape((docs + 2 * META, half - PREFIX), BF16)],
        [embeddings, cluster_id.reshape(1, docs)],
    )
    leads, rests = {0: lead}, {0: rest}
    send(leads, 0, lead)

    inv, centre, own_prefix, prior, cent_prefix = call(
        functools.partial(prep_kernel, subs, per),
        "prep",
        [
            shape((subs * per, 1), F32),
            shape((subs * per, half), BF16),
            shape((subs * per, PREFIX), BF16),
            shape((per, half), BF16),
            shape((clusters, PREFIX), BF16),
        ],
        [cluster_place.reshape(1, clusters), centroids],
        cost=4 * 1024 * 1024,
    )

    lead_sum, rest_sum = shape((per + SUBLANES, PREFIX), F32), shape((per, half - PREFIX), F32)
    sent_rest = shape((per + 2 * SUBLANES, half - PREFIX), BF16)
    sum_shapes = [lead_sum] * subs + [rest_sum] * subs
    own_cost = 2 * 1024 * 1024

    prefix = near(lead)
    found = call(
        select_kernel, "select", [shape((groups, packed, half), BF16)] * subs, [lead, rest, inv, centre], cost=own_cost
    )
    members = [across(found)]
    rests[0] = tied(rest, found)
    send(rests, 0, rests[0])
    sums = call(
        functools.partial(sums_kernel, subs),
        "sums",
        sum_shapes,
        [lead, rest, prefix, cent_prefix, own_prefix],
        cost=own_cost,
    )
    lead_sums, rest_sums = list(sums[:subs]), list(sums[subs:])

    for group in groups_of_bits:
        last = group == groups_of_bits[-1]
        count = len(group)
        before = members[:-1] if last else members
        leads.update(zip(group, tied([leads[bits] for bits in group], found, lead_sums, rest_sums, before)))
        if last:
            lead = leads[group[0]]
            halves = [near(lead[: docs // 2]), near(lead[docs // 2 : docs])]
        row_shape = shape((count, groups, packed, PREFIX), BF16)
        pick_shapes = [shape((subs * per * MOST, docs), BF16)] * count
        weight_shape = shape((subs * per, docs), BF16)
        if last:
            sent_lead = shape((groups * packed + per + 2 * SUBLANES, PREFIX), BF16)
            weight, pick, own_sums, *found = call(
                functools.partial(last_lead_kernel, subs),
                "last_lead",
                [weight_shape] + pick_shapes + [lead_sum, row_shape] + [sent_lead] * (subs - 1),
                [lead] + halves + [cent_prefix, own_prefix, inv, centre] + lead_sums,
                {7: 2},
                scratch=[pltpu.VMEM(lead_sum.shape, F32)] * (subs - 1),
            )
            weights, picks = [weight], [pick]
            members.append(across(tied(found, members)))
            lead_sums = [own_sums] + members[-1][1:]
            before = (found, weights)
        else:
            found = call(
                functools.partial(select_lead_kernel, count, subs),
                "select_lead",
                pick_shapes + [row_shape] * subs,
                [inv, centre] + [leads[bits] for bits in group],
            )
            picks, found = list(found[:count]), list(found[count:])
            members.append(across(found))
            before = (found, members)
            weights = []
            for bits in group:
                prefix = near(leads[bits])
                weight, *lead_sums = call(
                    functools.partial(sums_lead_kernel, subs),
                    "sums_lead",
                    [weight_shape] + [lead_sum] * subs,
                    [leads[bits], prefix, cent_prefix, own_prefix] + lead_sums,
                    {4 + i: 1 + i for i in range(subs)},
                )
                weights.append(weight)
        rests.update(zip(group, tied([rests[bits] for bits in group], before)))
        for bits in group:
            send(leads, bits, tied(leads[bits], rests[bits]))
        row_shapes = [shape((count, groups, packed, half - PREFIX), BF16)] * subs
        found = call(
            functools.partial(select_rest_kernel, count, subs),
            "select_rest",
            row_shapes,
            [centre] + picks + [rests[bits] for bits in group],
        )
        members.append(across(found))
        if last:
            rest_sums = tied(rest_sums, members[:-1])
        rest_sums = call(
            functools.partial(sums_rest_kernel, count, subs),
            "sums_rest",
            [rest_sum] + [sent_rest if last else rest_sum] * (subs - 1),
            weights + [rests[bits] for bits in group] + list(rest_sums),
            {2 * count + i: i for i in range(1 if last else subs)},
        )
        for bits in group:
            rests[bits] = tied(rests[bits], weights[:1])
            send(rests, bits, rests[bits])
    members = tied(members, rest_sums)
    rest_sums = across(rest_sums)

    parts = 2 if groups % 2 == 0 else 1
    grams = call(
        functools.partial(gram_kernel, groups_of_bits, subs, parts),
        "gram",
        [shape((groups // parts, slots, slots * SUBLANES), F32)] * parts,
        [arrays[t] for t in range(subs) for arrays in members],
        scratch=[pltpu.VMEM((owners, groups, packed, half), BF16)],
    )
    new_centroids, tiles = call(
        functools.partial(finish_kernel, width, subs, parts),
        "finish",
        [shape((per, half), F32), shape((slots // 2, slots, per), BF16)],
        list(grams) + [near(gram) for gram in grams] + lead_sums + rest_sums + [prior],
        scratch=[pltpu.VMEM((groups, slots // 2, slots * SUBLANES), F32)],
    )
    return (new_centroids, jnp.transpose(tiles, (2, 0, 1)))


def solution(mesh):
    in_specs = (
        P(("parts", "rows", "sub"), "dim"),
        P("parts", None),
        P(("parts", "rows", "sub"), None),
        P(),
    )
    out_specs = (P(("parts", "rows", "sub"), "dim"), P(("parts", "rows", "sub"), "dim", None))
    return jax.shard_map(shards, mesh=mesh, in_specs=in_specs, out_specs=out_specs, check_vma=False)
```

```python
import functools

import jax
import jax.numpy as jnp
from jax import lax
from jax.experimental import pallas as pl
from jax.experimental.pallas import tpu as pltpu
from jax.sharding import PartitionSpec as P

PREFIX = 256
MOST = 2

TEMP = 0.125
SMOOTH = 1.0
EPS = 1e-05

DIGIT = 32
META = 16
SUBLANES = 8
LANES = 128
F32 = jnp.float32
BF16 = jnp.bfloat16
VMEM_LIMIT = 40 * 1024 * 1024

NT = (((1,), (1,)), ((), ()))


def call(kernel, name, out_shape, operands, aliases=None, scratch=(), cost=0):
    def whole(_):
        return pl.BlockSpec(memory_space=pltpu.VMEM)

    return pl.pallas_call(
        kernel,
        out_shape=tuple(out_shape),
        in_specs=[whole(operand) for operand in operands],
        out_specs=tuple(whole(out) for out in out_shape),
        input_output_aliases=aliases or {},
        scratch_shapes=list(scratch),
        compiler_params=pltpu.CompilerParams(vmem_limit_bytes=VMEM_LIMIT),
        cost_estimate=pl.CostEstimate(flops=50 * cost, bytes_accessed=cost, transcendentals=0),
        name=name,
    )(*operands)


def dot(a, b):
    return jnp.dot(a, b, preferred_element_type=F32)


def dot_nt(a, b):
    return lax.dot_general(a, b, NT, preferred_element_type=F32)


def tied(values, *others):
    leaves, tree = jax.tree.flatten(values)
    kept = lax.optimization_barrier(tuple(leaves) + tuple(jax.tree.leaves(others)))
    return jax.tree.unflatten(tree, kept[: len(leaves)])


def bits_by_count(rows):
    return [[bits for bits in range(rows) if bits.bit_count() == n] for n in range(1, (rows - 1).bit_count() + 1)]


def pack_kernel(emb_ref, cid_ref, lead_ref, rest_ref):
    docs = emb_ref.shape[0]
    lead_ref[:docs, :] = emb_ref[:, :PREFIX]
    rest_ref[:docs, :] = emb_ref[:, PREFIX:]
    rest_ref[docs:, :] = jnp.zeros((META, rest_ref.shape[1]), BF16)
    cid = cid_ref[...]
    high, low = (cid // DIGIT + 1).astype(F32), (cid % DIGIT).astype(F32)
    rows = []
    for digit in (high, low):
        rows += [digit[:, at : at + PREFIX] for at in range(0, docs, PREFIX)]
    rows.append(jnp.zeros((META - len(rows), PREFIX), F32))
    lead_ref[docs:, :] = jnp.concatenate(rows, axis=0).astype(BF16)


def ids_of(lead_ref):
    docs = lead_ref.shape[0] - META
    meta = lead_ref[docs:, :].astype(F32)
    parts = docs // PREFIX
    high = jnp.concatenate([meta[i : i + 1] for i in range(parts)], axis=1)
    low = jnp.concatenate([meta[parts + i : parts + i + 1] for i in range(parts)], axis=1)
    return (high - 1.0) * DIGIT + low


def prep_kernel(subs, per, place_ref, cent_ref, inv_ref, centre_ref, own_prefix_ref, prior_ref, prefix_ref):
    clusters = cent_ref.shape[0]
    half = centre_ref.shape[1]
    z, x, h = lax.axis_index("rows"), lax.axis_index("sub"), lax.axis_index("dim")
    row = lax.broadcasted_iota(jnp.int32, (subs * per, clusters), 0)
    ids = lax.broadcasted_iota(jnp.int32, (subs * per, clusters), 1)
    turn, within = row // per, row % per
    target = (z * subs + (x + turn) % subs) * per + within
    chosen = (place_ref[...] == target).astype(F32)
    inv_ref[...] = jnp.sum(chosen * ids.astype(F32), axis=1, keepdims=True)
    columns = cent_ref[:, pl.ds(pl.multiple_of(h * half, LANES), half)]
    centre_ref[...] = dot(chosen.astype(BF16), columns).astype(BF16)
    natural = (ids == target).astype(BF16)
    prior_ref[...] = dot(natural[:per], columns).astype(BF16)
    prefix_ref[...] = cent_ref[:, :PREFIX]
    own_prefix_ref[...] = dot(natural, prefix_ref[...]).astype(BF16)


def centred(pick, centre, columns):
    slots = pick.shape[0]
    groups = slots // (MOST * SUBLANES)
    width = columns.shape[1]
    present = jnp.sum(pick.astype(F32), axis=1, keepdims=True)
    raw = dot(pick, columns)
    middle = centre.astype(F32).reshape(groups, 1, SUBLANES, width)
    middle = jnp.broadcast_to(middle, (groups, MOST, SUBLANES, width)).reshape(slots, width)
    return jnp.where(present > 0.0, raw - middle, 0.0).astype(BF16)


def picked(lead_ref, inv_ref):
    cid = ids_of(lead_ref)
    docs = cid.shape[1]
    groups = inv_ref.shape[0] // SUBLANES
    match = (inv_ref[...] == cid).astype(F32)
    before = lax.broadcasted_iota(jnp.int32, (docs, docs), 0) < lax.broadcasted_iota(jnp.int32, (docs, docs), 1)
    earlier = dot(match.astype(BF16), before.astype(F32).astype(BF16))
    ranked = [jnp.where(earlier == r, match, 0.0).reshape(groups, SUBLANES, docs) for r in range(MOST)]
    return jnp.stack(ranked, axis=1).reshape(groups * MOST * SUBLANES, docs).astype(BF16)


def select_kernel(lead_ref, rest_ref, inv_ref, centre_ref, *row_refs):
    docs = rest_ref.shape[0] - META
    pick = picked(lead_ref, inv_ref)
    groups, packed, _ = row_refs[0].shape
    for columns, at in ((lead_ref[:docs, :], 0), (rest_ref[:docs, :], PREFIX)):
        width = columns.shape[1]
        rows = centred(pick, centre_ref[:, at : at + width], columns)
        rows = rows.reshape(len(row_refs), groups, packed, width)
        for t, ref in enumerate(row_refs):
            ref[:, :, at : at + width] = rows[t]


def select_lead_kernel(count, subs, inv_ref, centre_ref, *refs):
    lead_refs, pick_refs, row_refs = refs[:count], refs[count : 2 * count], refs[2 * count :]
    for i in range(count):
        docs = lead_refs[i].shape[0] - META
        pick = picked(lead_refs[i], inv_ref)
        pick_refs[i][...] = pick
        rows = centred(pick, centre_ref[:, :PREFIX], lead_refs[i][:docs, :])
        rows = rows.reshape((subs,) + row_refs[0].shape[1:])
        for t in range(subs):
            row_refs[t][i] = rows[t]


def select_rest_kernel(count, subs, centre_ref, *refs):
    pick_refs, rest_refs, row_refs = refs[:count], refs[count : 2 * count], refs[2 * count :]
    for i in range(count):
        pick = pick_refs[i][...]
        rows = centred(pick, centre_ref[:, PREFIX:], rest_refs[i][: pick.shape[1], :])
        rows = rows.reshape((subs,) + row_refs[0].shape[1:])
        for t in range(subs):
            row_refs[t][i] = rows[t]


def soft_weights(lead_ref, near_ref, cent_ref, own_prefix_ref):
    docs = lead_ref.shape[0] - META
    h = lax.axis_index("dim")
    prefix = jnp.where(h == 0, lead_ref[:docs, :], near_ref[:docs, :])
    scores = dot_nt(cent_ref[...], prefix) * TEMP
    top = jnp.max(scores, axis=0, keepdims=True)
    scale = 1.0 / jnp.sum(jnp.exp(scores - top), axis=0, keepdims=True)
    own = dot_nt(own_prefix_ref[...], prefix) * TEMP
    return jnp.where(ids_of(lead_ref) >= 0.0, jnp.exp(own - top) * scale, 0.0)


def add_lead(weights, lead_ref, old_refs, new_refs):
    docs = lead_ref.shape[0] - META
    per = new_refs[0].shape[0] - SUBLANES
    sums = dot(weights.astype(BF16), lead_ref[:docs, :])
    ones = jnp.ones((SUBLANES, docs), BF16)
    for t, new in enumerate(new_refs):
        here = slice(t * per, (t + 1) * per)
        mass = dot_nt(ones, weights[here].astype(BF16))
        if old_refs:
            old = old_refs[t]
            new[:per, :] = old[:per, :] + sums[here]
            new[per:, :] = old[per:, :]
            new[per:, :per] = old[per:, :per] + mass
        else:
            new[:per, :] = sums[here]
            new[per:, :] = jnp.zeros((SUBLANES, new.shape[1]), F32)
            new[per:, :per] = mass


def add_rest(weights, rest, old_refs, new_refs):
    per = new_refs[0].shape[0]
    sums = dot(weights, rest)
    for t, new in enumerate(new_refs):
        part = sums[t * per : (t + 1) * per]
        new[...] = old_refs[t][...] + part if old_refs else part


def sums_kernel(subs, lead_ref, rest_ref, near_ref, cent_ref, own_prefix_ref, *new):
    weights = soft_weights(lead_ref, near_ref, cent_ref, own_prefix_ref)
    add_lead(weights, lead_ref, (), new[:subs])
    add_rest(weights.astype(BF16), rest_ref[: weights.shape[1], :], (), new[subs:])


def sums_lead_kernel(subs, lead_ref, near_ref, cent_ref, own_prefix_ref, *refs):
    old, weights_ref, new = refs[:subs], refs[subs], refs[subs + 1 :]
    weights = soft_weights(lead_ref, near_ref, cent_ref, own_prefix_ref)
    weights_ref[...] = weights.astype(BF16)
    add_lead(weights, lead_ref, old, new)


def last_sums_kernel(subs, lead_ref, rest_ref, near_ref, cent_ref, own_prefix_ref, *refs):
    old, new, totals = refs[: 2 * subs], refs[2 * subs : 3 * subs + 1], refs[3 * subs + 1 :]
    weights = soft_weights(lead_ref, near_ref, cent_ref, own_prefix_ref)
    add_lead(weights, lead_ref, old[:subs], new[:1] + totals[: subs - 1])
    add_rest(weights.astype(BF16), rest_ref[: weights.shape[1], :], old[subs:], new[1:2] + totals[subs - 1 :])
    for t in range(subs - 1):
        lead, rest = totals[t][...], totals[subs - 1 + t][...]
        mass = lead[-SUBLANES:]
        high = mass.astype(BF16).astype(F32)
        new[2 + t][...] = jnp.concatenate([lead[:-SUBLANES], rest, high, mass - high], axis=0).astype(BF16)


def sums_rest_kernel(count, subs, *refs):
    weights_refs, rest_refs, old, new = refs[:count], refs[count : 2 * count], refs[-2 * subs : -subs], refs[-subs:]
    total = sum(dot(w[...], rest[: w.shape[1], :]) for w, rest in zip(weights_refs, rest_refs))
    per = new[0].shape[0]
    for t in range(subs):
        new[t][...] = old[t][...] + total[t * per : (t + 1) * per]


def gram_kernel(groups_of_bits, subs, *refs):
    *member_refs, gram_ref, held = refs
    z, x = lax.axis_index("rows"), lax.axis_index("sub")
    owners, groups, packed, half = held.shape
    each = len(member_refs) // subs
    for t in range(subs):
        own, *chunks = member_refs[t * each : (t + 1) * each]
        column = (x - t + subs) % subs
        held[z * subs + column] = own[...]
        for k, group in enumerate(groups_of_bits):
            for i, bits in enumerate(group):
                row = (z ^ bits) * subs + column
                held[row, :, :, :PREFIX] = chunks[2 * k][i]
                held[row, :, :, PREFIX:] = chunks[2 * k + 1][i]

    size = owners * packed
    lane = lax.broadcasted_iota(jnp.int32, (1, SUBLANES, size), 2) % SUBLANES
    same = (lane == lax.broadcasted_iota(jnp.int32, (1, SUBLANES, size), 1)).astype(F32)
    tile = min(size, 2 * LANES)
    for g in range(groups):
        mine = held[:, g].reshape(size, half)
        for start in range(0, size, tile):
            part = dot_nt(mine[start : start + tile], mine)
            part = part.reshape(tile // SUBLANES, SUBLANES, size)
            gram_ref[g, start // SUBLANES : (start + tile) // SUBLANES, :] = jnp.sum(part * same, axis=1)


def scaled_tiles(width, mine_ref, other_ref, scaled_ref):
    groups, slots, size = mine_ref.shape
    kept = scaled_ref.shape[1]
    h = lax.axis_index("dim")
    start = pl.multiple_of(h * kept, kept)
    row = lax.broadcasted_iota(jnp.int32, (slots, size), 0)
    lane = lax.broadcasted_iota(jnp.int32, (slots, size), 1)
    diagonal = row == lane // SUBLANES
    kept_row = lax.broadcasted_iota(jnp.int32, (kept, size), 0) + start
    kept_lane = lax.broadcasted_iota(jnp.int32, (kept, size), 1)
    kept_diagonal = kept_row == kept_lane // SUBLANES
    for g in range(groups):
        total = mine_ref[g] + other_ref[g]
        norms = jnp.sum(jnp.where(diagonal, total, 0.0), axis=0, keepdims=True)
        scale = lax.rsqrt(norms / width + EPS)
        spread = jnp.where(kept_diagonal, jnp.broadcast_to(scale, (kept, size)), 0.0)
        folded = spread[:, :LANES]
        for at in range(LANES, size, LANES):
            folded = folded + spread[:, at : at + LANES]
        step = SUBLANES
        while step < LANES:
            folded = folded + pltpu.roll(folded, step, 1)
            step *= 2
        row_scale = jnp.concatenate([folded] * (size // LANES), axis=1)
        own = mine_ref[g, pl.ds(start, kept), :] + other_ref[g, pl.ds(start, kept), :]
        scaled_ref[g] = own / width * row_scale * scale


def centroid_kernel(lead_ref, rest_ref, *refs):
    *sent_refs, prior_ref, new_ref = refs
    per = prior_ref.shape[0]
    lead, mass, rest = lead_ref[:per, :], lead_ref[per:, :], rest_ref[...]
    for ref in sent_refs:
        sent = ref[...].astype(F32)
        lead = lead + sent[:per]
        rest = rest + sent[per : 2 * per]
        mass = mass + sent[2 * per : 2 * per + SUBLANES] + sent[2 * per + SUBLANES :]
    mass = jnp.transpose(mass[:, :LANES])[:per, :1] + SMOOTH
    prior = SMOOTH * prior_ref[...].astype(F32)
    new_ref[:, :PREFIX] = (lead + prior[:, :PREFIX]) / mass
    new_ref[:, PREFIX:] = (rest + prior[:, PREFIX:]) / mass


def tile_kernel(width, mine_ref, other_ref, tile_ref, scaled_ref):
    scaled_tiles(width, mine_ref, other_ref, scaled_ref)
    per = tile_ref.shape[2]
    groups, kept, size = scaled_ref.shape
    slots = size // SUBLANES
    at = lax.broadcasted_iota(jnp.int32, (groups * size, per), 0)
    to = lax.broadcasted_iota(jnp.int32, (groups * size, per), 1)
    move = ((at // size == to // SUBLANES) & (at % SUBLANES == to % SUBLANES)).astype(F32).astype(BF16)
    row = lax.broadcasted_iota(jnp.int32, (slots, size), 0)
    lane = lax.broadcasted_iota(jnp.int32, (slots, size), 1)
    here = row == lane // SUBLANES
    batch = max(1, LANES // slots)

    def some(step, carry):
        spread = []
        for b in range(batch):
            i = step * batch + b
            lines = [jnp.broadcast_to(scaled_ref[g, pl.ds(i, 1), :], (slots, size)) for g in range(groups)]
            spread.append(jnp.concatenate([jnp.where(here, line, 0.0) for line in lines], axis=1))
        moved = dot(jnp.concatenate(spread, axis=0).astype(BF16), move).astype(BF16)
        for b in range(batch):
            tile_ref[step * batch + b] = moved[b * slots : (b + 1) * slots]
        return carry

    if kept == batch:
        some(0, 0)
    else:
        lax.fori_loop(0, kept // batch, some, 0)


def shards(embeddings, centroids, cluster_id, cluster_place):
    docs, half = embeddings.shape
    clusters, width = centroids.shape
    rows, subs = lax.axis_size("rows"), lax.axis_size("sub")
    owners = rows * subs
    per = clusters // owners
    groups = per // SUBLANES
    packed = MOST * SUBLANES
    slots = owners * MOST
    groups_of_bits = bits_by_count(rows)
    shape = jax.ShapeDtypeStruct

    def across(values):
        got = [values[0]]
        for t in range(1, subs):
            got.append(lax.ppermute(values[t], "sub", [(i, (i + t) % subs) for i in range(subs)]))
        return got

    def near(value):
        return lax.ppermute(value, "dim", [(0, 1), (1, 0)])

    def swap(value, bit):
        return lax.ppermute(value, "rows", [(i, i ^ bit) for i in range(rows)])

    def send(blocks, bits):
        bit = (bits & -bits or rows) // 2
        while bit:
            blocks[bits | bit] = swap(blocks[bits], bit)
            bit //= 2

    lead, rest = call(
        pack_kernel,
        "pack",
        [shape((docs + META, PREFIX), BF16), shape((docs + META, half - PREFIX), BF16)],
        [embeddings, cluster_id.reshape(1, docs)],
    )
    leads, rests = {0: lead}, {0: rest}
    send(leads, 0)

    inv, centre, own_prefix, prior, cent_prefix = call(
        functools.partial(prep_kernel, subs, per),
        "prep",
        [
            shape((subs * per, 1), F32),
            shape((subs * per, half), BF16),
            shape((subs * per, PREFIX), BF16),
            shape((per, half), BF16),
            shape((clusters, PREFIX), BF16),
        ],
        [cluster_place.reshape(1, clusters), centroids],
        cost=4 * 1024 * 1024,
    )

    lead_sum, rest_sum = shape((per + SUBLANES, PREFIX), F32), shape((per, half - PREFIX), F32)
    sum_shapes = [lead_sum] * subs + [rest_sum] * subs
    own_cost = 2 * 1024 * 1024

    prefix = near(lead)
    found = call(
        select_kernel, "select", [shape((groups, packed, half), BF16)] * subs, [lead, rest, inv, centre], cost=own_cost
    )
    members = [across(found)]
    rests[0] = tied(rest, found)
    send(rests, 0)
    sums = call(
        functools.partial(sums_kernel, subs),
        "sums",
        sum_shapes,
        [lead, rest, prefix, cent_prefix, own_prefix],
        cost=own_cost,
    )
    lead_sums, rest_sums = list(sums[:subs]), list(sums[subs:])

    for group in groups_of_bits:
        last = group == groups_of_bits[-1]
        count = len(group)
        before = members[:-1] if last else members
        leads.update(zip(group, tied([leads[bits] for bits in group], found, lead_sums, rest_sums, before)))
        for bits in group:
            send(leads, bits)
        prefixes = [near(leads[bits]) for bits in group]
        row_shapes = [shape((count, groups, packed, PREFIX), BF16)] * subs
        found = call(
            functools.partial(select_lead_kernel, count, subs),
            "select_lead",
            [shape((subs * per * MOST, docs), BF16)] * count + row_shapes,
            [inv, centre] + [leads[bits] for bits in group],
        )
        picks, found = list(found[:count]), list(found[count:])
        members.append(across(found))
        if last:
            before = (found, members[:-1])
        else:
            before = (found, members)
            weights = []
            for bits, prefix in zip(group, prefixes):
                weight, *lead_sums = call(
                    functools.partial(sums_lead_kernel, subs),
                    "sums_lead",
                    [shape((subs * per, docs), BF16)] + [lead_sum] * subs,
                    [leads[bits], prefix, cent_prefix, own_prefix] + lead_sums,
                    {4 + i: 1 + i for i in range(subs)},
                )
                weights.append(weight)
        rests.update(zip(group, tied([rests[bits] for bits in group], before)))
        for bits in group:
            send(rests, bits)
        row_shapes = [shape((count, groups, packed, half - PREFIX), BF16)] * subs
        found = call(
            functools.partial(select_rest_kernel, count, subs),
            "select_rest",
            row_shapes,
            [centre] + picks + [rests[bits] for bits in group],
        )
        members.append(across(found))
        if last:
            break
        rest_sums = call(
            functools.partial(sums_rest_kernel, count, subs),
            "sums_rest",
            [rest_sum] * subs,
            weights + [rests[bits] for bits in group] + list(rest_sums),
            {2 * count + i: i for i in range(subs)},
        )

    (bits,), (prefix,) = group, prefixes
    lead, rest, *sent = call(
        functools.partial(last_sums_kernel, subs),
        "last_sums",
        [lead_sum, rest_sum] + [shape((2 * per + 2 * SUBLANES, PREFIX), BF16)] * (subs - 1),
        [leads[bits], rests[bits], prefix, cent_prefix, own_prefix] + list(lead_sums) + list(tied(rest_sums, members[:-1])),
        {5: 0, 5 + subs: 1},
        scratch=[pltpu.VMEM(total.shape, F32) for total in [lead_sum] * (subs - 1) + [rest_sum] * (subs - 1)],
    )
    _, *sent = across([None] + sent)

    (gram,) = call(
        functools.partial(gram_kernel, groups_of_bits, subs),
        "gram",
        [shape((groups, slots, slots * SUBLANES), F32)],
        [arrays[t] for t in range(subs) for arrays in members],
        scratch=[pltpu.VMEM((owners, groups, packed, half), BF16)],
    )
    (tiles,) = call(
        functools.partial(tile_kernel, width),
        "tiles",
        [shape((slots // 2, slots, per), BF16)],
        [gram, near(gram)],
        scratch=[pltpu.VMEM((groups, slots // 2, slots * SUBLANES), F32)],
    )
    (new_centroids,) = call(centroid_kernel, "centroids", [shape((per, half), F32)], [lead, rest] + tied(sent, tiles) + [prior])
    return (new_centroids, jnp.transpose(tiles, (2, 0, 1)))


def solution(mesh):
    in_specs = (
        P(("parts", "rows", "sub"), "dim"),
        P("parts", None),
        P(("parts", "rows", "sub"), None),
        P(),
    )
    out_specs = (P(("parts", "rows", "sub"), "dim"), P(("parts", "rows", "sub"), "dim", None))
    return jax.shard_map(shards, mesh=mesh, in_specs=in_specs, out_specs=out_specs, check_vma=False)
```

```python
import functools

import jax
import jax.numpy as jnp
from jax import lax
from jax.experimental import pallas as pl
from jax.experimental.pallas import tpu as pltpu
from jax.sharding import PartitionSpec as P

PREFIX = 256
MOST = 2

TEMP = 0.125
SMOOTH = 1.0
EPS = 1e-05

DIGIT = 32
META = 16
SUBLANES = 8
LANES = 128
F32 = jnp.float32
BF16 = jnp.bfloat16
VMEM_LIMIT = 40 * 1024 * 1024

NT = (((1,), (1,)), ((), ()))


def call(kernel, name, out_shape, operands, aliases=None, scratch=(), cost=0):
    def whole(_):
        return pl.BlockSpec(memory_space=pltpu.VMEM)

    return pl.pallas_call(
        kernel,
        out_shape=tuple(out_shape),
        in_specs=[whole(operand) for operand in operands],
        out_specs=tuple(whole(out) for out in out_shape),
        input_output_aliases=aliases or {},
        scratch_shapes=list(scratch),
        compiler_params=pltpu.CompilerParams(vmem_limit_bytes=VMEM_LIMIT),
        cost_estimate=pl.CostEstimate(flops=50 * cost, bytes_accessed=cost, transcendentals=0),
        name=name,
    )(*operands)


def dot(a, b):
    return jnp.dot(a, b, preferred_element_type=F32)


def dot_nt(a, b):
    return lax.dot_general(a, b, NT, preferred_element_type=F32)


def tied(values, *others):
    leaves, tree = jax.tree.flatten(values)
    kept = lax.optimization_barrier(tuple(leaves) + tuple(jax.tree.leaves(others)))
    return jax.tree.unflatten(tree, kept[: len(leaves)])


def bits_by_count(rows):
    return [[bits for bits in range(rows) if bits.bit_count() == n] for n in range(1, (rows - 1).bit_count() + 1)]


def pack_kernel(emb_ref, cid_ref, lead_ref, rest_ref):
    docs = emb_ref.shape[0]
    lead_ref[:docs, :] = emb_ref[:, :PREFIX]
    rest_ref[:docs, :] = emb_ref[:, PREFIX:]
    rest_ref[docs:, :] = jnp.zeros((META, rest_ref.shape[1]), BF16)
    cid = cid_ref[...]
    high, low = (cid // DIGIT + 1).astype(F32), (cid % DIGIT).astype(F32)
    rows = []
    for digit in (high, low):
        rows += [digit[:, at : at + PREFIX] for at in range(0, docs, PREFIX)]
    rows.append(jnp.zeros((META - len(rows), PREFIX), F32))
    lead_ref[docs:, :] = jnp.concatenate(rows, axis=0).astype(BF16)


def ids_of(lead_ref):
    docs = lead_ref.shape[0] - META
    meta = lead_ref[docs:, :].astype(F32)
    parts = docs // PREFIX
    high = jnp.concatenate([meta[i : i + 1] for i in range(parts)], axis=1)
    low = jnp.concatenate([meta[parts + i : parts + i + 1] for i in range(parts)], axis=1)
    return (high - 1.0) * DIGIT + low


def prep_kernel(subs, per, place_ref, cent_ref, inv_ref, centre_ref, own_prefix_ref, prior_ref, prefix_ref):
    clusters = cent_ref.shape[0]
    half = centre_ref.shape[1]
    z, x, h = lax.axis_index("rows"), lax.axis_index("sub"), lax.axis_index("dim")
    row = lax.broadcasted_iota(jnp.int32, (subs * per, clusters), 0)
    ids = lax.broadcasted_iota(jnp.int32, (subs * per, clusters), 1)
    turn, within = row // per, row % per
    target = (z * subs + (x + turn) % subs) * per + within
    chosen = (place_ref[...] == target).astype(F32)
    inv_ref[...] = jnp.sum(chosen * ids.astype(F32), axis=1, keepdims=True)
    columns = cent_ref[:, pl.ds(pl.multiple_of(h * half, LANES), half)]
    centre_ref[...] = dot(chosen.astype(BF16), columns).astype(BF16)
    natural = (ids == target).astype(BF16)
    prior_ref[...] = dot(natural[:per], columns).astype(BF16)
    prefix_ref[...] = cent_ref[:, :PREFIX]
    own_prefix_ref[...] = dot(natural, prefix_ref[...]).astype(BF16)


def centred(pick, centre, columns):
    slots = pick.shape[0]
    groups = slots // (MOST * SUBLANES)
    width = columns.shape[1]
    present = jnp.sum(pick.astype(F32), axis=1, keepdims=True)
    raw = dot(pick, columns)
    middle = centre.astype(F32).reshape(groups, 1, SUBLANES, width)
    middle = jnp.broadcast_to(middle, (groups, MOST, SUBLANES, width)).reshape(slots, width)
    return jnp.where(present > 0.0, raw - middle, 0.0).astype(BF16)


def picked(lead_ref, inv_ref):
    cid = ids_of(lead_ref)
    docs = cid.shape[1]
    groups = inv_ref.shape[0] // SUBLANES
    match = (inv_ref[...] == cid).astype(F32)
    before = lax.broadcasted_iota(jnp.int32, (docs, docs), 0) < lax.broadcasted_iota(jnp.int32, (docs, docs), 1)
    earlier = dot(match.astype(BF16), before.astype(F32).astype(BF16))
    ranked = [jnp.where(earlier == r, match, 0.0).reshape(groups, SUBLANES, docs) for r in range(MOST)]
    return jnp.stack(ranked, axis=1).reshape(groups * MOST * SUBLANES, docs).astype(BF16)


def select_kernel(lead_ref, rest_ref, inv_ref, centre_ref, *row_refs):
    docs = rest_ref.shape[0] - META
    pick = picked(lead_ref, inv_ref)
    groups, packed, _ = row_refs[0].shape
    for columns, at in ((lead_ref[:docs, :], 0), (rest_ref[:docs, :], PREFIX)):
        width = columns.shape[1]
        rows = centred(pick, centre_ref[:, at : at + width], columns)
        rows = rows.reshape(len(row_refs), groups, packed, width)
        for t, ref in enumerate(row_refs):
            ref[:, :, at : at + width] = rows[t]


def select_lead_kernel(count, subs, inv_ref, centre_ref, *refs):
    lead_refs, pick_refs, row_refs = refs[:count], refs[count : 2 * count], refs[2 * count :]
    for i in range(count):
        docs = lead_refs[i].shape[0] - META
        pick = picked(lead_refs[i], inv_ref)
        pick_refs[i][...] = pick
        rows = centred(pick, centre_ref[:, :PREFIX], lead_refs[i][:docs, :])
        rows = rows.reshape((subs,) + row_refs[0].shape[1:])
        for t in range(subs):
            row_refs[t][i] = rows[t]


def select_rest_kernel(count, subs, centre_ref, *refs):
    pick_refs, rest_refs, row_refs = refs[:count], refs[count : 2 * count], refs[2 * count :]
    for i in range(count):
        pick = pick_refs[i][...]
        rows = centred(pick, centre_ref[:, PREFIX:], rest_refs[i][: pick.shape[1], :])
        rows = rows.reshape((subs,) + row_refs[0].shape[1:])
        for t in range(subs):
            row_refs[t][i] = rows[t]


def soft_weights(lead_ref, near_ref, cent_ref, own_prefix_ref):
    docs = lead_ref.shape[0] - META
    h = lax.axis_index("dim")
    prefix = jnp.where(h == 0, lead_ref[:docs, :], near_ref[:docs, :])
    scores = dot_nt(cent_ref[...], prefix) * TEMP
    top = jnp.max(scores, axis=0, keepdims=True)
    scale = 1.0 / jnp.sum(jnp.exp(scores - top), axis=0, keepdims=True)
    own = dot_nt(own_prefix_ref[...], prefix) * TEMP
    return jnp.where(ids_of(lead_ref) >= 0.0, jnp.exp(own - top) * scale, 0.0)


def add_lead(weights, lead_ref, old_refs, new_refs):
    docs = lead_ref.shape[0] - META
    per = new_refs[0].shape[0] - SUBLANES
    sums = dot(weights.astype(BF16), lead_ref[:docs, :])
    ones = jnp.ones((SUBLANES, docs), BF16)
    for t, new in enumerate(new_refs):
        here = slice(t * per, (t + 1) * per)
        mass = dot_nt(ones, weights[here].astype(BF16))
        if old_refs:
            old = old_refs[t]
            new[:per, :] = old[:per, :] + sums[here]
            new[per:, :] = old[per:, :]
            new[per:, :per] = old[per:, :per] + mass
        else:
            new[:per, :] = sums[here]
            new[per:, :] = jnp.zeros((SUBLANES, new.shape[1]), F32)
            new[per:, :per] = mass


def add_rest(weights, rest, old_refs, new_refs):
    per = new_refs[0].shape[0]
    sums = dot(weights, rest)
    for t, new in enumerate(new_refs):
        part = sums[t * per : (t + 1) * per]
        new[...] = old_refs[t][...] + part if old_refs else part


def sums_kernel(subs, lead_ref, rest_ref, near_ref, cent_ref, own_prefix_ref, *new):
    weights = soft_weights(lead_ref, near_ref, cent_ref, own_prefix_ref)
    add_lead(weights, lead_ref, (), new[:subs])
    add_rest(weights.astype(BF16), rest_ref[: weights.shape[1], :], (), new[subs:])


def sums_lead_kernel(subs, lead_ref, near_ref, cent_ref, own_prefix_ref, *refs):
    old, weights_ref, new = refs[:subs], refs[subs], refs[subs + 1 :]
    weights = soft_weights(lead_ref, near_ref, cent_ref, own_prefix_ref)
    weights_ref[...] = weights.astype(BF16)
    add_lead(weights, lead_ref, old, new)


def last_sums_kernel(subs, lead_ref, rest_ref, near_ref, cent_ref, own_prefix_ref, *refs):
    old, new, totals = refs[: 2 * subs], refs[2 * subs : 3 * subs + 1], refs[3 * subs + 1 :]
    weights = soft_weights(lead_ref, near_ref, cent_ref, own_prefix_ref)
    add_lead(weights, lead_ref, old[:subs], new[:1] + totals[: subs - 1])
    add_rest(weights.astype(BF16), rest_ref[: weights.shape[1], :], old[subs:], new[1:2] + totals[subs - 1 :])
    for t in range(subs - 1):
        lead, rest = totals[t][...], totals[subs - 1 + t][...]
        mass = lead[-SUBLANES:]
        high = mass.astype(BF16).astype(F32)
        new[2 + t][...] = jnp.concatenate([lead[:-SUBLANES], rest, high, mass - high], axis=0).astype(BF16)


def sums_rest_kernel(count, subs, *refs):
    weights_refs, rest_refs, old, new = refs[:count], refs[count : 2 * count], refs[-2 * subs : -subs], refs[-subs:]
    total = sum(dot(w[...], rest[: w.shape[1], :]) for w, rest in zip(weights_refs, rest_refs))
    per = new[0].shape[0]
    for t in range(subs):
        new[t][...] = old[t][...] + total[t * per : (t + 1) * per]


def gram_kernel(groups_of_bits, subs, *refs):
    *member_refs, gram_ref, held = refs
    z, x = lax.axis_index("rows"), lax.axis_index("sub")
    owners, groups, packed, half = held.shape
    each = len(member_refs) // subs
    for t in range(subs):
        own, *chunks = member_refs[t * each : (t + 1) * each]
        column = (x - t + subs) % subs
        held[z * subs + column] = own[...]
        for k, group in enumerate(groups_of_bits):
            for i, bits in enumerate(group):
                row = (z ^ bits) * subs + column
                held[row, :, :, :PREFIX] = chunks[2 * k][i]
                held[row, :, :, PREFIX:] = chunks[2 * k + 1][i]

    size = owners * packed
    lane = lax.broadcasted_iota(jnp.int32, (1, SUBLANES, size), 2) % SUBLANES
    same = (lane == lax.broadcasted_iota(jnp.int32, (1, SUBLANES, size), 1)).astype(F32)
    tile = min(size, 2 * LANES)
    for g in range(groups):
        mine = held[:, g].reshape(size, half)
        for start in range(0, size, tile):
            part = dot_nt(mine[start : start + tile], mine)
            part = part.reshape(tile // SUBLANES, SUBLANES, size)
            gram_ref[g, start // SUBLANES : (start + tile) // SUBLANES, :] = jnp.sum(part * same, axis=1)


def scaled_tiles(width, mine_ref, other_ref, scaled_ref):
    groups, slots, size = mine_ref.shape
    kept = scaled_ref.shape[1]
    h = lax.axis_index("dim")
    start = pl.multiple_of(h * kept, kept)
    row = lax.broadcasted_iota(jnp.int32, (slots, size), 0)
    lane = lax.broadcasted_iota(jnp.int32, (slots, size), 1)
    diagonal = row == lane // SUBLANES
    kept_row = lax.broadcasted_iota(jnp.int32, (kept, size), 0) + start
    kept_lane = lax.broadcasted_iota(jnp.int32, (kept, size), 1)
    kept_diagonal = kept_row == kept_lane // SUBLANES
    for g in range(groups):
        total = mine_ref[g] + other_ref[g]
        norms = jnp.sum(jnp.where(diagonal, total, 0.0), axis=0, keepdims=True)
        scale = lax.rsqrt(norms / width + EPS)
        spread = jnp.where(kept_diagonal, jnp.broadcast_to(scale, (kept, size)), 0.0)
        folded = spread[:, :LANES]
        for at in range(LANES, size, LANES):
            folded = folded + spread[:, at : at + LANES]
        step = SUBLANES
        while step < LANES:
            folded = folded + pltpu.roll(folded, step, 1)
            step *= 2
        row_scale = jnp.concatenate([folded] * (size // LANES), axis=1)
        own = mine_ref[g, pl.ds(start, kept), :] + other_ref[g, pl.ds(start, kept), :]
        scaled_ref[g] = own / width * row_scale * scale


def centroid_kernel(lead_ref, rest_ref, *refs):
    *sent_refs, prior_ref, new_ref = refs
    per = prior_ref.shape[0]
    lead, mass, rest = lead_ref[:per, :], lead_ref[per:, :], rest_ref[...]
    for ref in sent_refs:
        sent = ref[...].astype(F32)
        lead = lead + sent[:per]
        rest = rest + sent[per : 2 * per]
        mass = mass + sent[2 * per : 2 * per + SUBLANES] + sent[2 * per + SUBLANES :]
    mass = jnp.transpose(mass[:, :LANES])[:per, :1] + SMOOTH
    prior = SMOOTH * prior_ref[...].astype(F32)
    new_ref[:, :PREFIX] = (lead + prior[:, :PREFIX]) / mass
    new_ref[:, PREFIX:] = (rest + prior[:, PREFIX:]) / mass


def tile_kernel(width, mine_ref, other_ref, tile_ref, scaled_ref):
    scaled_tiles(width, mine_ref, other_ref, scaled_ref)
    per = tile_ref.shape[2]
    groups, kept, size = scaled_ref.shape
    slots = size // SUBLANES
    at = lax.broadcasted_iota(jnp.int32, (groups * size, per), 0)
    to = lax.broadcasted_iota(jnp.int32, (groups * size, per), 1)
    move = ((at // size == to // SUBLANES) & (at % SUBLANES == to % SUBLANES)).astype(F32).astype(BF16)
    row = lax.broadcasted_iota(jnp.int32, (slots, size), 0)
    lane = lax.broadcasted_iota(jnp.int32, (slots, size), 1)
    here = row == lane // SUBLANES
    batch = max(1, LANES // slots)

    def some(step, carry):
        spread = []
        for b in range(batch):
            i = step * batch + b
            lines = [jnp.broadcast_to(scaled_ref[g, pl.ds(i, 1), :], (slots, size)) for g in range(groups)]
            spread.append(jnp.concatenate([jnp.where(here, line, 0.0) for line in lines], axis=1))
        moved = dot(jnp.concatenate(spread, axis=0).astype(BF16), move).astype(BF16)
        for b in range(batch):
            tile_ref[step * batch + b] = moved[b * slots : (b + 1) * slots]
        return carry

    if kept == batch:
        some(0, 0)
    else:
        lax.fori_loop(0, kept // batch, some, 0)


def shards(embeddings, centroids, cluster_id, cluster_place):
    docs, half = embeddings.shape
    clusters, width = centroids.shape
    rows, subs = lax.axis_size("rows"), lax.axis_size("sub")
    owners = rows * subs
    per = clusters // owners
    groups = per // SUBLANES
    packed = MOST * SUBLANES
    slots = owners * MOST
    groups_of_bits = bits_by_count(rows)
    shape = jax.ShapeDtypeStruct

    def across(values):
        got = [values[0]]
        for t in range(1, subs):
            got.append(lax.ppermute(values[t], "sub", [(i, (i + t) % subs) for i in range(subs)]))
        return got

    def near(value):
        return lax.ppermute(value, "dim", [(0, 1), (1, 0)])

    def swap(value, bit):
        return lax.ppermute(value, "rows", [(i, i ^ bit) for i in range(rows)])

    def send(blocks, bits):
        bit = (bits & -bits or rows) // 2
        while bit:
            blocks[bits | bit] = swap(blocks[bits], bit)
            bit //= 2

    lead, rest = call(
        pack_kernel,
        "pack",
        [shape((docs + META, PREFIX), BF16), shape((docs + META, half - PREFIX), BF16)],
        [embeddings, cluster_id.reshape(1, docs)],
    )
    leads, rests = {0: lead}, {0: rest}
    send(leads, 0)

    inv, centre, own_prefix, prior, cent_prefix = call(
        functools.partial(prep_kernel, subs, per),
        "prep",
        [
            shape((subs * per, 1), F32),
            shape((subs * per, half), BF16),
            shape((subs * per, PREFIX), BF16),
            shape((per, half), BF16),
            shape((clusters, PREFIX), BF16),
        ],
        [cluster_place.reshape(1, clusters), centroids],
        cost=4 * 1024 * 1024,
    )

    lead_sum, rest_sum = shape((per + SUBLANES, PREFIX), F32), shape((per, half - PREFIX), F32)
    sum_shapes = [lead_sum] * subs + [rest_sum] * subs
    own_cost = 2 * 1024 * 1024

    prefix = near(lead)
    found = call(
        select_kernel, "select", [shape((groups, packed, half), BF16)] * subs, [lead, rest, inv, centre], cost=own_cost
    )
    members = [across(found)]
    rests[0] = tied(rest, found)
    send(rests, 0)
    sums = call(
        functools.partial(sums_kernel, subs),
        "sums",
        sum_shapes,
        [lead, rest, prefix, cent_prefix, own_prefix],
        cost=own_cost,
    )
    lead_sums, rest_sums = list(sums[:subs]), list(sums[subs:])

    for group in groups_of_bits:
        last = group == groups_of_bits[-1]
        count = len(group)
        before = members[:-1] if last else members
        leads.update(zip(group, tied([leads[bits] for bits in group], found, lead_sums, rest_sums, before)))
        for bits in group:
            send(leads, bits)
        prefixes = [near(leads[bits]) for bits in group]
        row_shapes = [shape((count, groups, packed, PREFIX), BF16)] * subs
        found = call(
            functools.partial(select_lead_kernel, count, subs),
            "select_lead",
            [shape((subs * per * MOST, docs), BF16)] * count + row_shapes,
            [inv, centre] + [leads[bits] for bits in group],
        )
        picks, found = list(found[:count]), list(found[count:])
        members.append(across(found))
        if last:
            before = (found, members[:-1])
        else:
            before = (found, members)
            weights = []
            for bits, prefix in zip(group, prefixes):
                weight, *lead_sums = call(
                    functools.partial(sums_lead_kernel, subs),
                    "sums_lead",
                    [shape((subs * per, docs), BF16)] + [lead_sum] * subs,
                    [leads[bits], prefix, cent_prefix, own_prefix] + lead_sums,
                    {4 + i: 1 + i for i in range(subs)},
                )
                weights.append(weight)
        rests.update(zip(group, tied([rests[bits] for bits in group], before)))
        for bits in group:
            send(rests, bits)
        row_shapes = [shape((count, groups, packed, half - PREFIX), BF16)] * subs
        found = call(
            functools.partial(select_rest_kernel, count, subs),
            "select_rest",
            row_shapes,
            [centre] + picks + [rests[bits] for bits in group],
        )
        members.append(across(found))
        if last:
            break
        rest_sums = call(
            functools.partial(sums_rest_kernel, count, subs),
            "sums_rest",
            [rest_sum] * subs,
            weights + [rests[bits] for bits in group] + list(rest_sums),
            {2 * count + i: i for i in range(subs)},
        )

    (bits,), (prefix,) = group, prefixes
    lead, rest, *sent = call(
        functools.partial(last_sums_kernel, subs),
        "last_sums",
        [lead_sum, rest_sum] + [shape((2 * per + 2 * SUBLANES, PREFIX), BF16)] * (subs - 1),
        [leads[bits], rests[bits], prefix, cent_prefix, own_prefix] + list(lead_sums) + list(tied(rest_sums, members[:-2])),
        {5: 0, 5 + subs: 1},
        scratch=[pltpu.VMEM(total.shape, F32) for total in [lead_sum] * (subs - 1) + [rest_sum] * (subs - 1)],
    )
    _, *sent = across([None] + sent)

    (gram,) = call(
        functools.partial(gram_kernel, groups_of_bits, subs),
        "gram",
        [shape((groups, slots, slots * SUBLANES), F32)],
        [arrays[t] for t in range(subs) for arrays in members],
        scratch=[pltpu.VMEM((owners, groups, packed, half), BF16)],
    )
    (tiles,) = call(
        functools.partial(tile_kernel, width),
        "tiles",
        [shape((slots // 2, slots, per), BF16)],
        [gram, near(gram)],
        scratch=[pltpu.VMEM((groups, slots // 2, slots * SUBLANES), F32)],
    )
    (new_centroids,) = call(centroid_kernel, "centroids", [shape((per, half), F32)], [lead, rest] + tied(sent, tiles) + [prior])
    return (new_centroids, jnp.transpose(tiles, (2, 0, 1)))


def solution(mesh):
    in_specs = (
        P(("parts", "rows", "sub"), "dim"),
        P("parts", None),
        P(("parts", "rows", "sub"), None),
        P(),
    )
    out_specs = (P(("parts", "rows", "sub"), "dim"), P(("parts", "rows", "sub"), "dim", None))
    return jax.shard_map(shards, mesh=mesh, in_specs=in_specs, out_specs=out_specs, check_vma=False)
```
